128 devices in a mesh: region: 4 (over x), inner: 32 (over z, y, core).
Axes of the slice: x: 4, y: 4, z: 4, core: 2. Of those that a mesh axis runs over, the one named last changes fastest.
Arguments:
- coarse_state: float32 [5, 64, 512, 128], P(None, 'region', 'inner'), may hold values from -6 to 6
- fine_state: float32 [128, 5, 32, 1024], P(('region', 'inner')), may hold values from -6 to 6
- coarse_rate: float32 [64, 512, 128], P('region', 'inner'), may hold values from 0.5 to 4
- fine_rate: float32 [128, 32, 1024], P(('region', 'inner')), may hold values from 0.5 to 4
- parents: int32 [4, 32], P('region'), may hold values from 0 to 255, as said below
- burn_steps: int32 [128], P(('region', 'inner')), may hold values from 1 to 8, as said below
Outputs:
- coarse_new: float32 [5, 64, 512, 128], P(None, 'region', 'inner')
- fine_new: float32 [128, 5, 32, 1024], P(('region', 'inner'))
The draws below stay inside these ranges and needn't reach their ends.
Inputs may be any that keep to these rules, and one draw needn't show every extreme that they name: `parents`: each row lists 32 different blocks of its region; block b lies on inner index b // 8. At most 2 listed blocks lie on one inner index, and exactly 2 on some. `burn_steps`: some patch takes 8 sub-steps.
All inputs are finite; a program needn't handle non-finite values.
Results may differ from the reference program's by a relative error of at most 0.0003.
Values sent between devices are 32-bit elements; how exact they have to be, the bound alone decides.
A program may use at most 128 MiB of HBM per device.

```python
import math
import jax
import jax.numpy as jnp
from jax import lax

FIELDS = 5
BLOCK = 16
ZBLOCKS = 8
PATCH_DEV = 1
BURN_MAX = 8
PATCH = 32
NXC = 64
NYC = 512
NZC = 128
PATCHES = 128
N_REGION = 4
N_INNER = 32


def region_table(key):
    keys = jax.random.split(key, 4)
    order = jax.random.permutation(keys[0], N_INNER)
    half = N_INNER // 2
    shifts = jax.random.randint(keys[1], (half,), 0, PATCH_DEV + 1)
    shifts = shifts.at[0].set(PATCH_DEV)
    loads = jnp.concatenate([PATCH_DEV + shifts, PATCH_DEV - shifts]).astype(jnp.int32)
    counts = jnp.zeros((N_INNER,), jnp.int32).at[order].set(loads)

    def ranking_row(subkey):
        return jax.random.permutation(subkey, ZBLOCKS)
    ranking = jax.vmap(ranking_row)(jax.random.split(keys[2], N_INNER))
    chosen = (ranking < counts[:, None]).reshape(-1)
    labels = jnp.arange(N_INNER * ZBLOCKS, dtype=jnp.int32)
    scores = jnp.where(chosen, labels, labels + N_INNER * ZBLOCKS)
    refined = jnp.argsort(scores, stable=True)[:N_INNER * PATCH_DEV]
    shuffle = jax.random.permutation(keys[3], N_INNER * PATCH_DEV)
    return refined[shuffle].astype(jnp.int32)


def draw_parents(key, part):
    key = jax.random.fold_in(key, 1)
    return jax.vmap(region_table)(jax.random.split(key, N_REGION))


def draw_burn_steps(key, part):
    key = jax.random.fold_in(key, 2)
    first, second = jax.random.split(key, 2)
    counts = jax.random.randint(first, (PATCHES,), 1, BURN_MAX + 1)
    target = jax.random.randint(second, (), 0, PATCHES)
    return counts.at[target].set(BURN_MAX).astype(jnp.int32)


def levels(stream_key, extent, pieces, smallest, high):
    def one(dim, blocks):
        heights = jax.random.uniform(jax.random.fold_in(jax.random.fold_in(stream_key, 6), dim), (blocks,), jnp.float32, smallest / len(pieces), high / len(pieces))
        return jnp.repeat(jnp.exp(heights), extent[dim] // blocks).reshape((-1,) + (1,) * (len(extent) - dim - 1))

    gain = one(*pieces[0])
    for cut in pieces[1:]:
        gain = gain * one(*cut)
    return gain


def gaussian(stream_key, extent, width, bound, shards=(), held_as=jnp.bfloat16):
    result = width * jax.random.normal(stream_key, extent, jnp.float32)
    if shards:
        result = result * levels(stream_key, extent, shards, -0.22, 0.18)
    return jnp.clip(result, -bound, bound).astype(held_as)


def setup_inputs(seed: int = 0) -> dict:
    seeds = jax.random.split(jax.random.key(seed), 7)
    coarse_state = gaussian(seeds[0], (FIELDS, NXC, NYC, NZC), 1.0, 6.0, ((1, 4), (2, 32)), jnp.float32)
    fine_state = gaussian(seeds[1], (PATCHES, FIELDS, PATCH, PATCH * PATCH), 1.0, 6.0, ((0, 128),), jnp.float32)
    coarse_rate = jnp.clip(jnp.exp(math.log(4.0) - 2.0794415 * jax.random.uniform(seeds[2], (NXC, NYC, NZC), jnp.float32) ** levels(seeds[2], (NXC, NYC, NZC), ((0, 4), (1, 32)), -0.2, 0.2)), 0.5, 4.0)
    fine_rate = jnp.clip(jnp.exp(math.log(4.0) - 2.0794415 * jax.random.uniform(seeds[3], (PATCHES, PATCH, PATCH * PATCH), jnp.float32) ** levels(seeds[3], (PATCHES, PATCH, PATCH * PATCH), ((0, 128),), -0.2, 0.2)), 0.5, 4.0)
    parents = draw_parents(jax.random.fold_in(seeds[6], 71), 0)
    burn_steps = draw_burn_steps(jax.random.fold_in(seeds[6], 71), 0)
    return {"coarse_state": coarse_state, "fine_state": fine_state, "coarse_rate": coarse_rate, "fine_rate": fine_rate, "parents": parents, "burn_steps": burn_steps}


sound_speed = 1.0
max_speed = 1.0
courant = 0.3
advection = (0.5, -0.3, 0.2)
release_heat = 0.5
coarse_step = 0.5
fine_step = 0.25


def face_flux(lower_side, upper_side, axis):
    average = 0.5 * (lower_side + upper_side)
    components = []
    for number in range(5):
        if number == 0:
            component = sound_speed * average[1 + axis]
        elif number == 1 + axis:
            component = sound_speed * average[0]
        elif number == 4:
            component = advection[axis] * average[4]
        else:
            component = jnp.zeros_like(average[0])
        components.append(component)
    return jnp.stack(components) - 0.5 * max_speed * (upper_side - lower_side)


def hydro(padded):
    interior = padded[:, 1:-1, 1:-1, 1:-1]
    flux_x = face_flux(padded[:, :-1, 1:-1, 1:-1], padded[:, 1:, 1:-1, 1:-1], 0)
    flux_y = face_flux(padded[:, 1:-1, :-1, 1:-1], padded[:, 1:-1, 1:, 1:-1], 1)
    flux_z = face_flux(padded[:, 1:-1, 1:-1, :-1], padded[:, 1:-1, 1:-1, 1:], 2)
    change = (flux_x[:, 1:] - flux_x[:, :-1]) + (flux_y[:, :, 1:] - flux_y[:, :, :-1]) + (flux_z[:, :, :, 1:] - flux_z[:, :, :, :-1])
    return interior - courant * change


def burn_step(state, rate, span):
    pressure = state[0]
    fuel = state[4]
    burned = fuel / (1.0 + span * rate * (1.0 + 0.5 * jnp.tanh(pressure)))
    return jnp.stack([pressure + release_heat * (fuel - burned), state[1], state[2], state[3], burned])


def burn_patch(state, rate, count):
    counted = count.astype(jnp.float32)
    span = fine_step / counted
    for turn in range(BURN_MAX):
        burned = burn_step(state, rate, span)
        state = jnp.where(turn < counted, burned, state)
    return state


def fine_padded(state, faces, block):
    shaped = faces.reshape(5, 6, block, block)
    widened = jnp.repeat(jnp.repeat(shaped, 2, axis=2), 2, axis=3)
    padded = jnp.pad(state, ((0, 0), (1, 1), (1, 1), (1, 1)))
    padded = padded.at[:, 0, 1:-1, 1:-1].set(widened[:, 0])
    padded = padded.at[:, -1, 1:-1, 1:-1].set(widened[:, 1])
    padded = padded.at[:, 1:-1, 0, 1:-1].set(widened[:, 2])
    padded = padded.at[:, 1:-1, -1, 1:-1].set(widened[:, 3])
    padded = padded.at[:, 1:-1, 1:-1, 0].set(widened[:, 4])
    padded = padded.at[:, 1:-1, 1:-1, -1].set(widened[:, 5])
    return padded


def advance_patch(state, rate, count, old_faces, new_faces, block):
    state = burn_patch(hydro(fine_padded(state, old_faces, block)), rate, count)
    middle = 0.5 * (old_faces + new_faces)
    state = burn_patch(hydro(fine_padded(state, middle, block)), rate, count)
    return state


def average_down(state, block):
    return state.reshape(5, block, 2, block, 2, block, 2).mean(axis=(2, 4, 6))


def cube_faces(cube, block):
    stacked = jnp.stack([cube[:, 0, 1:-1, 1:-1], cube[:, -1, 1:-1, 1:-1], cube[:, 1:-1, 0, 1:-1],
                         cube[:, 1:-1, -1, 1:-1], cube[:, 1:-1, 1:-1, 0], cube[:, 1:-1, 1:-1, -1]], axis=1)
    return stacked.reshape(5, 6, block * block)


def reference(coarse_state, fine_state, coarse_rate, fine_rate, parents, burn_steps):
    block = BLOCK
    patch = 2 * BLOCK
    widths = ((0, 0), (1, 1), (1, 1), (1, 1))
    padded_old = jnp.pad(coarse_state, widths)
    stepped = burn_step(hydro(padded_old), coarse_rate, coarse_step)
    padded_new = jnp.pad(stepped, widths)
    per_region = N_INNER * PATCH_DEV

    def locate(number):
        region_index = (number // per_region).astype(jnp.int32)
        target = parents[region_index, number % per_region]
        column = (target // ZBLOCKS).astype(jnp.int32)
        layer = (target % ZBLOCKS).astype(jnp.int32)
        return region_index, column, layer

    def one_patch(number):
        region_index, column, layer = locate(number)
        anchor = (jnp.int32(0), block * region_index, block * column, block * layer)
        edge = (5, block + 2, block + 2, block + 2)
        old_faces = cube_faces(lax.dynamic_slice(padded_old, anchor, edge), block)
        new_faces = cube_faces(lax.dynamic_slice(padded_new, anchor, edge), block)
        state = fine_state[number].reshape(5, patch, patch, patch)
        rate = fine_rate[number].reshape(patch, patch, patch)
        final = advance_patch(state, rate, burn_steps[number], old_faces, new_faces, block)
        return final.reshape(5, patch, patch * patch), average_down(final, block)

    finals, means = lax.map(one_patch, jnp.arange(PATCHES, dtype=jnp.int32))

    def place(number, coarse):
        region_index, column, layer = locate(number)
        anchor = (jnp.int32(0), block * region_index, block * column, block * layer)
        return lax.dynamic_update_slice(coarse, means[number], anchor)

    coarse_new = lax.fori_loop(0, PATCHES, place, stepped)
    return coarse_new, finals
```

```python
import functools

import jax
import jax.numpy as jnp
from jax import lax
from jax.experimental import pallas as pl
from jax.experimental.pallas import tpu as pltpu
from jax.sharding import PartitionSpec as P

MESH = pl.DeviceIdType.MESH
F32 = jnp.float32
ADV = (0.5, -0.3, 0.2)
KEEP = 0.1
NB = 0.15
BURN_MAX = 8
REGIONS = 4
INNER = 32


def iota(shape, axis):
    return lax.broadcasted_iota(jnp.int32, shape, axis)


def lanes(q, shift):
    return pltpu.roll(q, shift % 128, 1)


def rows(q, shift):
    return pltpu.roll(q, shift % q.shape[0], 0)


def hydro(c, xm, xp, yd, yu, zd, zu):
    p, u, v, w, f = c
    sx, mx = xm[0] + xm[1], xp[0] - xp[1]
    sy, my = yd(p + v), yu(p - v)
    sz, mz = zd(p + w), zu(p - w)
    hp = (sx + mx) + (sy + my) + (sz + mz)
    hu = (sx - mx) + (yd(u) + yu(u)) + (zd(u) + zu(u))
    hv = (xm[2] + xp[2]) + (sy - my) + (zd(v) + zu(v))
    hw = (xm[3] + xp[3]) + (yd(w) + yu(w)) + (sz - mz)
    hf = (
        ((1 + ADV[0]) * xm[4] + (1 - ADV[0]) * xp[4])
        + ((1 + ADV[1]) * yd(f) + (1 - ADV[1]) * yu(f))
        + ((1 + ADV[2]) * zd(f) + (1 - ADV[2]) * zu(f))
    )
    return [KEEP * a + NB * b for a, b in zip(c, (hp, hu, hv, hw, hf))]


def take(q, index):
    return jnp.take_along_axis(q, index, axis=1, mode="promise_in_bounds")


def coarse_shifts(shape):
    row, lane = iota(shape, 0), iota(shape, 1)
    zd = lambda q: jnp.where(lane == 0, 0.0, lanes(q, 1))
    zu = lambda q: jnp.where(lane == 127, 0.0, lanes(q, -1))
    yd = lambda q: jnp.where(row == 0, 0.0, rows(q, 1))
    yu = lambda q: jnp.where(row == shape[0] - 1, 0.0, rows(q, -1))
    return yd, yu, zd, zu


def fine_shifts():
    sub, lane = iota((8, 128), 0), iota((8, 128), 1)
    z = lane % 32

    def yd(q):
        t = lanes(q, 32)
        t = jnp.where(lane < 32, rows(t, 1), t)
        return jnp.where((lane < 32) & (sub == 0), 0.0, t)

    def yu(q):
        t = lanes(q, -32)
        t = jnp.where(lane >= 96, rows(t, -1), t)
        return jnp.where((lane >= 96) & (sub == 7), 0.0, t)

    zd = lambda q: jnp.where(z == 0, 0.0, lanes(q, 1))
    zu = lambda q: jnp.where(z == 31, 0.0, lanes(q, -1))
    return yd, yu, zd, zu


def burn_once(p, f, rate):
    burned = f * pl.reciprocal(1.0 + 0.5 * rate * (1.0 + 0.5 * jnp.tanh(p)), approx=True)
    return p + 0.5 * (f - burned), burned


def face_values(p, n, t1, t2, f, axis, high):
    sign = -1.0 if high else 1.0
    return [NB * (p + sign * n), NB * t1, NB * t2, NB * (1 + sign * ADV[axis]) * f]


def ghost_step(near, far, own, dlo, dhi, rate, axis, high):
    n, r = (1, 2) if axis == 0 else (2, 1)
    row, lane = iota((16, 128), 0), iota((16, 128), 1)
    an, ar, az = ADV[axis], ADV[1 - axis], ADV[2]
    minus, plus = (own, far) if high else (far, own)
    p, w, f = near[0], near[3], near[4]

    def rd(q, d):
        return jnp.where(row == 0, d, rows(q, 1))

    def ru(q, d):
        return jnp.where(row == 15, d, rows(q, -1))

    zd = lambda q: jnp.where(lane == 0, 0.0, lanes(q, 1))
    zu = lambda q: jnp.where(lane == 127, 0.0, lanes(q, -1))
    sn, mn = minus[0] + minus[n], plus[0] - plus[n]
    sr, mr = rd(p + near[r], dlo[0] + dlo[r]), ru(p - near[r], dhi[0] - dhi[r])
    sz, mz = zd(p + w), zu(p - w)
    hp = (sn + mn) + (sr + mr) + (sz + mz)
    hn = (sn - mn) + (rd(near[n], dlo[n]) + ru(near[n], dhi[n])) + (zd(near[n]) + zu(near[n]))
    hr = (minus[r] + plus[r]) + (sr - mr) + (zd(near[r]) + zu(near[r]))
    hw = (minus[3] + plus[3]) + (rd(w, dlo[3]) + ru(w, dhi[3])) + (sz - mz)
    hf = (
        ((1 + an) * minus[4] + (1 - an) * plus[4])
        + ((1 + ar) * rd(f, dlo[4]) + (1 - ar) * ru(f, dhi[4]))
        + ((1 + az) * zd(f) + (1 - az) * zu(f))
    )
    pressure, normal, tangent, across, fuel = (
        KEEP * a + NB * b for a, b in zip((p, near[n], near[r], w, f), (hp, hn, hr, hw, hf))
    )
    pressure, fuel = burn_once(pressure, fuel, rate)
    return face_values(pressure, normal, tangent, across, fuel, axis, high)


def kernel(
    coarse, fine, crate, frate, parents, steps, coarse_out, fine_out,
    c, h, cr, xh, xr, ys, yh, ds, dr, fv, zv, table, keys, p1, r1a, r1b, p2, r2a, r2b, f0, f1, fa, fb, fr, gt, ey,
    mb, r3, p4, r4, ssem, rsem, lsem, tsem,
):
    r1, r2 = (r1a, r1b), (r2a, r2b)
    region, me = lax.axis_index("region"), lax.axis_index("inner")
    up, down = lax.rem(region + 1, REGIONS), lax.rem(region + REGIONS - 1, REGIONS)
    right, left = lax.rem(me + 1, INNER), lax.rem(me + INNER - 1, INNER)
    plane, mine = (me // 8) * 8, lax.rem(me, 8)
    sub, lane = iota((8, 128), 0), iota((8, 128), 1)

    loads = [
        pltpu.make_async_copy(coarse, c.at[:, pl.ds(16, 256)], lsem.at[0]),
        pltpu.make_async_copy(crate, cr, lsem.at[1]),
    ]
    for j in range(8):
        cut = pl.ds(j * 128, 128)
        loads.append(pltpu.make_async_copy(fine.at[:, :, cut], f0.at[:, pl.ds(1, 32), j], lsem.at[2 + j]))
        loads.append(pltpu.make_async_copy(frate.at[:, cut], fr.at[:, j], lsem.at[10 + j]))
    for load in loads:
        load.start()
    barrier = pltpu.get_barrier_semaphore()

    def greet(k, carry):
        pl.semaphore_signal(
            barrier, inc=1, device_id=(region, lax.rem(me + 1 + k, INNER)), device_id_type=MESH
        )
        return carry

    lax.fori_loop(0, INNER - 1, greet, 0)
    others = [(up, me), (down, me), (up, right), (up, left), (down, right), (down, left)]
    for other in others:
        pl.semaphore_signal(barrier, inc=1, device_id=other, device_id_type=MESH)

    block_row = jnp.broadcast_to(parents[...], (32, 32))
    ri, ci = iota((32, 32), 0), iota((32, 32), 1)
    block = jnp.sum(jnp.where(ri == ci, block_row, 0), axis=1, keepdims=True)
    owner = block >> 3
    slot = jnp.sum(
        jnp.where((jnp.broadcast_to(owner, (32, 32)) == (block_row >> 3)) & (ci < ri), 1, 0),
        axis=1,
        keepdims=True,
    )
    key = jnp.broadcast_to(owner * 2 + slot, (32, 128))
    ri, ci = iota((32, 128), 0), iota((32, 128), 1)
    layer = jnp.broadcast_to((block & 7) + 1, (32, 128))
    key_row = jnp.sum(jnp.where(ri == ci, key, 0), axis=0, keepdims=True)
    patch_row = jnp.sum(jnp.where(key == ci, ri, 0), axis=0, keepdims=True)
    layer_row = jnp.sum(jnp.where(key == ci, layer, 0), axis=0, keepdims=True) - 1
    table[...] = jnp.where(
        sub == 0,
        jnp.broadcast_to(key_row, (8, 128)),
        jnp.where(sub == 1, jnp.broadcast_to(patch_row, (8, 128)), jnp.broadcast_to(layer_row, (8, 128))),
    )
    look = pltpu.make_async_copy(table, keys, tsem)
    look.start()

    zero = jnp.zeros((8, 128), F32)
    for i in range(5):
        c[i, 0:16] = jnp.zeros((16, 128), F32)
        c[i, 272:288] = jnp.zeros((16, 128), F32)
        for a in (0, 33):
            f0[i, a] = zero
            f1[i, a] = zero
    loads[0].wait()
    loads[1].wait()
    for side, (near, far) in enumerate(((15, 14), (0, 1))):
        for half in range(2):
            dst = pl.ds(half * 8, 8)
            for i in range(5):
                ys[side, i, dst] = c[i, pl.ds(16 + half * 128 + near, 8, stride=16)]
                ys[side, 6 + i, dst] = c[i, pl.ds(16 + half * 128 + far, 8, stride=16)]
            ys[side, 5, dst] = cr[pl.ds(half * 128 + near, 8, stride=16)]
    for n, at in enumerate((255, 240, 15, 0)):
        for i in range(5):
            ds[n, i : i + 1] = c[i, 16 + at : 17 + at]
        ds[n, 5:8] = jnp.zeros((3, 128), F32)

    pl.semaphore_wait(barrier, INNER - 1 + len(others))

    def remote(src, dst, n, to):
        return pltpu.make_async_remote_copy(
            src_ref=src, dst_ref=dst, send_sem=ssem.at[n], recv_sem=rsem.at[n], device_id=to, device_id_type=MESH
        )

    halos = [
        remote(ds.at[0], dr.at[0], 0, (up, right)),
        remote(ds.at[1], dr.at[1], 1, (up, left)),
        remote(ds.at[2], dr.at[2], 2, (down, right)),
        remote(ds.at[3], dr.at[3], 3, (down, left)),
        remote(ys.at[0], yh.at[0], 4, (region, right)),
        remote(ys.at[1], yh.at[1], 5, (region, left)),
        remote(c.at[:, pl.ds(16 + 224, 32)], xh.at[0], 6, (up, me)),
        remote(c.at[:, pl.ds(16, 32)], xh.at[1], 7, (down, me)),
        remote(cr.at[pl.ds(240, 16)], xr.at[0], 8, (up, me)),
        remote(cr.at[pl.ds(0, 16)], xr.at[1], 9, (down, me)),
    ]
    for halo in halos:
        halo.start()

    shifts = coarse_shifts((16, 128))

    def coarse_plane(x, carry):
        at = pl.multiple_of(x * 16, 16)
        cells = [c[i, pl.ds(at + 16, 16)] for i in range(5)]
        below = [c[i, pl.ds(at, 16)] for i in range(5)]
        above = [c[i, pl.ds(at + 32, 16)] for i in range(5)]
        for i, q in enumerate(hydro(cells, below, above, *shifts)):
            h[i, pl.ds(at, 16)] = q
        return carry

    lax.fori_loop(0, 16, coarse_plane, 0)

    look.wait()
    slots = [keys[2, 2 * me], keys[2, 2 * me + 1]]
    my_key = keys[0, me]

    side = lane % 2
    code = ((lane % 64) // 4) * 4 + (lane // 64) * 2 + (lane % 4) // 2
    picks = [lax.rem(jnp.where(side == 0, 16 * s + 127, 16 * s + 16) + 128, 128) for s in slots]
    cuts = [16 * jnp.maximum(s, 0) + lane % 16 for s in slots]
    inside = [
        jnp.where(((side == 0) & (s == 0)) | ((side == 1) & (s == 7)), 0.0, 1.0) for s in slots
    ]

    def z_values(src, base):
        low = iota((16, 128), 1) % 16 == 15

        def body(x, carry):
            at = pl.multiple_of(x * 16, 16)
            p, u, v, w, f = (src[i, pl.ds(at + base, 16)] for i in range(5))
            zv[0, pl.ds(at, 16)] = NB * (p + jnp.where(low, w, -w))
            zv[1, pl.ds(at, 16)] = NB * u
            zv[2, pl.ds(at, 16)] = NB * v
            zv[3, pl.ds(at, 16)] = f * jnp.where(low, NB * (1 + ADV[2]), NB * (1 - ADV[2]))
            return carry

        lax.fori_loop(0, 16, body, 0)

    def z_tiles():
        def body(x, tiles):
            tiles = list(tiles)
            for v in range(4):
                for odd in range(2):
                    q = zv[v, pl.ds(x * 16 + odd, 8, stride=2)]
                    here = code == x * 4 + (v % 2) * 2 + odd
                    for s in range(2):
                        tiles[s * 2 + v // 2] = jnp.where(here, take(q, picks[s]), tiles[s * 2 + v // 2])
            return tuple(tiles)

        tiles = lax.fori_loop(0, 16, body, (zero,) * 4)
        return [[tiles[s * 2 + w] * inside[s] for w in range(2)] for s in range(2)]

    def xy_tile(face, s):
        tile = zero
        for v in range(4):
            for odd in range(2):
                pos = v * 32 + odd * 16
                q = fv[face, v, pl.ds(odd, 8, stride=2)]
                tile = jnp.where(lane // 16 == pos // 16, take(q, cuts[s]), tile)
        return tile

    def put_tile(t, s, face, tile):
        p1[t, pl.ds(s * 8 + face, 8, stride=16)] = tile

    def get_tile(t, s, face):
        return p1[t, pl.ds(s * 8 + face, 8, stride=16)]

    for t in range(2):
        for s in range(2):
            for face in (6, 7):
                put_tile(t, s, face, zero)

    z_values(c, 16)
    for s, pair in enumerate(z_tiles()):
        for w, tile in enumerate(pair):
            put_tile(0, s, 4 + w, tile)

    for halo in halos:
        halo.wait_recv()
    mx = [jnp.where(region > 0, 1.0, 0.0), jnp.where(region < REGIONS - 1, 1.0, 0.0)]
    my = [jnp.where(me > 0, 1.0, 0.0), jnp.where(me < INNER - 1, 1.0, 0.0)]

    def near_x(e):
        return [xh[e, i, pl.ds(16 - 16 * e, 16)] for i in range(5)]

    def near_y(e):
        return [yh[e, i] for i in range(5)]

    for e in range(2):
        p, u, v, w, f = near_x(e)
        for i, q in enumerate(face_values(p, u, v, w, f, 0, e == 1)):
            fv[e, i] = mx[e] * q
        p, u, v, w, f = near_y(e)
        for i, q in enumerate(face_values(p, v, u, w, f, 1, e == 1)):
            fv[2 + e, i] = my[e] * q
    for s in range(2):
        for face in range(4):
            put_tile(0, s, face, xy_tile(face, s))

    def send_pieces(t):
        r1[t][mine] = p1[t, pl.ds(mine * 16, 16)]

        def body(k, carry):
            to = lax.rem(mine + 1 + k, 8)
            remote(
                p1.at[t, pl.ds(to * 16, 16)], r1[t].at[mine], 10 + t, (region, plane + to)
            ).start()
            return carry

        lax.fori_loop(0, 7, body, 0)

    def far_first(k):
        return lax.rem(me + 1 + lax.rem(15 + k, INNER - 1), INNER)

    send_pieces(0)

    def add_face(ref, cut, face, n, t1, high):
        e0, e1, e2, e3 = (fv[face, v, pl.ds(8 * cut[0], 8)] for v in range(4))
        at = cut[1]
        ref[0, at] = ref[0, at] + e0
        ref[n, at] = ref[n, at] - e0 if high else ref[n, at] + e0
        ref[t1, at] = ref[t1, at] + e1
        ref[3, at] = ref[3, at] + e2
        ref[4, at] = ref[4, at] + e3

    for half in range(2):
        add_face(h, (half, pl.ds(half * 8, 8)), 0, 1, 2, False)
        add_face(h, (half, pl.ds(240 + half * 8, 8)), 1, 1, 2, True)
        add_face(h, (half, pl.ds(half * 128, 8, stride=16)), 2, 2, 1, False)
        add_face(h, (half, pl.ds(half * 128 + 15, 8, stride=16)), 3, 2, 1, True)

    def coarse_burn(x, carry):
        at = pl.multiple_of(x * 64, 64)
        p, f = burn_once(h[0, pl.ds(at, 64)], h[4, pl.ds(at, 64)], cr[pl.ds(at, 64)])
        h[0, pl.ds(at, 64)] = p
        h[4, pl.ds(at, 64)] = f
        return carry

    lax.fori_loop(0, 4, coarse_burn, 0)

    def own_rows(axis, e):
        if axis == 0:
            return [c[i, pl.ds(16 + 240 * e, 16)] for i in range(5)]
        return [
            jnp.concatenate([c[i, pl.ds(16 + 128 * b + 15 * e, 8, stride=16)] for b in range(2)], axis=0)
            for i in range(5)
        ]

    def corner(n, scale):
        return [dr[n, i : i + 1] * scale for i in range(5)]

    for e in range(2):
        far = [xh[e, i, pl.ds(16 * e, 16)] for i in range(5)]
        values = ghost_step(
            near_x(e), far, own_rows(0, e), corner(2 * e, my[0]), corner(2 * e + 1, my[1]), xr[e], 0, e == 1
        )
        for i, q in enumerate(values):
            fv[e, i] = mx[e] * q
        far = [yh[e, 6 + i] for i in range(5)]
        values = ghost_step(
            near_y(e), far, own_rows(1, e), corner(e, mx[0]), corner(2 + e, mx[1]), yh[e, 5], 1, e == 1
        )
        for i, q in enumerate(values):
            fv[2 + e, i] = my[e] * q
    z_values(h, 0)
    for s, pair in enumerate(z_tiles()):
        for w, tile in enumerate(pair):
            put_tile(1, s, 4 + w, 0.5 * (get_tile(0, s, 4 + w) + tile))
        for face in range(4):
            put_tile(1, s, face, 0.5 * (get_tile(0, s, face) + xy_tile(face, s)))
    send_pieces(1)

    for load in loads[2:]:
        load.wait()
    count = steps[0]
    counted = jnp.broadcast_to(count, (8, 128)).astype(F32)
    span = 0.25 / counted
    fine_shift = fine_shifts()

    def rates(x, carry):
        q = span * fr[x]
        fa[x] = 1.0 + q
        fb[x] = 0.5 * q
        return carry

    lax.fori_loop(0, 32, rates, 0)

    def fine_hydro(src, dst):
        def body(x, carry):
            cells = [src[i, x + 1] for i in range(5)]
            below = [src[i, x] for i in range(5)]
            above = [src[i, x + 2] for i in range(5)]
            for i, q in enumerate(hydro(cells, below, above, *fine_shift)):
                dst[i, x + 1] = q
            return carry

        lax.fori_loop(0, 32, body, 0)

    fine_hydro(f0, f1)

    def wait_all(ref, sem):
        pltpu.make_async_copy(ref, ref, sem).wait()

    def send_faces(t):
        wait_all(r1[t].at[pl.ds(0, 7)], rsem.at[10 + t])

        def piece(key):
            pair = r1[t][(key & 15) >> 1]
            return jnp.where((key & 1) == 0, pair[0:8], pair[8:16])

        r2[t][me] = piece(my_key)

        def body(k, carry):
            to = far_first(k)
            p2[t, to] = piece(keys[0, to])
            remote(p2.at[t, to], r2[t].at[me], 12 + t, (region, to)).start()
            return carry

        lax.fori_loop(0, INNER - 1, body, 0)

    send_faces(0)
    send_faces(1)

    q4, z = lane // 32, lane % 32
    edge_y = jnp.where((lane < 32) & (sub == 0) | (lane >= 96) & (sub == 7), 1.0, 0.0)
    sign_y = jnp.where(lane < 64, edge_y, -edge_y)
    edge_z = jnp.where((z == 0) | (z == 31), 1.0, 0.0)
    sign_z = jnp.where(z < 16, edge_z, -edge_z)
    pick_x = (q4 // 2) * 16 + z // 2
    pick_z = (q4 // 2) * 2 + z // 16

    def add_ghosts(t, dst):
        wait_all(r2[t].at[pl.ds(0, INNER - 1)], rsem.at[12 + t])
        start = (my_key >> 4) * 8
        for k in range(8):
            gt[pl.ds(k * 8, 8)] = r2[t][start + k]
        tiles = [gt[pl.ds(face, 8, stride=8)] for face in range(6)]
        for face, x in ((0, 1), (1, 32)):
            e = [take(tiles[face], pick_x + 32 * v) for v in range(4)]
            dst[0, x] = dst[0, x] + e[0]
            dst[1, x] = dst[1, x] + e[0] if face == 0 else dst[1, x] - e[0]
            dst[2, x] = dst[2, x] + e[1]
            dst[3, x] = dst[3, x] + e[2]
            dst[4, x] = dst[4, x] + e[3]
        for v in range(4):
            for odd in range(2):
                pick = v * 32 + odd * 16 + z // 2
                ey[v, pl.ds(odd, 8, stride=2)] = jnp.where(lane < 64, take(tiles[2], pick), take(tiles[3], pick))

        def body(x, carry):
            y = [jnp.broadcast_to(ey[v, pl.ds(x, 1)], (8, 128)) for v in range(4)]
            zz = [take(tiles[4 + v // 2], pick_z + ((v % 2) * 64 + x * 4)) for v in range(4)]
            add = [
                edge_y * y[0] + edge_z * zz[0],
                edge_y * y[1] + edge_z * zz[1],
                sign_y * y[0] + edge_z * zz[2],
                edge_y * y[2] + sign_z * zz[0],
                edge_y * y[3] + edge_z * zz[3],
            ]
            for i in range(5):
                dst[i, 2 * x + 1] = dst[i, 2 * x + 1] + add[i]
                dst[i, 2 * x + 2] = dst[i, 2 * x + 2] + add[i]
            return carry

        lax.fori_loop(0, 16, body, 0)

    live = [jnp.where(turn < count, 1.0, 0.0) for turn in range(BURN_MAX)]
    group = 16

    def burn(dst):
        def body(g, carry):
            at = g * group
            p = [dst[0, at + i + 1] for i in range(group)]
            f = [dst[4, at + i + 1] for i in range(group)]
            for turn in range(BURN_MAX):
                for i in range(group):
                    r = pl.reciprocal(fa[at + i] + fb[at + i] * jnp.tanh(p[i]), approx=True)
                    d = live[turn] * (f[i] - f[i] * r)
                    f[i] = f[i] - d
                    p[i] = p[i] + 0.5 * d
            for i in range(group):
                dst[0, at + i + 1] = p[i]
                dst[4, at + i + 1] = f[i]
            return carry

        lax.fori_loop(0, 32 // group, body, 0)

    add_ghosts(0, f1)
    burn(f1)
    fine_hydro(f1, f0)
    add_ghosts(1, f0)
    burn(f0)

    stores = []
    for j in range(8):
        stores.append(
            pltpu.make_async_copy(
                f0.at[:, pl.ds(1, 32), j], fine_out.at[:, :, pl.ds(j * 128, 128)], lsem.at[2 + j]
            )
        )
        stores[-1].start()
    pick_m = ((lane % 32) // 16) * 64 + 2 * (lane % 16)

    def means(a, carry):
        for i in range(5):
            tile = zero
            for g in range(4):
                at = a * 8 + 2 * g
                q = f0[i, at + 1] + f0[i, at + 2]
                q = q + lanes(q, -1)
                q = q + lanes(q, -32)
                tile = jnp.where(q4 == g, take(q, pick_m), tile)
            mb[pl.ds(a * 64 + i, 8, stride=8)] = 0.125 * tile
        for i in range(5, 8):
            mb[pl.ds(a * 64 + i, 8, stride=8)] = zero
        return carry

    lax.fori_loop(0, 4, means, 0)

    r3[me] = mb[pl.ds(me * 8, 8)]

    def send_mean(k, carry):
        to = far_first(k)
        remote(mb.at[pl.ds(to * 8, 8)], r3.at[me], 14, (region, to)).start()
        return carry

    lax.fori_loop(0, INNER - 1, send_mean, 0)
    wait_all(r3.at[pl.ds(0, 31)], rsem.at[14])

    def pick_pair(to):
        return [r3[keys[1, 2 * to + s]] for s in range(2)]

    for s, q in enumerate(pick_pair(me)):
        r4[pl.ds(me * 16 + 8 * s, 8)] = q

    def send_pair(k, carry):
        to = far_first(k)
        for s, q in enumerate(pick_pair(to)):
            p4[pl.ds(to * 16 + 8 * s, 8)] = q
        remote(p4.at[pl.ds(to * 16, 16)], r4.at[pl.ds(me * 16, 16)], 15, (region, to)).start()
        return carry

    lax.fori_loop(0, INNER - 1, send_pair, 0)
    wait_all(r4.at[pl.ds(0, 31 * 16)], rsem.at[15])

    def place(n, carry):
        i, a = n // 4, n % 4
        for s in range(2):
            tile = r4[pl.ds(a * 128 + s * 8 + i, 8, stride=16)]
            here = lane // 16 == slots[s]
            for g in range(4):
                for odd in range(2):
                    at = pl.ds((a * 4 + g) * 16 + odd, 8, stride=2)
                    h[i, at] = jnp.where(here, take(tile, lane % 16 + (g * 32 + odd * 16)), h[i, at])
        return carry

    lax.fori_loop(0, 20, place, 0)
    last = pltpu.make_async_copy(h, coarse_out, lsem.at[0])
    last.start()

    for halo in halos:
        halo.wait_send()
    for t in range(2):
        wait_all(p1.at[t, pl.ds(0, 7 * 16)], ssem.at[10 + t])
        wait_all(p2.at[t, pl.ds(0, INNER - 1)], ssem.at[12 + t])
    wait_all(mb.at[pl.ds(0, 31 * 8)], ssem.at[14])
    wait_all(p4.at[pl.ds(0, 31 * 16)], ssem.at[15])
    for store in stores:
        store.wait()
    last.wait()


def per_device(coarse_state, fine_state, coarse_rate, fine_rate, parents, burn_steps):
    vmem, smem, anywhere = (
        pl.BlockSpec(memory_space=pltpu.VMEM),
        pl.BlockSpec(memory_space=pltpu.SMEM),
        pl.BlockSpec(memory_space=pl.ANY),
    )
    coarse_new, fine_new = pl.pallas_call(
        kernel,
        out_shape=(
            jax.ShapeDtypeStruct((5, 256, 128), F32),
            jax.ShapeDtypeStruct((5, 32, 1024), F32),
        ),
        in_specs=[anywhere, anywhere, anywhere, anywhere, vmem, smem],
        out_specs=(anywhere, anywhere),
        scratch_shapes=[
            pltpu.VMEM((5, 288, 128), F32),
            pltpu.VMEM((5, 256, 128), F32),
            pltpu.VMEM((256, 128), F32),
            pltpu.VMEM((2, 5, 32, 128), F32),
            pltpu.VMEM((2, 16, 128), F32),
            pltpu.VMEM((2, 11, 16, 128), F32),
            pltpu.VMEM((2, 11, 16, 128), F32),
            pltpu.VMEM((4, 8, 128), F32),
            pltpu.VMEM((4, 8, 128), F32),
            pltpu.VMEM((4, 4, 16, 128), F32),
            pltpu.VMEM((4, 256, 128), F32),
            pltpu.VMEM((8, 128), jnp.int32),
            pltpu.SMEM((8, 128), jnp.int32),
            pltpu.VMEM((2, 128, 128), F32),
            pltpu.VMEM((8, 16, 128), F32),
            pltpu.VMEM((8, 16, 128), F32),
            pltpu.VMEM((2, 32, 8, 128), F32),
            pltpu.VMEM((32, 8, 128), F32),
            pltpu.VMEM((32, 8, 128), F32),
            pltpu.VMEM((5, 34, 8, 128), F32),
            pltpu.VMEM((5, 34, 8, 128), F32),
            pltpu.VMEM((32, 8, 128), F32),
            pltpu.VMEM((32, 8, 128), F32),
            pltpu.VMEM((32, 8, 128), F32),
            pltpu.VMEM((64, 128), F32),
            pltpu.VMEM((4, 16, 128), F32),
            pltpu.VMEM((256, 128), F32),
            pltpu.VMEM((32, 8, 128), F32),
            pltpu.VMEM((512, 128), F32),
            pltpu.VMEM((512, 128), F32),
            pltpu.SemaphoreType.DMA((16,)),
            pltpu.SemaphoreType.DMA((16,)),
            pltpu.SemaphoreType.DMA((18,)),
            pltpu.SemaphoreType.DMA,
        ],
        compiler_params=pltpu.CompilerParams(
            collective_id=0, has_side_effects=True, vmem_limit_bytes=40 * 2**20
        ),
        name="reactive_step",
    )(
        coarse_state.reshape(5, 256, 128),
        fine_state.reshape(5, 32, 1024),
        coarse_rate.reshape(256, 128),
        fine_rate.reshape(32, 1024),
        parents,
        burn_steps,
    )
    return coarse_new.reshape(5, 16, 16, 128), fine_new.reshape(1, 5, 32, 1024)


def solution(mesh):
    in_specs = (
        P(None, "region", "inner", None),
        P(("region", "inner"), None, None, None),
        P("region", "inner", None),
        P(("region", "inner"), None, None),
        P("region", None),
        P(("region", "inner")),
    )
    out_specs = (P(None, "region", "inner", None), P(("region", "inner"), None, None, None))
    return jax.shard_map(per_device, mesh=mesh, in_specs=in_specs, out_specs=out_specs, check_vma=False)
```

```python
import functools

import jax
import jax.numpy as jnp
from jax import lax
from jax.experimental import pallas as pl
from jax.experimental.pallas import tpu as pltpu
from jax.sharding import PartitionSpec as P

MESH = pl.DeviceIdType.MESH
F32 = jnp.float32
ADV = (0.5, -0.3, 0.2)
KEEP = 0.1
NB = 0.15
BURN_MAX = 8
REGIONS = 4
INNER = 32


def iota(shape, axis):
    return lax.broadcasted_iota(jnp.int32, shape, axis)


def lanes(q, shift):
    return pltpu.roll(q, shift % 128, 1)


def rows(q, shift):
    return pltpu.roll(q, shift % q.shape[0], 0)


def hydro(c, xm, xp, yd, yu, zd, zu):
    p, u, v, w, f = c
    sx, mx = xm[0] + xm[1], xp[0] - xp[1]
    sy, my = yd(p + v), yu(p - v)
    sz, mz = zd(p + w), zu(p - w)
    hp = (sx + mx) + (sy + my) + (sz + mz)
    hu = (sx - mx) + (yd(u) + yu(u)) + (zd(u) + zu(u))
    hv = (xm[2] + xp[2]) + (sy - my) + (zd(v) + zu(v))
    hw = (xm[3] + xp[3]) + (yd(w) + yu(w)) + (sz - mz)
    hf = (
        ((1 + ADV[0]) * xm[4] + (1 - ADV[0]) * xp[4])
        + ((1 + ADV[1]) * yd(f) + (1 - ADV[1]) * yu(f))
        + ((1 + ADV[2]) * zd(f) + (1 - ADV[2]) * zu(f))
    )
    return [KEEP * a + NB * b for a, b in zip(c, (hp, hu, hv, hw, hf))]


def take(q, index):
    return jnp.take_along_axis(q, index, axis=1, mode="promise_in_bounds")


def coarse_shifts(shape):
    row, lane = iota(shape, 0), iota(shape, 1)
    zd = lambda q: jnp.where(lane == 0, 0.0, lanes(q, 1))
    zu = lambda q: jnp.where(lane == 127, 0.0, lanes(q, -1))
    yd = lambda q: jnp.where(row == 0, 0.0, rows(q, 1))
    yu = lambda q: jnp.where(row == shape[0] - 1, 0.0, rows(q, -1))
    return yd, yu, zd, zu


def fine_shifts():
    sub, lane = iota((8, 128), 0), iota((8, 128), 1)
    z = lane % 32

    def yd(q):
        t = lanes(q, 32)
        t = jnp.where(lane < 32, rows(t, 1), t)
        return jnp.where((lane < 32) & (sub == 0), 0.0, t)

    def yu(q):
        t = lanes(q, -32)
        t = jnp.where(lane >= 96, rows(t, -1), t)
        return jnp.where((lane >= 96) & (sub == 7), 0.0, t)

    zd = lambda q: jnp.where(z == 0, 0.0, lanes(q, 1))
    zu = lambda q: jnp.where(z == 31, 0.0, lanes(q, -1))
    return yd, yu, zd, zu


def burn_once(p, f, rate):
    burned = f * pl.reciprocal(1.0 + 0.5 * rate * (1.0 + 0.5 * jnp.tanh(p)), approx=True)
    return p + 0.5 * (f - burned), burned


def face_values(p, n, t1, t2, f, axis, high):
    sign = -1.0 if high else 1.0
    return [NB * (p + sign * n), NB * t1, NB * t2, NB * (1 + sign * ADV[axis]) * f]


def ghost_step(near, far, own, dlo, dhi, rate, axis, high):
    n, r = (1, 2) if axis == 0 else (2, 1)
    row, lane = iota((16, 128), 0), iota((16, 128), 1)
    an, ar, az = ADV[axis], ADV[1 - axis], ADV[2]
    minus, plus = (own, far) if high else (far, own)
    p, w, f = near[0], near[3], near[4]

    def rd(q, d):
        return jnp.where(row == 0, d, rows(q, 1))

    def ru(q, d):
        return jnp.where(row == 15, d, rows(q, -1))

    zd = lambda q: jnp.where(lane == 0, 0.0, lanes(q, 1))
    zu = lambda q: jnp.where(lane == 127, 0.0, lanes(q, -1))
    sn, mn = minus[0] + minus[n], plus[0] - plus[n]
    sr, mr = rd(p + near[r], dlo[0] + dlo[r]), ru(p - near[r], dhi[0] - dhi[r])
    sz, mz = zd(p + w), zu(p - w)
    hp = (sn + mn) + (sr + mr) + (sz + mz)
    hn = (sn - mn) + (rd(near[n], dlo[n]) + ru(near[n], dhi[n])) + (zd(near[n]) + zu(near[n]))
    hr = (minus[r] + plus[r]) + (sr - mr) + (zd(near[r]) + zu(near[r]))
    hw = (minus[3] + plus[3]) + (rd(w, dlo[3]) + ru(w, dhi[3])) + (sz - mz)
    hf = (
        ((1 + an) * minus[4] + (1 - an) * plus[4])
        + ((1 + ar) * rd(f, dlo[4]) + (1 - ar) * ru(f, dhi[4]))
        + ((1 + az) * zd(f) + (1 - az) * zu(f))
    )
    pressure, normal, tangent, across, fuel = (
        KEEP * a + NB * b for a, b in zip((p, near[n], near[r], w, f), (hp, hn, hr, hw, hf))
    )
    pressure, fuel = burn_once(pressure, fuel, rate)
    return face_values(pressure, normal, tangent, across, fuel, axis, high)


def kernel(
    coarse, fine, crate, frate, parents, steps, h_out, fine_out, r4, table_out,
    c, h, cr, xh, xr, ys, yh, ds, dr, fv, zv, table, keys, p1, r1a, r1b, p2, r2a, r2b, f0, f1, fa, fb, fr, gt, ey,
    mb, r3, p4, pv, sv, ssem, rsem, lsem, tsem,
):
    r1, r2 = (r1a, r1b), (r2a, r2b)
    region, me = lax.axis_index("region"), lax.axis_index("inner")
    up, down = lax.rem(region + 1, REGIONS), lax.rem(region + REGIONS - 1, REGIONS)
    right, left = lax.rem(me + 1, INNER), lax.rem(me + INNER - 1, INNER)
    plane, mine = (me // 8) * 8, lax.rem(me, 8)
    sub, lane = iota((8, 128), 0), iota((8, 128), 1)

    def far_first(k):
        return lax.rem(me + 1 + lax.rem(15 + k, INNER - 1), INNER)

    barrier = pltpu.get_barrier_semaphore()
    others = [(up, right), (up, left), (down, right), (down, left), (up, me), (down, me)]
    for other in others:
        pl.semaphore_signal(barrier, inc=1, device_id=other, device_id_type=MESH)

    def greet(k, carry):
        pl.semaphore_signal(barrier, inc=1, device_id=(region, far_first(k)), device_id_type=MESH)
        return carry

    lax.fori_loop(0, INNER - 1, greet, 0)
    loads = [
        pltpu.make_async_copy(coarse, c.at[:, pl.ds(16, 256)], lsem.at[0]),
        pltpu.make_async_copy(crate, cr, lsem.at[1]),
        pltpu.make_async_copy(parents, pv, lsem.at[18]),
        pltpu.make_async_copy(steps, sv, lsem.at[19]),
    ]
    for j in range(8):
        cut = pl.ds(j * 128, 128)
        loads.append(pltpu.make_async_copy(fine.at[:, :, cut], f0.at[:, pl.ds(1, 32), j], lsem.at[2 + j]))
        loads.append(pltpu.make_async_copy(frate.at[:, cut], fr.at[:, j], lsem.at[10 + j]))
    for load in loads:
        load.start()

    zero = jnp.zeros((8, 128), F32)
    for i in range(5):
        c[i, 0:16] = jnp.zeros((16, 128), F32)
        c[i, 272:288] = jnp.zeros((16, 128), F32)
        for a in (0, 33):
            f0[i, a] = zero
            f1[i, a] = zero
    loads[0].wait()
    loads[1].wait()
    for side, (near, far) in enumerate(((15, 14), (0, 1))):
        for half in range(2):
            dst = pl.ds(half * 8, 8)
            for i in range(5):
                ys[side, i, dst] = c[i, pl.ds(16 + half * 128 + near, 8, stride=16)]
                ys[side, 6 + i, dst] = c[i, pl.ds(16 + half * 128 + far, 8, stride=16)]
            ys[side, 5, dst] = cr[pl.ds(half * 128 + near, 8, stride=16)]
    for n, at in enumerate((255, 240, 15, 0)):
        for i in range(5):
            ds[n, i : i + 1] = c[i, 16 + at : 17 + at]
        ds[n, 5:8] = jnp.zeros((3, 128), F32)

    pl.semaphore_wait(barrier, INNER - 1 + len(others))

    def remote(src, dst, n, to):
        return pltpu.make_async_remote_copy(
            src_ref=src, dst_ref=dst, send_sem=ssem.at[n], recv_sem=rsem.at[n], device_id=to, device_id_type=MESH
        )

    halos = [
        remote(ds.at[0], dr.at[0], 0, (up, right)),
        remote(ds.at[1], dr.at[1], 1, (up, left)),
        remote(ds.at[2], dr.at[2], 2, (down, right)),
        remote(ds.at[3], dr.at[3], 3, (down, left)),
        remote(ys.at[0], yh.at[0], 4, (region, right)),
        remote(ys.at[1], yh.at[1], 5, (region, left)),
        remote(c.at[:, pl.ds(16 + 224, 32)], xh.at[0], 6, (up, me)),
        remote(c.at[:, pl.ds(16, 32)], xh.at[1], 7, (down, me)),
        remote(cr.at[pl.ds(240, 16)], xr.at[0], 8, (up, me)),
        remote(cr.at[pl.ds(0, 16)], xr.at[1], 9, (down, me)),
    ]
    for halo in halos:
        halo.start()

    loads[2].wait()
    block_row = jnp.broadcast_to(pv[...], (32, 32))
    ri, ci = iota((32, 32), 0), iota((32, 32), 1)
    block = jnp.sum(jnp.where(ri == ci, block_row, 0), axis=1, keepdims=True)
    owner = block >> 3
    slot = jnp.sum(
        jnp.where((jnp.broadcast_to(owner, (32, 32)) == (block_row >> 3)) & (ci < ri), 1, 0),
        axis=1,
        keepdims=True,
    )
    key = jnp.broadcast_to(owner * 2 + slot, (32, 128))
    ri, ci = iota((32, 128), 0), iota((32, 128), 1)
    layer = jnp.broadcast_to((block & 7) + 1, (32, 128))
    key_row = jnp.sum(jnp.where(ri == ci, key, 0), axis=0, keepdims=True)
    patch_row = jnp.sum(jnp.where(key == ci, ri, 0), axis=0, keepdims=True)
    layer_row = jnp.sum(jnp.where(key == ci, layer, 0), axis=0, keepdims=True) - 1
    table[...] = jnp.where(
        sub == 0,
        jnp.broadcast_to(key_row, (8, 128)),
        jnp.where(sub == 1, jnp.broadcast_to(patch_row, (8, 128)), jnp.broadcast_to(layer_row, (8, 128))),
    )
    keep = pltpu.make_async_copy(table, table_out, lsem.at[18])
    keep.start()
    look = pltpu.make_async_copy(table, keys, tsem)
    look.start()

    shifts = coarse_shifts((16, 128))

    def coarse_plane(x, carry):
        at = pl.multiple_of(x * 16, 16)
        cells = [c[i, pl.ds(at + 16, 16)] for i in range(5)]
        below = [c[i, pl.ds(at, 16)] for i in range(5)]
        above = [c[i, pl.ds(at + 32, 16)] for i in range(5)]
        for i, q in enumerate(hydro(cells, below, above, *shifts)):
            h[i, pl.ds(at, 16)] = q
        return carry

    lax.fori_loop(0, 16, coarse_plane, 0, unroll=4)

    look.wait()
    slots = [keys[2, 2 * me], keys[2, 2 * me + 1]]
    my_key = keys[0, me]

    side = lane % 2
    code = ((lane % 64) // 4) * 4 + (lane // 64) * 2 + (lane % 4) // 2
    picks = [lax.rem(jnp.where(side == 0, 16 * s + 127, 16 * s + 16) + 128, 128) for s in slots]
    cuts = [16 * jnp.maximum(s, 0) + lane % 16 for s in slots]
    inside = [
        jnp.where(((side == 0) & (s == 0)) | ((side == 1) & (s == 7)), 0.0, 1.0) for s in slots
    ]

    def z_values(src, base):
        low = iota((16, 128), 1) % 16 == 15

        def body(x, carry):
            at = pl.multiple_of(x * 16, 16)
            p, u, v, w, f = (src[i, pl.ds(at + base, 16)] for i in range(5))
            zv[0, pl.ds(at, 16)] = NB * (p + jnp.where(low, w, -w))
            zv[1, pl.ds(at, 16)] = NB * u
            zv[2, pl.ds(at, 16)] = NB * v
            zv[3, pl.ds(at, 16)] = f * jnp.where(low, NB * (1 + ADV[2]), NB * (1 - ADV[2]))
            return carry

        lax.fori_loop(0, 16, body, 0, unroll=4)

    def z_tiles():
        def body(x, tiles):
            tiles = list(tiles)
            for v in range(4):
                for odd in range(2):
                    q = zv[v, pl.ds(x * 16 + odd, 8, stride=2)]
                    here = code == x * 4 + (v % 2) * 2 + odd
                    for s in range(2):
                        tiles[s * 2 + v // 2] = jnp.where(here, take(q, picks[s]), tiles[s * 2 + v // 2])
            return tuple(tiles)

        tiles = lax.fori_loop(0, 16, body, (zero,) * 4, unroll=8)
        return [[tiles[s * 2 + w] * inside[s] for w in range(2)] for s in range(2)]

    def xy_tile(face, s):
        tile = zero
        for v in range(4):
            for odd in range(2):
                pos = v * 32 + odd * 16
                q = fv[face, v, pl.ds(odd, 8, stride=2)]
                tile = jnp.where(lane // 16 == pos // 16, take(q, cuts[s]), tile)
        return tile

    def put_tile(t, s, face, tile):
        p1[t, pl.ds(s * 6 + face, 8, stride=16)] = tile

    def get_tile(t, s, face):
        return p1[t, pl.ds(s * 6 + face, 8, stride=16)]

    z_values(c, 16)
    for s, pair in enumerate(z_tiles()):
        for w, tile in enumerate(pair):
            put_tile(0, s, 4 + w, tile)

    for halo in halos:
        halo.wait_recv()
    mx = [jnp.where(region > 0, 1.0, 0.0), jnp.where(region < REGIONS - 1, 1.0, 0.0)]
    my = [jnp.where(me > 0, 1.0, 0.0), jnp.where(me < INNER - 1, 1.0, 0.0)]

    def near_x(e):
        return [xh[e, i, pl.ds(16 - 16 * e, 16)] for i in range(5)]

    def near_y(e):
        return [yh[e, i] for i in range(5)]

    for e in range(2):
        p, u, v, w, f = near_x(e)
        for i, q in enumerate(face_values(p, u, v, w, f, 0, e == 1)):
            fv[e, i] = mx[e] * q
        p, u, v, w, f = near_y(e)
        for i, q in enumerate(face_values(p, v, u, w, f, 1, e == 1)):
            fv[2 + e, i] = my[e] * q
    for s in range(2):
        for face in range(4):
            put_tile(0, s, face, xy_tile(face, s))

    def send_pieces(t):
        r1[t][mine, 0:12] = p1[t, pl.ds(mine * 16, 12)]

        def body(k, carry):
            to = lax.rem(mine + 1 + k, 8)
            remote(
                p1.at[t, pl.ds(to * 16, 12)], r1[t].at[mine, pl.ds(0, 12)], 10 + t, (region, plane + to)
            ).start()
            return carry

        lax.fori_loop(0, 7, body, 0)

    send_pieces(0)

    def add_face(ref, cut, face, n, t1, high):
        e0, e1, e2, e3 = (fv[face, v, pl.ds(8 * cut[0], 8)] for v in range(4))
        at = cut[1]
        ref[0, at] = ref[0, at] + e0
        ref[n, at] = ref[n, at] - e0 if high else ref[n, at] + e0
        ref[t1, at] = ref[t1, at] + e1
        ref[3, at] = ref[3, at] + e2
        ref[4, at] = ref[4, at] + e3

    for half in range(2):
        add_face(h, (half, pl.ds(half * 8, 8)), 0, 1, 2, False)
        add_face(h, (half, pl.ds(240 + half * 8, 8)), 1, 1, 2, True)
        add_face(h, (half, pl.ds(half * 128, 8, stride=16)), 2, 2, 1, False)
        add_face(h, (half, pl.ds(half * 128 + 15, 8, stride=16)), 3, 2, 1, True)

    def coarse_burn(x, carry):
        at = pl.multiple_of(x * 64, 64)
        p, f = burn_once(h[0, pl.ds(at, 64)], h[4, pl.ds(at, 64)], cr[pl.ds(at, 64)])
        h[0, pl.ds(at, 64)] = p
        h[4, pl.ds(at, 64)] = f
        return carry

    lax.fori_loop(0, 4, coarse_burn, 0, unroll=4)

    def own_rows(axis, e):
        if axis == 0:
            return [c[i, pl.ds(16 + 240 * e, 16)] for i in range(5)]
        return [
            jnp.concatenate([c[i, pl.ds(16 + 128 * b + 15 * e, 8, stride=16)] for b in range(2)], axis=0)
            for i in range(5)
        ]

    def corner(n, scale):
        return [dr[n, i : i + 1] * scale for i in range(5)]

    for e in range(2):
        far = [xh[e, i, pl.ds(16 * e, 16)] for i in range(5)]
        values = ghost_step(
            near_x(e), far, own_rows(0, e), corner(2 * e, my[0]), corner(2 * e + 1, my[1]), xr[e], 0, e == 1
        )
        for i, q in enumerate(values):
            fv[e, i] = mx[e] * q
        far = [yh[e, 6 + i] for i in range(5)]
        values = ghost_step(
            near_y(e), far, own_rows(1, e), corner(e, mx[0]), corner(2 + e, mx[1]), yh[e, 5], 1, e == 1
        )
        for i, q in enumerate(values):
            fv[2 + e, i] = my[e] * q
    z_values(h, 0)
    for s, pair in enumerate(z_tiles()):
        for w, tile in enumerate(pair):
            put_tile(1, s, 4 + w, 0.5 * (get_tile(0, s, 4 + w) + tile))
        for face in range(4):
            put_tile(1, s, face, 0.5 * (get_tile(0, s, face) + xy_tile(face, s)))
    send_pieces(1)
    stores = [pltpu.make_async_copy(h, h_out, lsem.at[0])]
    stores[0].start()

    for load in loads[3:]:
        load.wait()
    count = sv[0]
    counted = jnp.broadcast_to(count, (8, 128)).astype(F32)
    span = 0.25 / counted
    fine_shift = fine_shifts()

    def rates(x, carry):
        q = span * fr[x]
        fa[x] = 1.0 + q
        fb[x] = 0.5 * q
        return carry

    lax.fori_loop(0, 32, rates, 0, unroll=8)

    def fine_hydro(src, dst):
        def body(x, carry):
            cells = [src[i, x + 1] for i in range(5)]
            below = [src[i, x] for i in range(5)]
            above = [src[i, x + 2] for i in range(5)]
            for i, q in enumerate(hydro(cells, below, above, *fine_shift)):
                dst[i, x + 1] = q
            return carry

        lax.fori_loop(0, 32, body, 0, unroll=8)

    fine_hydro(f0, f1)

    def wait_all(ref, sem):
        pltpu.make_async_copy(ref, ref, sem).wait()

    def send_faces(t):
        wait_all(r1[t].at[pl.ds(0, 7), pl.ds(0, 12)], rsem.at[10 + t])

        def piece(key):
            pair = r1[t][(key & 15) >> 1]
            return jnp.where((key & 1) == 0, pair[0:6], pair[6:12])

        r2[t][me, 0:6] = piece(my_key)

        def body(k, carry):
            to = far_first(k)
            p2[t, to, 0:6] = piece(keys[0, to])
            remote(p2.at[t, to, pl.ds(0, 6)], r2[t].at[me, pl.ds(0, 6)], 12 + t, (region, to)).start()
            return carry

        lax.fori_loop(0, INNER - 1, body, 0)

    send_faces(0)
    send_faces(1)

    q4, z = lane // 32, lane % 32
    edge_y = jnp.where((lane < 32) & (sub == 0) | (lane >= 96) & (sub == 7), 1.0, 0.0)
    sign_y = jnp.where(lane < 64, edge_y, -edge_y)
    edge_z = jnp.where((z == 0) | (z == 31), 1.0, 0.0)
    sign_z = jnp.where(z < 16, edge_z, -edge_z)
    pick_x = (q4 // 2) * 16 + z // 2
    pick_z = (q4 // 2) * 2 + z // 16

    def add_ghosts(t, dst):
        wait_all(r2[t].at[pl.ds(0, INNER - 1), pl.ds(0, 6)], rsem.at[12 + t])
        start = (my_key >> 4) * 8
        for k in range(8):
            gt[pl.ds(k * 8, 8)] = r2[t][start + k]
        tiles = [gt[pl.ds(face, 8, stride=8)] for face in range(6)]
        for face, x in ((0, 1), (1, 32)):
            e = [take(tiles[face], pick_x + 32 * v) for v in range(4)]
            dst[0, x] = dst[0, x] + e[0]
            dst[1, x] = dst[1, x] + e[0] if face == 0 else dst[1, x] - e[0]
            dst[2, x] = dst[2, x] + e[1]
            dst[3, x] = dst[3, x] + e[2]
            dst[4, x] = dst[4, x] + e[3]
        for v in range(4):
            for odd in range(2):
                pick = v * 32 + odd * 16 + z // 2
                ey[v, pl.ds(odd, 8, stride=2)] = jnp.where(lane < 64, take(tiles[2], pick), take(tiles[3], pick))

        def body(x, carry):
            y = [jnp.broadcast_to(ey[v, pl.ds(x, 1)], (8, 128)) for v in range(4)]
            zz = [take(tiles[4 + v // 2], pick_z + ((v % 2) * 64 + x * 4)) for v in range(4)]
            add = [
                edge_y * y[0] + edge_z * zz[0],
                edge_y * y[1] + edge_z * zz[1],
                sign_y * y[0] + edge_z * zz[2],
                edge_y * y[2] + sign_z * zz[0],
                edge_y * y[3] + edge_z * zz[3],
            ]
            for i in range(5):
                dst[i, 2 * x + 1] = dst[i, 2 * x + 1] + add[i]
                dst[i, 2 * x + 2] = dst[i, 2 * x + 2] + add[i]
            return carry

        lax.fori_loop(0, 16, body, 0, unroll=8)

    live = [jnp.where(turn < count, 1.0, 0.0) for turn in range(BURN_MAX)]
    group = 16

    def burn(dst):
        def body(g, carry):
            at = g * group
            p = [dst[0, at + i + 1] for i in range(group)]
            f = [dst[4, at + i + 1] for i in range(group)]
            for turn in range(BURN_MAX):
                for i in range(group):
                    r = pl.reciprocal(fa[at + i] + fb[at + i] * jnp.tanh(p[i]), approx=True)
                    d = live[turn] * (f[i] - f[i] * r)
                    f[i] = f[i] - d
                    p[i] = p[i] + 0.5 * d
            for i in range(group):
                dst[0, at + i + 1] = p[i]
                dst[4, at + i + 1] = f[i]
            return carry

        lax.fori_loop(0, 32 // group, body, 0)

    add_ghosts(0, f1)
    burn(f1)
    fine_hydro(f1, f0)
    add_ghosts(1, f0)
    burn(f0)

    for j in range(8):
        stores.append(
            pltpu.make_async_copy(
                f0.at[:, pl.ds(1, 32), j], fine_out.at[:, :, pl.ds(j * 128, 128)], lsem.at[2 + j]
            )
        )
        stores[-1].start()
    pick_m = ((lane % 32) // 16) * 64 + 2 * (lane % 16)

    def means(a, carry):
        for i in range(5):
            tile = zero
            for g in range(4):
                at = a * 8 + 2 * g
                q = f0[i, at + 1] + f0[i, at + 2]
                q = q + lanes(q, -1)
                q = q + lanes(q, -32)
                tile = jnp.where(q4 == g, take(q, pick_m), tile)
            mb[pl.ds(a * 64 + i, 8, stride=8)] = 0.125 * tile
        return carry

    lax.fori_loop(0, 4, means, 0, unroll=2)

    r3[me, 0:5] = mb[pl.ds(me * 8, 5)]

    def send_mean(k, carry):
        to = far_first(k)
        remote(mb.at[pl.ds(to * 8, 5)], r3.at[me, pl.ds(0, 5)], 14, (region, to)).start()
        return carry

    lax.fori_loop(0, INNER - 1, send_mean, 0)
    wait_all(r3.at[pl.ds(0, 31), pl.ds(0, 5)], rsem.at[14])

    def pick_pair(to):
        for s in range(2):
            p4[to, 5 * s : 5 * s + 5] = r3[keys[1, 2 * to + s], 0:5]

    pick_pair(me)
    stores.append(pltpu.make_async_copy(p4.at[me], r4.at[me], lsem.at[1]))
    stores[-1].start()

    def send_pair(k, carry):
        to = far_first(k)
        pick_pair(to)
        remote(p4.at[to], r4.at[me], 15, (region, to)).start()
        return carry

    lax.fori_loop(0, INNER - 1, send_pair, 0)

    for halo in halos:
        halo.wait_send()
    for t in range(2):
        wait_all(r1[t].at[pl.ds(0, 7), pl.ds(0, 12)], ssem.at[10 + t])
        wait_all(r2[t].at[pl.ds(0, INNER - 1), pl.ds(0, 6)], ssem.at[12 + t])
    wait_all(r3.at[pl.ds(0, 31), pl.ds(0, 5)], ssem.at[14])
    wait_all(p4.at[pl.ds(0, 31)], ssem.at[15])
    for store in stores:
        store.wait()
    keep.wait()
    wait_all(r4.at[pl.ds(0, 31)], rsem.at[15])


def place(stepped, means, fine, table, coarse_out, fine_out, h, m, f, keys, sem):
    me = lax.axis_index("inner")
    loads = [
        pltpu.make_async_copy(means, m.at[:, pl.ds(0, 10)], sem.at[0]),
        pltpu.make_async_copy(table, keys, sem.at[1]),
        pltpu.make_async_copy(stepped, h, sem.at[2]),
    ]
    move = pltpu.make_async_copy(fine, f, sem.at[3])
    for load in loads:
        load.start()
    move.start()
    for load in loads:
        load.wait()
    lane = iota((8, 128), 1)
    here = [lane // 16 == keys[2, 2 * me + s] for s in range(2)]
    rows_of = m.reshape(512, 128)
    move.wait()
    stores = [pltpu.make_async_copy(f, fine_out, sem.at[3])]
    stores[0].start()
    for i in range(5):

        def body(a, carry):
            tiles = [rows_of[pl.ds(a * 128 + s * 5 + i, 8, stride=16)] for s in range(2)]
            for g in range(4):
                for odd in range(2):
                    at = pl.ds((a * 4 + g) * 16 + odd, 8, stride=2)
                    q = h[i, at]
                    for s in range(2):
                        q = jnp.where(here[s], take(tiles[s], lane % 16 + (g * 32 + odd * 16)), q)
                    h[i, at] = q
            return carry

        lax.fori_loop(0, 4, body, 0, unroll=4)
        stores.append(pltpu.make_async_copy(h.at[i], coarse_out.at[i], sem.at[4 + i]))
        stores[-1].start()
    for store in stores:
        store.wait()


def per_device(coarse_state, fine_state, coarse_rate, fine_rate, parents, burn_steps):
    anywhere = pl.BlockSpec(memory_space=pl.ANY)
    stepped, fine_mid, means, table = pl.pallas_call(
        kernel,
        out_shape=(
            jax.ShapeDtypeStruct((5, 256, 128), F32),
            jax.ShapeDtypeStruct((5, 32, 1024), F32),
            jax.ShapeDtypeStruct((32, 10, 128), F32),
            jax.ShapeDtypeStruct((8, 128), jnp.int32),
        ),
        in_specs=[anywhere] * 6,
        out_specs=(anywhere,) * 4,
        scratch_shapes=[
            pltpu.VMEM((5, 288, 128), F32),
            pltpu.VMEM((5, 256, 128), F32),
            pltpu.VMEM((256, 128), F32),
            pltpu.VMEM((2, 5, 32, 128), F32),
            pltpu.VMEM((2, 16, 128), F32),
            pltpu.VMEM((2, 11, 16, 128), F32),
            pltpu.VMEM((2, 11, 16, 128), F32),
            pltpu.VMEM((4, 8, 128), F32),
            pltpu.VMEM((4, 8, 128), F32),
            pltpu.VMEM((4, 4, 16, 128), F32),
            pltpu.VMEM((4, 256, 128), F32),
            pltpu.VMEM((8, 128), jnp.int32),
            pltpu.SMEM((8, 128), jnp.int32),
            pltpu.VMEM((2, 128, 128), F32),
            pltpu.VMEM((8, 16, 128), F32),
            pltpu.VMEM((8, 16, 128), F32),
            pltpu.VMEM((2, 32, 8, 128), F32),
            pltpu.VMEM((32, 8, 128), F32),
            pltpu.VMEM((32, 8, 128), F32),
            pltpu.VMEM((5, 34, 8, 128), F32),
            pltpu.VMEM((5, 34, 8, 128), F32),
            pltpu.VMEM((32, 8, 128), F32),
            pltpu.VMEM((32, 8, 128), F32),
            pltpu.VMEM((32, 8, 128), F32),
            pltpu.VMEM((64, 128), F32),
            pltpu.VMEM((4, 16, 128), F32),
            pltpu.VMEM((256, 128), F32),
            pltpu.VMEM((32, 8, 128), F32),
            pltpu.VMEM((32, 10, 128), F32),
            pltpu.VMEM((1, 32), jnp.int32),
            pltpu.SMEM((1,), jnp.int32),
            pltpu.SemaphoreType.DMA((16,)),
            pltpu.SemaphoreType.DMA((16,)),
            pltpu.SemaphoreType.DMA((20,)),
            pltpu.SemaphoreType.DMA,
        ],
        compiler_params=pltpu.CompilerParams(
            collective_id=0, has_side_effects=True, vmem_limit_bytes=60 * 2**20
        ),
        name="reactive_step",
    )(
        coarse_state.reshape(5, 256, 128),
        fine_state.reshape(5, 32, 1024),
        coarse_rate.reshape(256, 128),
        fine_rate.reshape(32, 1024),
        parents,
        burn_steps,
    )
    coarse_new, fine_new = pl.pallas_call(
        place,
        out_shape=(
            jax.ShapeDtypeStruct((5, 256, 128), F32),
            jax.ShapeDtypeStruct((5, 32, 1024), F32),
        ),
        in_specs=[anywhere] * 4,
        out_specs=(anywhere,) * 2,
        scratch_shapes=[
            pltpu.VMEM((5, 256, 128), F32),
            pltpu.VMEM((32, 16, 128), F32),
            pltpu.VMEM((5, 32, 1024), F32),
            pltpu.SMEM((8, 128), jnp.int32),
            pltpu.SemaphoreType.DMA((9,)),
        ],
        compiler_params=pltpu.CompilerParams(vmem_limit_bytes=60 * 2**20),
        name="place",
    )(stepped, means, fine_mid, table)
    return coarse_new.reshape(5, 16, 16, 128), fine_new.reshape(1, 5, 32, 1024)


def solution(mesh):
    in_specs = (
        P(None, "region", "inner", None),
        P(("region", "inner"), None, None, None),
        P("region", "inner", None),
        P(("region", "inner"), None, None),
        P("region", None),
        P(("region", "inner")),
    )
    out_specs = (P(None, "region", "inner", None), P(("region", "inner"), None, None, None))
    return jax.shard_map(per_device, mesh=mesh, in_specs=in_specs, out_specs=out_specs, check_vma=False)
```

```python
import functools

import jax
import jax.numpy as jnp
from jax import lax
from jax.experimental import pallas as pl
from jax.experimental.pallas import tpu as pltpu
from jax.sharding import PartitionSpec as P

MESH = pl.DeviceIdType.MESH
F32 = jnp.float32
ADV = (0.5, -0.3, 0.2)
KEEP = 0.1
NB = 0.15
BURN_MAX = 8
REGIONS = 4
INNER = 32


def iota(shape, axis):
    return lax.broadcasted_iota(jnp.int32, shape, axis)


def lanes(q, shift):
    return pltpu.roll(q, shift % 128, 1)


def rows(q, shift):
    return pltpu.roll(q, shift % q.shape[0], 0)


def hydro(c, xm, xp, yd, yu, zd, zu):
    p, u, v, w, f = c
    sx, mx = xm[0] + xm[1], xp[0] - xp[1]
    sy, my = yd(p + v), yu(p - v)
    sz, mz = zd(p + w), zu(p - w)
    hp = (sx + mx) + (sy + my) + (sz + mz)
    hu = (sx - mx) + (yd(u) + yu(u)) + (zd(u) + zu(u))
    hv = (xm[2] + xp[2]) + (sy - my) + (zd(v) + zu(v))
    hw = (xm[3] + xp[3]) + (yd(w) + yu(w)) + (sz - mz)
    hf = (
        ((1 + ADV[0]) * xm[4] + (1 - ADV[0]) * xp[4])
        + ((1 + ADV[1]) * yd(f) + (1 - ADV[1]) * yu(f))
        + ((1 + ADV[2]) * zd(f) + (1 - ADV[2]) * zu(f))
    )
    return [KEEP * a + NB * b for a, b in zip(c, (hp, hu, hv, hw, hf))]


def take(q, index):
    return jnp.take_along_axis(q, index, axis=1, mode="promise_in_bounds")


def coarse_shifts(shape):
    row, lane = iota(shape, 0), iota(shape, 1)
    zd = lambda q: jnp.where(lane == 0, 0.0, lanes(q, 1))
    zu = lambda q: jnp.where(lane == 127, 0.0, lanes(q, -1))
    yd = lambda q: jnp.where(row == 0, 0.0, rows(q, 1))
    yu = lambda q: jnp.where(row == shape[0] - 1, 0.0, rows(q, -1))
    return yd, yu, zd, zu


def fine_shifts():
    sub, lane = iota((8, 128), 0), iota((8, 128), 1)
    z = lane % 32

    def yd(q):
        t = lanes(q, 32)
        t = jnp.where(lane < 32, rows(t, 1), t)
        return jnp.where((lane < 32) & (sub == 0), 0.0, t)

    def yu(q):
        t = lanes(q, -32)
        t = jnp.where(lane >= 96, rows(t, -1), t)
        return jnp.where((lane >= 96) & (sub == 7), 0.0, t)

    zd = lambda q: jnp.where(z == 0, 0.0, lanes(q, 1))
    zu = lambda q: jnp.where(z == 31, 0.0, lanes(q, -1))
    return yd, yu, zd, zu


def burn_once(p, f, rate):
    burned = f * pl.reciprocal(1.0 + 0.5 * rate * (1.0 + 0.5 * jnp.tanh(p)), approx=True)
    return p + 0.5 * (f - burned), burned


def face_values(p, n, t1, t2, f, axis, high):
    sign = -1.0 if high else 1.0
    return [NB * (p + sign * n), NB * t1, NB * t2, NB * (1 + sign * ADV[axis]) * f]


def ghost_step(near, far, own, dlo, dhi, rate, axis, high):
    n, r = (1, 2) if axis == 0 else (2, 1)
    row, lane = iota((16, 128), 0), iota((16, 128), 1)
    an, ar, az = ADV[axis], ADV[1 - axis], ADV[2]
    minus, plus = (own, far) if high else (far, own)
    p, w, f = near[0], near[3], near[4]

    def rd(q, d):
        return jnp.where(row == 0, d, rows(q, 1))

    def ru(q, d):
        return jnp.where(row == 15, d, rows(q, -1))

    zd = lambda q: jnp.where(lane == 0, 0.0, lanes(q, 1))
    zu = lambda q: jnp.where(lane == 127, 0.0, lanes(q, -1))
    sn, mn = minus[0] + minus[n], plus[0] - plus[n]
    sr, mr = rd(p + near[r], dlo[0] + dlo[r]), ru(p - near[r], dhi[0] - dhi[r])
    sz, mz = zd(p + w), zu(p - w)
    hp = (sn + mn) + (sr + mr) + (sz + mz)
    hn = (sn - mn) + (rd(near[n], dlo[n]) + ru(near[n], dhi[n])) + (zd(near[n]) + zu(near[n]))
    hr = (minus[r] + plus[r]) + (sr - mr) + (zd(near[r]) + zu(near[r]))
    hw = (minus[3] + plus[3]) + (rd(w, dlo[3]) + ru(w, dhi[3])) + (sz - mz)
    hf = (
        ((1 + an) * minus[4] + (1 - an) * plus[4])
        + ((1 + ar) * rd(f, dlo[4]) + (1 - ar) * ru(f, dhi[4]))
        + ((1 + az) * zd(f) + (1 - az) * zu(f))
    )
    pressure, normal, tangent, across, fuel = (
        KEEP * a + NB * b for a, b in zip((p, near[n], near[r], w, f), (hp, hn, hr, hw, hf))
    )
    pressure, fuel = burn_once(pressure, fuel, rate)
    return face_values(pressure, normal, tangent, across, fuel, axis, high)


def kernel(
    coarse, fine, crate, frate, parents, steps, h_out, fine_out, r4, table_out,
    c, h, cr, xh, xr, ys, yh, ds, dr, fv, zv, table, keys, p1, r1a, r1b, p2, r2a, r2b, f0, f1, fa, fb, fr, gt, ey,
    mb, r3, p4, pv, sv, ssem, rsem, lsem, tsem, ready,
):
    r1, r2 = (r1a, r1b), (r2a, r2b)
    region, me = lax.axis_index("region"), lax.axis_index("inner")
    up, down = lax.rem(region + 1, REGIONS), lax.rem(region + REGIONS - 1, REGIONS)
    right, left = lax.rem(me + 1, INNER), lax.rem(me + INNER - 1, INNER)
    plane, mine = (me // 8) * 8, lax.rem(me, 8)
    sub, lane = iota((8, 128), 0), iota((8, 128), 1)

    def far_first(k):
        return lax.rem(me + 1 + lax.rem(15 + k, INNER - 1), INNER)

    barrier = pltpu.get_barrier_semaphore()
    others = [(up, right), (up, left), (down, right), (down, left), (up, me), (down, me)]
    columns = [(region, lax.rem(me + 8 * k, INNER)) for k in (2, 1, 3)]
    outside = [jnp.where(mine == 7, 1, 0), jnp.where(mine == 0, 1, 0)]
    for other in others + columns:
        pl.semaphore_signal(barrier, inc=1, device_id=other, device_id_type=MESH)
    for k in range(1, 8):
        pl.semaphore_signal(
            barrier, inc=1, device_id=(region, plane + lax.rem(mine + k, 8)), device_id_type=MESH
        )
    for e, other in enumerate((right, left)):

        @pl.when(outside[e] == 1)
        def _():
            pl.semaphore_signal(barrier, inc=1, device_id=(region, other), device_id_type=MESH)

    loads = [
        pltpu.make_async_copy(coarse, c.at[:, pl.ds(16, 256)], lsem.at[0]),
        pltpu.make_async_copy(crate, cr, lsem.at[1]),
        pltpu.make_async_copy(parents, pv, lsem.at[18]),
        pltpu.make_async_copy(steps, sv, lsem.at[19]),
    ]
    for j in range(8):
        cut = pl.ds(j * 128, 128)
        loads.append(pltpu.make_async_copy(fine.at[:, :, cut], f0.at[:, pl.ds(1, 32), j], lsem.at[2 + j]))
        loads.append(pltpu.make_async_copy(frate.at[:, cut], fr.at[:, j], lsem.at[10 + j]))
    for load in loads:
        load.start()

    zero = jnp.zeros((8, 128), F32)
    for i in range(5):
        c[i, 0:16] = jnp.zeros((16, 128), F32)
        c[i, 272:288] = jnp.zeros((16, 128), F32)
        for a in (0, 33):
            f0[i, a] = zero
            f1[i, a] = zero
    loads[0].wait()
    loads[1].wait()
    for side, (near, far) in enumerate(((15, 14), (0, 1))):
        for half in range(2):
            dst = pl.ds(half * 8, 8)
            for i in range(5):
                ys[side, 0, i, dst] = c[i, pl.ds(16 + half * 128 + near, 8, stride=16)]
                ys[side, 1, i, dst] = c[i, pl.ds(16 + half * 128 + far, 8, stride=16)]
            ys[side, 1, 5, dst] = cr[pl.ds(half * 128 + near, 8, stride=16)]
    for n, at in enumerate((255, 240, 15, 0)):
        for i in range(5):
            ds[n, i : i + 1] = c[i, 16 + at : 17 + at]
        ds[n, 5:8] = jnp.zeros((3, 128), F32)

    pl.semaphore_wait(barrier, len(others) + len(columns) + 7 + outside[0] + outside[1])

    def remote(src, dst, n, to):
        return pltpu.make_async_remote_copy(
            src_ref=src, dst_ref=dst, send_sem=ssem.at[n], recv_sem=rsem.at[n], device_id=to, device_id_type=MESH
        )

    near = [
        remote(c.at[:, pl.ds(16 + 240, 16)], xh.at[0, 0], 0, (up, me)),
        remote(c.at[:, pl.ds(16, 16)], xh.at[1, 0], 1, (down, me)),
        remote(ys.at[0, 0, pl.ds(0, 5)], yh.at[0, 0, pl.ds(0, 5)], 2, (region, right)),
        remote(ys.at[1, 0, pl.ds(0, 5)], yh.at[1, 0, pl.ds(0, 5)], 3, (region, left)),
    ]
    far = [
        remote(ds.at[0], dr.at[0], 4, (up, right)),
        remote(ds.at[1], dr.at[1], 5, (up, left)),
        remote(ds.at[2], dr.at[2], 6, (down, right)),
        remote(ds.at[3], dr.at[3], 7, (down, left)),
        remote(cr.at[pl.ds(240, 16)], xr.at[0], 8, (up, me)),
        remote(cr.at[pl.ds(0, 16)], xr.at[1], 9, (down, me)),
        remote(c.at[:, pl.ds(16 + 224, 16)], xh.at[0, 1], 16, (up, me)),
        remote(c.at[:, pl.ds(32, 16)], xh.at[1, 1], 17, (down, me)),
        remote(ys.at[0, 1], yh.at[0, 1], 18, (region, right)),
        remote(ys.at[1, 1], yh.at[1, 1], 19, (region, left)),
    ]
    for halo in near + far:
        halo.start()
    for other in columns:
        pl.semaphore_signal(ready, inc=1, device_id=other, device_id_type=MESH)

    loads[2].wait()
    block_row = jnp.broadcast_to(pv[...], (32, 32))
    ri, ci = iota((32, 32), 0), iota((32, 32), 1)
    block = jnp.sum(jnp.where(ri == ci, block_row, 0), axis=1, keepdims=True)
    owner = block >> 3
    slot = jnp.sum(
        jnp.where((jnp.broadcast_to(owner, (32, 32)) == (block_row >> 3)) & (ci < ri), 1, 0),
        axis=1,
        keepdims=True,
    )
    key = jnp.broadcast_to(owner * 2 + slot, (32, 128))
    ri, ci = iota((32, 128), 0), iota((32, 128), 1)
    layer = jnp.broadcast_to((block & 7) + 1, (32, 128))
    key_row = jnp.sum(jnp.where(ri == ci, key, 0), axis=0, keepdims=True)
    patch_row = jnp.sum(jnp.where(key == ci, ri, 0), axis=0, keepdims=True)
    layer_row = jnp.sum(jnp.where(key == ci, layer, 0), axis=0, keepdims=True) - 1
    table[...] = jnp.where(
        sub == 0,
        jnp.broadcast_to(key_row, (8, 128)),
        jnp.where(sub == 1, jnp.broadcast_to(patch_row, (8, 128)), jnp.broadcast_to(layer_row, (8, 128))),
    )
    keep = pltpu.make_async_copy(table, table_out, lsem.at[18])
    keep.start()
    look = pltpu.make_async_copy(table, keys, tsem)
    look.start()

    shifts = coarse_shifts((16, 128))

    def coarse_plane(x, carry):
        at = pl.multiple_of(x * 16, 16)
        cells = [c[i, pl.ds(at + 16, 16)] for i in range(5)]
        below = [c[i, pl.ds(at, 16)] for i in range(5)]
        above = [c[i, pl.ds(at + 32, 16)] for i in range(5)]
        for i, q in enumerate(hydro(cells, below, above, *shifts)):
            h[i, pl.ds(at, 16)] = q
        return carry

    lax.fori_loop(0, 16, coarse_plane, 0, unroll=4)

    look.wait()
    slots = [keys[2, 2 * me], keys[2, 2 * me + 1]]
    my_key = keys[0, me]

    side = lane % 2
    code = ((lane % 64) // 4) * 4 + (lane // 64) * 2 + (lane % 4) // 2
    picks = [lax.rem(jnp.where(side == 0, 16 * s + 127, 16 * s + 16) + 128, 128) for s in slots]
    cuts = [16 * jnp.maximum(s, 0) + lane % 16 for s in slots]
    inside = [
        jnp.where(((side == 0) & (s == 0)) | ((side == 1) & (s == 7)), 0.0, 1.0) for s in slots
    ]

    def z_values(src, base):
        low = iota((16, 128), 1) % 16 == 15

        def body(x, carry):
            at = pl.multiple_of(x * 16, 16)
            p, u, v, w, f = (src[i, pl.ds(at + base, 16)] for i in range(5))
            zv[0, pl.ds(at, 16)] = NB * (p + jnp.where(low, w, -w))
            zv[1, pl.ds(at, 16)] = NB * u
            zv[2, pl.ds(at, 16)] = NB * v
            zv[3, pl.ds(at, 16)] = f * jnp.where(low, NB * (1 + ADV[2]), NB * (1 - ADV[2]))
            return carry

        lax.fori_loop(0, 16, body, 0, unroll=4)

    def z_tiles():
        def body(x, tiles):
            tiles = list(tiles)
            for v in range(4):
                for odd in range(2):
                    q = zv[v, pl.ds(x * 16 + odd, 8, stride=2)]
                    here = code == x * 4 + (v % 2) * 2 + odd
                    for s in range(2):
                        tiles[s * 2 + v // 2] = jnp.where(here, take(q, picks[s]), tiles[s * 2 + v // 2])
            return tuple(tiles)

        tiles = lax.fori_loop(0, 16, body, (zero,) * 4, unroll=8)
        return [[tiles[s * 2 + w] * inside[s] for w in range(2)] for s in range(2)]

    def xy_tile(face, s):
        tile = zero
        for v in range(4):
            for odd in range(2):
                pos = v * 32 + odd * 16
                q = fv[face, v, pl.ds(odd, 8, stride=2)]
                tile = jnp.where(lane // 16 == pos // 16, take(q, cuts[s]), tile)
        return tile

    def put_tile(t, s, face, tile):
        p1[t, pl.ds(s * 6 + face, 8, stride=16)] = tile

    def get_tile(t, s, face):
        return p1[t, pl.ds(s * 6 + face, 8, stride=16)]

    z_values(c, 16)
    for s, pair in enumerate(z_tiles()):
        for w, tile in enumerate(pair):
            put_tile(0, s, 4 + w, tile)

    for halo in near:
        halo.wait_recv()
    mx = [jnp.where(region > 0, 1.0, 0.0), jnp.where(region < REGIONS - 1, 1.0, 0.0)]
    my = [jnp.where(me > 0, 1.0, 0.0), jnp.where(me < INNER - 1, 1.0, 0.0)]

    def near_x(e):
        return [xh[e, 0, i] for i in range(5)]

    def near_y(e):
        return [yh[e, 0, i] for i in range(5)]

    for e in range(2):
        p, u, v, w, f = near_x(e)
        for i, q in enumerate(face_values(p, u, v, w, f, 0, e == 1)):
            fv[e, i] = mx[e] * q
        p, u, v, w, f = near_y(e)
        for i, q in enumerate(face_values(p, v, u, w, f, 1, e == 1)):
            fv[2 + e, i] = my[e] * q
    for s in range(2):
        for face in range(4):
            put_tile(0, s, face, xy_tile(face, s))

    def send_pieces(t):
        r1[t][mine, 0:12] = p1[t, pl.ds(mine * 16, 12)]

        def body(k, carry):
            to = lax.rem(mine + 1 + k, 8)
            remote(
                p1.at[t, pl.ds(to * 16, 12)], r1[t].at[mine, pl.ds(0, 12)], 10 + t, (region, plane + to)
            ).start()
            return carry

        lax.fori_loop(0, 7, body, 0)

    send_pieces(0)

    def add_face(ref, cut, face, n, t1, high):
        e0, e1, e2, e3 = (fv[face, v, pl.ds(8 * cut[0], 8)] for v in range(4))
        at = cut[1]
        ref[0, at] = ref[0, at] + e0
        ref[n, at] = ref[n, at] - e0 if high else ref[n, at] + e0
        ref[t1, at] = ref[t1, at] + e1
        ref[3, at] = ref[3, at] + e2
        ref[4, at] = ref[4, at] + e3

    for half in range(2):
        add_face(h, (half, pl.ds(half * 8, 8)), 0, 1, 2, False)
        add_face(h, (half, pl.ds(240 + half * 8, 8)), 1, 1, 2, True)
        add_face(h, (half, pl.ds(half * 128, 8, stride=16)), 2, 2, 1, False)
        add_face(h, (half, pl.ds(half * 128 + 15, 8, stride=16)), 3, 2, 1, True)

    def coarse_burn(x, carry):
        at = pl.multiple_of(x * 64, 64)
        p, f = burn_once(h[0, pl.ds(at, 64)], h[4, pl.ds(at, 64)], cr[pl.ds(at, 64)])
        h[0, pl.ds(at, 64)] = p
        h[4, pl.ds(at, 64)] = f
        return carry

    lax.fori_loop(0, 4, coarse_burn, 0, unroll=4)

    for halo in far:
        halo.wait_recv()

    def own_rows(axis, e):
        if axis == 0:
            return [c[i, pl.ds(16 + 240 * e, 16)] for i in range(5)]
        return [
            jnp.concatenate([c[i, pl.ds(16 + 128 * b + 15 * e, 8, stride=16)] for b in range(2)], axis=0)
            for i in range(5)
        ]

    def corner(n, scale):
        return [dr[n, i : i + 1] * scale for i in range(5)]

    for e in range(2):
        values = ghost_step(
            near_x(e), [xh[e, 1, i] for i in range(5)], own_rows(0, e), corner(2 * e, my[0]), corner(2 * e + 1, my[1]), xr[e], 0, e == 1
        )
        for i, q in enumerate(values):
            fv[e, i] = mx[e] * q
        values = ghost_step(
            near_y(e), [yh[e, 1, i] for i in range(5)], own_rows(1, e),
            corner(e, mx[0]), corner(2 + e, mx[1]), yh[e, 1, 5], 1, e == 1,
        )
        for i, q in enumerate(values):
            fv[2 + e, i] = my[e] * q
    z_values(h, 0)
    for s, pair in enumerate(z_tiles()):
        for w, tile in enumerate(pair):
            put_tile(1, s, 4 + w, 0.5 * (get_tile(0, s, 4 + w) + tile))
        for face in range(4):
            put_tile(1, s, face, 0.5 * (get_tile(0, s, face) + xy_tile(face, s)))
    send_pieces(1)
    stores = [pltpu.make_async_copy(h, h_out, lsem.at[0])]
    stores[0].start()

    for load in loads[3:]:
        load.wait()
    count = sv[0]
    counted = jnp.broadcast_to(count, (8, 128)).astype(F32)
    span = 0.25 / counted
    fine_shift = fine_shifts()

    def rates(x, carry):
        q = span * fr[x]
        fa[x] = 1.0 + q
        fb[x] = 0.5 * q
        return carry

    lax.fori_loop(0, 32, rates, 0, unroll=8)

    def fine_hydro(src, dst):
        def body(x, carry):
            cells = [src[i, x + 1] for i in range(5)]
            below = [src[i, x] for i in range(5)]
            above = [src[i, x + 2] for i in range(5)]
            for i, q in enumerate(hydro(cells, below, above, *fine_shift)):
                dst[i, x + 1] = q
            return carry

        lax.fori_loop(0, 32, body, 0, unroll=8)

    fine_hydro(f0, f1)

    def wait_all(ref, sem):
        pltpu.make_async_copy(ref, ref, sem).wait()

    def send_faces(t):
        wait_all(r1[t].at[pl.ds(0, 7), pl.ds(0, 12)], rsem.at[10 + t])

        def piece(key):
            pair = r1[t][(key & 15) >> 1]
            return jnp.where((key & 1) == 0, pair[0:6], pair[6:12])

        r2[t][me, 0:6] = piece(my_key)

        def body(k, carry):
            to = far_first(k)
            p2[t, to, 0:6] = piece(keys[0, to])
            remote(p2.at[t, to, pl.ds(0, 6)], r2[t].at[me, pl.ds(0, 6)], 12 + t, (region, to)).start()
            return carry

        lax.fori_loop(0, INNER - 1, body, 0)

    pl.semaphore_wait(ready, len(columns))
    send_faces(0)
    send_faces(1)

    q4, z = lane // 32, lane % 32
    edge_y = jnp.where((lane < 32) & (sub == 0) | (lane >= 96) & (sub == 7), 1.0, 0.0)
    sign_y = jnp.where(lane < 64, edge_y, -edge_y)
    edge_z = jnp.where((z == 0) | (z == 31), 1.0, 0.0)
    sign_z = jnp.where(z < 16, edge_z, -edge_z)
    pick_x = (q4 // 2) * 16 + z // 2
    pick_z = (q4 // 2) * 2 + z // 16

    def add_ghosts(t, dst):
        wait_all(r2[t].at[pl.ds(0, INNER - 1), pl.ds(0, 6)], rsem.at[12 + t])
        start = (my_key >> 4) * 8
        for k in range(8):
            gt[pl.ds(k * 8, 8)] = r2[t][start + k]
        tiles = [gt[pl.ds(face, 8, stride=8)] for face in range(6)]
        for face, x in ((0, 1), (1, 32)):
            e = [take(tiles[face], pick_x + 32 * v) for v in range(4)]
            dst[0, x] = dst[0, x] + e[0]
            dst[1, x] = dst[1, x] + e[0] if face == 0 else dst[1, x] - e[0]
            dst[2, x] = dst[2, x] + e[1]
            dst[3, x] = dst[3, x] + e[2]
            dst[4, x] = dst[4, x] + e[3]
        for v in range(4):
            for odd in range(2):
                pick = v * 32 + odd * 16 + z // 2
                ey[v, pl.ds(odd, 8, stride=2)] = jnp.where(lane < 64, take(tiles[2], pick), take(tiles[3], pick))

        def body(x, carry):
            y = [jnp.broadcast_to(ey[v, pl.ds(x, 1)], (8, 128)) for v in range(4)]
            zz = [take(tiles[4 + v // 2], pick_z + ((v % 2) * 64 + x * 4)) for v in range(4)]
            add = [
                edge_y * y[0] + edge_z * zz[0],
                edge_y * y[1] + edge_z * zz[1],
                sign_y * y[0] + edge_z * zz[2],
                edge_y * y[2] + sign_z * zz[0],
                edge_y * y[3] + edge_z * zz[3],
            ]
            for i in range(5):
                dst[i, 2 * x + 1] = dst[i, 2 * x + 1] + add[i]
                dst[i, 2 * x + 2] = dst[i, 2 * x + 2] + add[i]
            return carry

        lax.fori_loop(0, 16, body, 0, unroll=8)

    live = [jnp.where(turn < count, 1.0, 0.0) for turn in range(BURN_MAX)]
    group = 16

    def burn(dst):
        def body(g, carry):
            at = g * group
            p = [dst[0, at + i + 1] for i in range(group)]
            f = [dst[4, at + i + 1] for i in range(group)]
            for turn in range(BURN_MAX):
                for i in range(group):
                    r = pl.reciprocal(fa[at + i] + fb[at + i] * jnp.tanh(p[i]), approx=True)
                    d = live[turn] * (f[i] - f[i] * r)
                    f[i] = f[i] - d
                    p[i] = p[i] + 0.5 * d
            for i in range(group):
                dst[0, at + i + 1] = p[i]
                dst[4, at + i + 1] = f[i]
            return carry

        lax.fori_loop(0, 32 // group, body, 0)

    add_ghosts(0, f1)
    burn(f1)
    fine_hydro(f1, f0)
    add_ghosts(1, f0)
    burn(f0)

    for j in range(8):
        stores.append(
            pltpu.make_async_copy(
                f0.at[:, pl.ds(1, 32), j], fine_out.at[:, :, pl.ds(j * 128, 128)], lsem.at[2 + j]
            )
        )
        stores[-1].start()
    pick_m = ((lane % 32) // 16) * 64 + 2 * (lane % 16)

    def means(a, carry):
        for i in range(5):
            tile = zero
            for g in range(4):
                at = a * 8 + 2 * g
                q = f0[i, at + 1] + f0[i, at + 2]
                q = q + lanes(q, -1)
                q = q + lanes(q, -32)
                tile = jnp.where(q4 == g, take(q, pick_m), tile)
            mb[pl.ds(a * 64 + i, 8, stride=8)] = 0.125 * tile
        return carry

    lax.fori_loop(0, 4, means, 0, unroll=2)

    r3[me, 0:5] = mb[pl.ds(me * 8, 5)]

    def send_mean(k, carry):
        to = far_first(k)
        remote(mb.at[pl.ds(to * 8, 5)], r3.at[me, pl.ds(0, 5)], 14, (region, to)).start()
        return carry

    lax.fori_loop(0, INNER - 1, send_mean, 0)
    wait_all(r3.at[pl.ds(0, 31), pl.ds(0, 5)], rsem.at[14])

    def pick_pair(to):
        for s in range(2):
            p4[to, 5 * s : 5 * s + 5] = r3[keys[1, 2 * to + s], 0:5]

    pick_pair(me)
    stores.append(pltpu.make_async_copy(p4.at[me], r4.at[me], lsem.at[1]))
    stores[-1].start()

    def send_pair(k, carry):
        to = far_first(k)
        pick_pair(to)
        remote(p4.at[to], r4.at[me], 15, (region, to)).start()
        return carry

    lax.fori_loop(0, INNER - 1, send_pair, 0)

    for halo in near + far:
        halo.wait_send()
    for t in range(2):
        wait_all(r1[t].at[pl.ds(0, 7), pl.ds(0, 12)], ssem.at[10 + t])
        wait_all(r2[t].at[pl.ds(0, INNER - 1), pl.ds(0, 6)], ssem.at[12 + t])
    wait_all(r3.at[pl.ds(0, 31), pl.ds(0, 5)], ssem.at[14])
    wait_all(p4.at[pl.ds(0, 31)], ssem.at[15])
    for store in stores:
        store.wait()
    keep.wait()
    wait_all(r4.at[pl.ds(0, 31)], rsem.at[15])


def place(stepped, means, fine, table, coarse_out, fine_out, h, m, f, keys, sem):
    me = lax.axis_index("inner")
    loads = [
        pltpu.make_async_copy(means, m.at[:, pl.ds(0, 10)], sem.at[0]),
        pltpu.make_async_copy(table, keys, sem.at[1]),
        pltpu.make_async_copy(stepped, h, sem.at[2]),
    ]
    move = pltpu.make_async_copy(fine, f, sem.at[3])
    for load in loads:
        load.start()
    move.start()
    for load in loads:
        load.wait()
    lane = iota((8, 128), 1)
    here = [lane // 16 == keys[2, 2 * me + s] for s in range(2)]
    rows_of = m.reshape(512, 128)
    stores = []
    for i in range(5):

        def body(a, carry):
            tiles = [rows_of[pl.ds(a * 128 + s * 5 + i, 8, stride=16)] for s in range(2)]
            for g in range(4):
                for odd in range(2):
                    at = pl.ds((a * 4 + g) * 16 + odd, 8, stride=2)
                    q = h[i, at]
                    for s in range(2):
                        q = jnp.where(here[s], take(tiles[s], lane % 16 + (g * 32 + odd * 16)), q)
                    h[i, at] = q
            return carry

        lax.fori_loop(0, 4, body, 0, unroll=4)
        stores.append(pltpu.make_async_copy(h.at[i], coarse_out.at[i], sem.at[4 + i]))
        stores[-1].start()
        if i == 0:
            move.wait()
            stores.append(pltpu.make_async_copy(f, fine_out, sem.at[3]))
            stores[-1].start()
    for store in stores:
        store.wait()


def per_device(coarse_state, fine_state, coarse_rate, fine_rate, parents, burn_steps):
    anywhere = pl.BlockSpec(memory_space=pl.ANY)
    stepped, fine_mid, means, table = pl.pallas_call(
        kernel,
        out_shape=(
            jax.ShapeDtypeStruct((5, 256, 128), F32),
            jax.ShapeDtypeStruct((5, 32, 1024), F32),
            jax.ShapeDtypeStruct((32, 10, 128), F32),
            jax.ShapeDtypeStruct((8, 128), jnp.int32),
        ),
        in_specs=[anywhere] * 6,
        out_specs=(anywhere,) * 4,
        scratch_shapes=[
            pltpu.VMEM((5, 288, 128), F32),
            pltpu.VMEM((5, 256, 128), F32),
            pltpu.VMEM((256, 128), F32),
            pltpu.VMEM((2, 2, 5, 16, 128), F32),
            pltpu.VMEM((2, 16, 128), F32),
            pltpu.VMEM((2, 2, 6, 16, 128), F32),
            pltpu.VMEM((2, 2, 6, 16, 128), F32),
            pltpu.VMEM((4, 8, 128), F32),
            pltpu.VMEM((4, 8, 128), F32),
            pltpu.VMEM((4, 4, 16, 128), F32),
            pltpu.VMEM((4, 256, 128), F32),
            pltpu.VMEM((8, 128), jnp.int32),
            pltpu.SMEM((8, 128), jnp.int32),
            pltpu.VMEM((2, 128, 128), F32),
            pltpu.VMEM((8, 16, 128), F32),
            pltpu.VMEM((8, 16, 128), F32),
            pltpu.VMEM((2, 32, 8, 128), F32),
            pltpu.VMEM((32, 8, 128), F32),
            pltpu.VMEM((32, 8, 128), F32),
            pltpu.VMEM((5, 34, 8, 128), F32),
            pltpu.VMEM((5, 34, 8, 128), F32),
            pltpu.VMEM((32, 8, 128), F32),
            pltpu.VMEM((32, 8, 128), F32),
            pltpu.VMEM((32, 8, 128), F32),
            pltpu.VMEM((64, 128), F32),
            pltpu.VMEM((4, 16, 128), F32),
            pltpu.VMEM((256, 128), F32),
            pltpu.VMEM((32, 8, 128), F32),
            pltpu.VMEM((32, 10, 128), F32),
            pltpu.VMEM((1, 32), jnp.int32),
            pltpu.SMEM((1,), jnp.int32),
            pltpu.SemaphoreType.DMA((20,)),
            pltpu.SemaphoreType.DMA((20,)),
            pltpu.SemaphoreType.DMA((20,)),
            pltpu.SemaphoreType.DMA,
            pltpu.SemaphoreType.REGULAR,
        ],
        compiler_params=pltpu.CompilerParams(
            collective_id=0, has_side_effects=True, vmem_limit_bytes=60 * 2**20
        ),
        name="reactive_step",
    )(
        coarse_state.reshape(5, 256, 128),
        fine_state.reshape(5, 32, 1024),
        coarse_rate.reshape(256, 128),
        fine_rate.reshape(32, 1024),
        parents,
        burn_steps,
    )
    coarse_new, fine_new = pl.pallas_call(
        place,
        out_shape=(
            jax.ShapeDtypeStruct((5, 256, 128), F32),
            jax.ShapeDtypeStruct((5, 32, 1024), F32),
        ),
        in_specs=[anywhere] * 4,
        out_specs=(anywhere,) * 2,
        scratch_shapes=[
            pltpu.VMEM((5, 256, 128), F32),
            pltpu.VMEM((32, 16, 128), F32),
            pltpu.VMEM((5, 32, 1024), F32),
            pltpu.SMEM((8, 128), jnp.int32),
            pltpu.SemaphoreType.DMA((9,)),
        ],
        compiler_params=pltpu.CompilerParams(vmem_limit_bytes=60 * 2**20),
        name="place",
    )(stepped, means, fine_mid, table)
    return coarse_new.reshape(5, 16, 16, 128), fine_new.reshape(1, 5, 32, 1024)


def solution(mesh):
    in_specs = (
        P(None, "region", "inner", None),
        P(("region", "inner"), None, None, None),
        P("region", "inner", None),
        P(("region", "inner"), None, None),
        P("region", None),
        P(("region", "inner")),
    )
    out_specs = (P(None, "region", "inner", None), P(("region", "inner"), None, None, None))
    return jax.shard_map(per_device, mesh=mesh, in_specs=in_specs, out_specs=out_specs, check_vma=False)
```

```python
import functools

import jax
import jax.numpy as jnp
from jax import lax
from jax.experimental import pallas as pl
from jax.experimental.pallas import tpu as pltpu
from jax.sharding import PartitionSpec as P

MESH = pl.DeviceIdType.MESH
F32 = jnp.float32
ADV = (0.5, -0.3, 0.2)
KEEP = 0.1
NB = 0.15
BURN_MAX = 8
REGIONS = 4
INNER = 32


def hops(offset):
    z, y = offset // 8, offset // 2 % 4
    return min(z, 4 - z) + min(y, 4 - y)


FAR_FIRST = sorted(range(1, INNER), key=hops, reverse=True)


def iota(shape, axis):
    return lax.broadcasted_iota(jnp.int32, shape, axis)


def lanes(q, shift):
    return pltpu.roll(q, shift % 128, 1)


def rows(q, shift):
    return pltpu.roll(q, shift % q.shape[0], 0)


def hydro(c, xm, xp, yd, yu, zd, zu):
    p, u, v, w, f = c
    sx, mx = xm[0] + xm[1], xp[0] - xp[1]
    sy, my = yd(p + v), yu(p - v)
    sz, mz = zd(p + w), zu(p - w)
    hp = (sx + mx) + (sy + my) + (sz + mz)
    hu = (sx - mx) + (yd(u) + yu(u)) + (zd(u) + zu(u))
    hv = (xm[2] + xp[2]) + (sy - my) + (zd(v) + zu(v))
    hw = (xm[3] + xp[3]) + (yd(w) + yu(w)) + (sz - mz)
    hf = (
        ((1 + ADV[0]) * xm[4] + (1 - ADV[0]) * xp[4])
        + ((1 + ADV[1]) * yd(f) + (1 - ADV[1]) * yu(f))
        + ((1 + ADV[2]) * zd(f) + (1 - ADV[2]) * zu(f))
    )
    return [KEEP * a + NB * b for a, b in zip(c, (hp, hu, hv, hw, hf))]


def take(q, index):
    return jnp.take_along_axis(q, index, axis=1, mode="promise_in_bounds")


def coarse_shifts(shape):
    row, lane = iota(shape, 0), iota(shape, 1)
    zd = lambda q: jnp.where(lane == 0, 0.0, lanes(q, 1))
    zu = lambda q: jnp.where(lane == 127, 0.0, lanes(q, -1))
    yd = lambda q: jnp.where(row == 0, 0.0, rows(q, 1))
    yu = lambda q: jnp.where(row == shape[0] - 1, 0.0, rows(q, -1))
    return yd, yu, zd, zu


def fine_shifts():
    sub, lane = iota((8, 128), 0), iota((8, 128), 1)
    z = lane % 32

    def yd(q):
        t = lanes(q, 32)
        t = jnp.where(lane < 32, rows(t, 1), t)
        return jnp.where((lane < 32) & (sub == 0), 0.0, t)

    def yu(q):
        t = lanes(q, -32)
        t = jnp.where(lane >= 96, rows(t, -1), t)
        return jnp.where((lane >= 96) & (sub == 7), 0.0, t)

    zd = lambda q: jnp.where(z == 0, 0.0, lanes(q, 1))
    zu = lambda q: jnp.where(z == 31, 0.0, lanes(q, -1))
    return yd, yu, zd, zu


def burn_once(p, f, rate):
    burned = f * pl.reciprocal(1.0 + 0.5 * rate * (1.0 + 0.5 * jnp.tanh(p)), approx=True)
    return p + 0.5 * (f - burned), burned


def face_values(p, n, t1, t2, f, axis, high):
    sign = -1.0 if high else 1.0
    return [NB * (p + sign * n), NB * t1, NB * t2, NB * (1 + sign * ADV[axis]) * f]


def ghost_step(near, far, own, dlo, dhi, rate, axis, high):
    n, r = (1, 2) if axis == 0 else (2, 1)
    row, lane = iota((16, 128), 0), iota((16, 128), 1)
    an, ar, az = ADV[axis], ADV[1 - axis], ADV[2]
    minus, plus = (own, far) if high else (far, own)
    p, w, f = near[0], near[3], near[4]

    def rd(q, d):
        return jnp.where(row == 0, d, rows(q, 1))

    def ru(q, d):
        return jnp.where(row == 15, d, rows(q, -1))

    zd = lambda q: jnp.where(lane == 0, 0.0, lanes(q, 1))
    zu = lambda q: jnp.where(lane == 127, 0.0, lanes(q, -1))
    sn, mn = minus[0] + minus[n], plus[0] - plus[n]
    sr, mr = rd(p + near[r], dlo[0] + dlo[r]), ru(p - near[r], dhi[0] - dhi[r])
    sz, mz = zd(p + w), zu(p - w)
    hp = (sn + mn) + (sr + mr) + (sz + mz)
    hn = (sn - mn) + (rd(near[n], dlo[n]) + ru(near[n], dhi[n])) + (zd(near[n]) + zu(near[n]))
    hr = (minus[r] + plus[r]) + (sr - mr) + (zd(near[r]) + zu(near[r]))
    hw = (minus[3] + plus[3]) + (rd(w, dlo[3]) + ru(w, dhi[3])) + (sz - mz)
    hf = (
        ((1 + an) * minus[4] + (1 - an) * plus[4])
        + ((1 + ar) * rd(f, dlo[4]) + (1 - ar) * ru(f, dhi[4]))
        + ((1 + az) * zd(f) + (1 - az) * zu(f))
    )
    pressure, normal, tangent, across, fuel = (
        KEEP * a + NB * b for a, b in zip((p, near[n], near[r], w, f), (hp, hn, hr, hw, hf))
    )
    pressure, fuel = burn_once(pressure, fuel, rate)
    return face_values(pressure, normal, tangent, across, fuel, axis, high)


def kernel(
    coarse, fine, crate, frate, parents, steps, h_out, fine_out, r4, table_out,
    c, h, cr, xh, xr, ys, yh, ds, dr, fv, zv, table, keys, p1, r1a, r1b, p2, r2a, r2b, f0, f1, fa, fb, fr, gt, ey,
    mb, r3, p4, pv, sv, ssem, rsem, lsem, tsem, ready,
):
    r1, r2 = (r1a, r1b), (r2a, r2b)
    region, me = lax.axis_index("region"), lax.axis_index("inner")
    up, down = lax.rem(region + 1, REGIONS), lax.rem(region + REGIONS - 1, REGIONS)
    right, left = lax.rem(me + 1, INNER), lax.rem(me + INNER - 1, INNER)
    plane, mine = (me // 8) * 8, lax.rem(me, 8)
    sub, lane = iota((8, 128), 0), iota((8, 128), 1)

    barrier = pltpu.get_barrier_semaphore()
    others = [(up, right), (up, left), (down, right), (down, left), (up, me), (down, me)]
    columns = [(region, lax.rem(me + 8 * k, INNER)) for k in (2, 1, 3)]
    outside = [jnp.where(mine == 7, 1, 0), jnp.where(mine == 0, 1, 0)]
    for other in others + columns:
        pl.semaphore_signal(barrier, inc=1, device_id=other, device_id_type=MESH)
    for k in range(1, 8):
        pl.semaphore_signal(
            barrier, inc=1, device_id=(region, plane + lax.rem(mine + k, 8)), device_id_type=MESH
        )
    for e, other in enumerate((right, left)):

        @pl.when(outside[e] == 1)
        def _():
            pl.semaphore_signal(barrier, inc=1, device_id=(region, other), device_id_type=MESH)

    loads = [
        pltpu.make_async_copy(coarse, c.at[:, pl.ds(16, 256)], lsem.at[0]),
        pltpu.make_async_copy(crate, cr, lsem.at[1]),
        pltpu.make_async_copy(parents, pv, lsem.at[18]),
        pltpu.make_async_copy(steps, sv, lsem.at[19]),
    ]
    for j in range(8):
        cut = pl.ds(j * 128, 128)
        loads.append(pltpu.make_async_copy(fine.at[:, :, cut], f0.at[:, pl.ds(1, 32), j], lsem.at[2 + j]))
        loads.append(pltpu.make_async_copy(frate.at[:, cut], fr.at[:, j], lsem.at[10 + j]))
    for load in loads:
        load.start()

    zero = jnp.zeros((8, 128), F32)
    for i in range(5):
        c[i, 0:16] = jnp.zeros((16, 128), F32)
        c[i, 272:288] = jnp.zeros((16, 128), F32)
        for a in (0, 33):
            f0[i, a] = zero
            f1[i, a] = zero
    loads[0].wait()
    loads[1].wait()
    for side, (near, far) in enumerate(((15, 14), (0, 1))):
        for half in range(2):
            dst = pl.ds(half * 8, 8)
            for i in range(5):
                ys[side, 0, i, dst] = c[i, pl.ds(16 + half * 128 + near, 8, stride=16)]
                ys[side, 1, i, dst] = c[i, pl.ds(16 + half * 128 + far, 8, stride=16)]
            ys[side, 1, 5, dst] = cr[pl.ds(half * 128 + near, 8, stride=16)]
    for n, at in enumerate((255, 240, 15, 0)):
        for i in range(5):
            ds[n, i : i + 1] = c[i, 16 + at : 17 + at]
        ds[n, 5:8] = jnp.zeros((3, 128), F32)

    pl.semaphore_wait(barrier, len(others) + len(columns) + 7 + outside[0] + outside[1])

    def remote(src, dst, n, to):
        return pltpu.make_async_remote_copy(
            src_ref=src, dst_ref=dst, send_sem=ssem.at[n], recv_sem=rsem.at[n], device_id=to, device_id_type=MESH
        )

    near = [
        remote(c.at[:, pl.ds(16 + 240, 16)], xh.at[0, 0], 0, (up, me)),
        remote(c.at[:, pl.ds(16, 16)], xh.at[1, 0], 1, (down, me)),
        remote(ys.at[0, 0, pl.ds(0, 5)], yh.at[0, 0, pl.ds(0, 5)], 2, (region, right)),
        remote(ys.at[1, 0, pl.ds(0, 5)], yh.at[1, 0, pl.ds(0, 5)], 3, (region, left)),
    ]
    far = [
        remote(ds.at[0], dr.at[0], 4, (up, right)),
        remote(ds.at[1], dr.at[1], 5, (up, left)),
        remote(ds.at[2], dr.at[2], 6, (down, right)),
        remote(ds.at[3], dr.at[3], 7, (down, left)),
        remote(cr.at[pl.ds(240, 16)], xr.at[0], 8, (up, me)),
        remote(cr.at[pl.ds(0, 16)], xr.at[1], 9, (down, me)),
        remote(c.at[:, pl.ds(16 + 224, 16)], xh.at[0, 1], 16, (up, me)),
        remote(c.at[:, pl.ds(32, 16)], xh.at[1, 1], 17, (down, me)),
        remote(ys.at[0, 1], yh.at[0, 1], 18, (region, right)),
        remote(ys.at[1, 1], yh.at[1, 1], 19, (region, left)),
    ]
    for halo in near + far:
        halo.start()
    for other in columns:
        pl.semaphore_signal(ready, inc=1, device_id=other, device_id_type=MESH)

    loads[2].wait()
    block_row = jnp.broadcast_to(pv[...], (32, 32))
    ri, ci = iota((32, 32), 0), iota((32, 32), 1)
    block = jnp.sum(jnp.where(ri == ci, block_row, 0), axis=1, keepdims=True)
    owner = block >> 3
    slot = jnp.sum(
        jnp.where((jnp.broadcast_to(owner, (32, 32)) == (block_row >> 3)) & (ci < ri), 1, 0),
        axis=1,
        keepdims=True,
    )
    key = jnp.broadcast_to(owner * 2 + slot, (32, 128))
    ri, ci = iota((32, 128), 0), iota((32, 128), 1)
    layer = jnp.broadcast_to((block & 7) + 1, (32, 128))
    key_row = jnp.sum(jnp.where(ri == ci, key, 0), axis=0, keepdims=True)
    patch_row = jnp.sum(jnp.where(key == ci, ri, 0), axis=0, keepdims=True)
    layer_row = jnp.sum(jnp.where(key == ci, layer, 0), axis=0, keepdims=True) - 1
    table[...] = jnp.where(
        sub == 0,
        jnp.broadcast_to(key_row, (8, 128)),
        jnp.where(sub == 1, jnp.broadcast_to(patch_row, (8, 128)), jnp.broadcast_to(layer_row, (8, 128))),
    )
    keep = pltpu.make_async_copy(table, table_out, lsem.at[18])
    keep.start()
    look = pltpu.make_async_copy(table, keys, tsem)
    look.start()

    shifts = coarse_shifts((16, 128))

    def coarse_plane(x, carry):
        at = pl.multiple_of(x * 16, 16)
        cells = [c[i, pl.ds(at + 16, 16)] for i in range(5)]
        below = [c[i, pl.ds(at, 16)] for i in range(5)]
        above = [c[i, pl.ds(at + 32, 16)] for i in range(5)]
        for i, q in enumerate(hydro(cells, below, above, *shifts)):
            h[i, pl.ds(at, 16)] = q
        return carry

    lax.fori_loop(0, 16, coarse_plane, 0, unroll=4)

    look.wait()
    slots = [keys[2, 2 * me], keys[2, 2 * me + 1]]
    my_key = keys[0, me]

    side = lane % 2
    code = ((lane % 64) // 4) * 4 + (lane // 64) * 2 + (lane % 4) // 2
    picks = [lax.rem(jnp.where(side == 0, 16 * s + 127, 16 * s + 16) + 128, 128) for s in slots]
    cuts = [16 * jnp.maximum(s, 0) + lane % 16 for s in slots]
    inside = [
        jnp.where(((side == 0) & (s == 0)) | ((side == 1) & (s == 7)), 0.0, 1.0) for s in slots
    ]

    def z_values(src, base):
        low = iota((16, 128), 1) % 16 == 15

        def body(x, carry):
            at = pl.multiple_of(x * 16, 16)
            p, u, v, w, f = (src[i, pl.ds(at + base, 16)] for i in range(5))
            zv[0, pl.ds(at, 16)] = NB * (p + jnp.where(low, w, -w))
            zv[1, pl.ds(at, 16)] = NB * u
            zv[2, pl.ds(at, 16)] = NB * v
            zv[3, pl.ds(at, 16)] = f * jnp.where(low, NB * (1 + ADV[2]), NB * (1 - ADV[2]))
            return carry

        lax.fori_loop(0, 16, body, 0, unroll=4)

    def z_tiles():
        def body(x, tiles):
            tiles = list(tiles)
            for v in range(4):
                for odd in range(2):
                    q = zv[v, pl.ds(x * 16 + odd, 8, stride=2)]
                    here = code == x * 4 + (v % 2) * 2 + odd
                    for s in range(2):
                        tiles[s * 2 + v // 2] = jnp.where(here, take(q, picks[s]), tiles[s * 2 + v // 2])
            return tuple(tiles)

        tiles = lax.fori_loop(0, 16, body, (zero,) * 4, unroll=8)
        return [[tiles[s * 2 + w] * inside[s] for w in range(2)] for s in range(2)]

    def xy_tile(face, s):
        tile = zero
        for v in range(4):
            for odd in range(2):
                pos = v * 32 + odd * 16
                q = fv[face, v, pl.ds(odd, 8, stride=2)]
                tile = jnp.where(lane // 16 == pos // 16, take(q, cuts[s]), tile)
        return tile

    def put_tile(t, s, face, tile):
        p1[t, pl.ds(s * 6 + face, 8, stride=16)] = tile

    def get_tile(t, s, face):
        return p1[t, pl.ds(s * 6 + face, 8, stride=16)]

    z_values(c, 16)
    for s, pair in enumerate(z_tiles()):
        for w, tile in enumerate(pair):
            put_tile(0, s, 4 + w, tile)

    for halo in near:
        halo.wait_recv()
    mx = [jnp.where(region > 0, 1.0, 0.0), jnp.where(region < REGIONS - 1, 1.0, 0.0)]
    my = [jnp.where(me > 0, 1.0, 0.0), jnp.where(me < INNER - 1, 1.0, 0.0)]

    def near_x(e):
        return [xh[e, 0, i] for i in range(5)]

    def near_y(e):
        return [yh[e, 0, i] for i in range(5)]

    for e in range(2):
        p, u, v, w, f = near_x(e)
        for i, q in enumerate(face_values(p, u, v, w, f, 0, e == 1)):
            fv[e, i] = mx[e] * q
        p, u, v, w, f = near_y(e)
        for i, q in enumerate(face_values(p, v, u, w, f, 1, e == 1)):
            fv[2 + e, i] = my[e] * q
    for s in range(2):
        for face in range(4):
            put_tile(0, s, face, xy_tile(face, s))

    def send_pieces(t):
        r1[t][mine, 0:12] = p1[t, pl.ds(mine * 16, 12)]

        for k in (4, 3, 5, 2, 6, 1, 7):
            to = lax.rem(mine + k, 8)
            remote(
                p1.at[t, pl.ds(to * 16, 12)], r1[t].at[mine, pl.ds(0, 12)], 10 + t, (region, plane + to)
            ).start()

    send_pieces(0)

    def add_face(ref, cut, face, n, t1, high):
        e0, e1, e2, e3 = (fv[face, v, pl.ds(8 * cut[0], 8)] for v in range(4))
        at = cut[1]
        ref[0, at] = ref[0, at] + e0
        ref[n, at] = ref[n, at] - e0 if high else ref[n, at] + e0
        ref[t1, at] = ref[t1, at] + e1
        ref[3, at] = ref[3, at] + e2
        ref[4, at] = ref[4, at] + e3

    for half in range(2):
        add_face(h, (half, pl.ds(half * 8, 8)), 0, 1, 2, False)
        add_face(h, (half, pl.ds(240 + half * 8, 8)), 1, 1, 2, True)
        add_face(h, (half, pl.ds(half * 128, 8, stride=16)), 2, 2, 1, False)
        add_face(h, (half, pl.ds(half * 128 + 15, 8, stride=16)), 3, 2, 1, True)

    def coarse_burn(x, carry):
        at = pl.multiple_of(x * 64, 64)
        p, f = burn_once(h[0, pl.ds(at, 64)], h[4, pl.ds(at, 64)], cr[pl.ds(at, 64)])
        h[0, pl.ds(at, 64)] = p
        h[4, pl.ds(at, 64)] = f
        return carry

    lax.fori_loop(0, 4, coarse_burn, 0, unroll=4)

    z_values(h, 0)
    for s, pair in enumerate(z_tiles()):
        for w, tile in enumerate(pair):
            put_tile(1, s, 4 + w, 0.5 * (get_tile(0, s, 4 + w) + tile))
    for halo in far:
        halo.wait_recv()

    def own_rows(axis, e):
        if axis == 0:
            return [c[i, pl.ds(16 + 240 * e, 16)] for i in range(5)]
        return [
            jnp.concatenate([c[i, pl.ds(16 + 128 * b + 15 * e, 8, stride=16)] for b in range(2)], axis=0)
            for i in range(5)
        ]

    def corner(n, scale):
        return [dr[n, i : i + 1] * scale for i in range(5)]

    for e in range(2):
        values = ghost_step(
            near_x(e), [xh[e, 1, i] for i in range(5)], own_rows(0, e), corner(2 * e, my[0]), corner(2 * e + 1, my[1]), xr[e], 0, e == 1
        )
        for i, q in enumerate(values):
            fv[e, i] = mx[e] * q
        values = ghost_step(
            near_y(e), [yh[e, 1, i] for i in range(5)], own_rows(1, e),
            corner(e, mx[0]), corner(2 + e, mx[1]), yh[e, 1, 5], 1, e == 1,
        )
        for i, q in enumerate(values):
            fv[2 + e, i] = my[e] * q
    for s in range(2):
        for face in range(4):
            put_tile(1, s, face, 0.5 * (get_tile(0, s, face) + xy_tile(face, s)))
    send_pieces(1)
    stores = [pltpu.make_async_copy(h, h_out, lsem.at[0])]
    stores[0].start()

    for load in loads[3:]:
        load.wait()
    count = sv[0]
    counted = jnp.broadcast_to(count, (8, 128)).astype(F32)
    span = 0.25 / counted
    fine_shift = fine_shifts()

    def rates(x, carry):
        q = span * fr[x]
        fa[x] = 1.0 + q
        fb[x] = 0.5 * q
        return carry

    lax.fori_loop(0, 32, rates, 0, unroll=8)

    def fine_hydro(src, dst):
        def body(x, carry):
            cells = [src[i, x + 1] for i in range(5)]
            below = [src[i, x] for i in range(5)]
            above = [src[i, x + 2] for i in range(5)]
            for i, q in enumerate(hydro(cells, below, above, *fine_shift)):
                dst[i, x + 1] = q
            return carry

        lax.fori_loop(0, 32, body, 0, unroll=8)

    fine_hydro(f0, f1)

    def wait_all(ref, sem):
        pltpu.make_async_copy(ref, ref, sem).wait()

    def send_faces(t):
        wait_all(r1[t].at[pl.ds(0, 7), pl.ds(0, 12)], rsem.at[10 + t])

        def piece(key):
            pair = r1[t][(key & 15) >> 1]
            return jnp.where((key & 1) == 0, pair[0:6], pair[6:12])

        r2[t][me, 0:6] = piece(my_key)

        for k in FAR_FIRST:
            to = lax.rem(me + k, INNER)
            p2[t, to, 0:6] = piece(keys[0, to])
            remote(p2.at[t, to, pl.ds(0, 6)], r2[t].at[me, pl.ds(0, 6)], 12 + t, (region, to)).start()

    pl.semaphore_wait(ready, len(columns))
    send_faces(0)
    send_faces(1)

    q4, z = lane // 32, lane % 32
    edge_y = jnp.where((lane < 32) & (sub == 0) | (lane >= 96) & (sub == 7), 1.0, 0.0)
    sign_y = jnp.where(lane < 64, edge_y, -edge_y)
    edge_z = jnp.where((z == 0) | (z == 31), 1.0, 0.0)
    sign_z = jnp.where(z < 16, edge_z, -edge_z)
    pick_x = (q4 // 2) * 16 + z // 2
    pick_z = (q4 // 2) * 2 + z // 16

    def add_ghosts(t, dst):
        wait_all(r2[t].at[pl.ds(0, INNER - 1), pl.ds(0, 6)], rsem.at[12 + t])
        start = (my_key >> 4) * 8
        for k in range(8):
            gt[pl.ds(k * 8, 8)] = r2[t][start + k]
        tiles = [gt[pl.ds(face, 8, stride=8)] for face in range(6)]
        for face, x in ((0, 1), (1, 32)):
            e = [take(tiles[face], pick_x + 32 * v) for v in range(4)]
            dst[0, x] = dst[0, x] + e[0]
            dst[1, x] = dst[1, x] + e[0] if face == 0 else dst[1, x] - e[0]
            dst[2, x] = dst[2, x] + e[1]
            dst[3, x] = dst[3, x] + e[2]
            dst[4, x] = dst[4, x] + e[3]
        for v in range(4):
            for odd in range(2):
                pick = v * 32 + odd * 16 + z // 2
                ey[v, pl.ds(odd, 8, stride=2)] = jnp.where(lane < 64, take(tiles[2], pick), take(tiles[3], pick))

        def body(x, carry):
            y = [jnp.broadcast_to(ey[v, pl.ds(x, 1)], (8, 128)) for v in range(4)]
            zz = [take(tiles[4 + v // 2], pick_z + ((v % 2) * 64 + x * 4)) for v in range(4)]
            add = [
                edge_y * y[0] + edge_z * zz[0],
                edge_y * y[1] + edge_z * zz[1],
                sign_y * y[0] + edge_z * zz[2],
                edge_y * y[2] + sign_z * zz[0],
                edge_y * y[3] + edge_z * zz[3],
            ]
            for i in range(5):
                dst[i, 2 * x + 1] = dst[i, 2 * x + 1] + add[i]
                dst[i, 2 * x + 2] = dst[i, 2 * x + 2] + add[i]
            return carry

        lax.fori_loop(0, 16, body, 0, unroll=8)

    live = [jnp.where(turn < count, 1.0, 0.0) for turn in range(BURN_MAX)]
    group = 16

    def burn(dst, at):
        p = [dst[0, at + i + 1] for i in range(group)]
        f = [dst[4, at + i + 1] for i in range(group)]
        for turn in range(BURN_MAX):
            for i in range(group):
                r = pl.reciprocal(fa[at + i] + fb[at + i] * jnp.tanh(p[i]), approx=True)
                d = live[turn] * (f[i] - f[i] * r)
                f[i] = f[i] - d
                p[i] = p[i] + 0.5 * d
        for i in range(group):
            dst[0, at + i + 1] = p[i]
            dst[4, at + i + 1] = f[i]

    add_ghosts(0, f1)
    for at in range(0, 32, group):
        burn(f1, at)
    fine_hydro(f1, f0)
    add_ghosts(1, f0)
    pick_m = ((lane % 32) // 16) * 64 + 2 * (lane % 16)

    def means(a):
        for i in range(5):
            tile = zero
            for g in range(4):
                at = a * 8 + 2 * g
                q = f0[i, at + 1] + f0[i, at + 2]
                q = q + lanes(q, -1)
                q = q + lanes(q, -32)
                tile = jnp.where(q4 == g, take(q, pick_m), tile)
            mb[pl.ds(a * 64 + i, 8, stride=8)] = 0.125 * tile

    def send_mean(to):
        remote(mb.at[pl.ds(to * 8, 5)], r3.at[me, pl.ds(0, 5)], 14, (region, to)).start()

    for half in range(2):
        burn(f0, 16 * half)
        means(2 * half)
        means(2 * half + 1)
        for k in range(8, 24):
            to = 16 * half + lax.rem(me + k, 16)
            if k != 16:
                send_mean(to)
            else:
                pl.when(me != to)(functools.partial(send_mean, to))
    r3[me, 0:5] = mb[pl.ds(me * 8, 5)]
    for j in range(8):
        stores.append(
            pltpu.make_async_copy(
                f0.at[:, pl.ds(1, 32), j], fine_out.at[:, :, pl.ds(j * 128, 128)], lsem.at[2 + j]
            )
        )
        stores[-1].start()
    wait_all(r3.at[pl.ds(0, 31), pl.ds(0, 5)], rsem.at[14])

    def pick_pair(to):
        for s in range(2):
            p4[to, 5 * s : 5 * s + 5] = r3[keys[1, 2 * to + s], 0:5]

    pick_pair(me)
    stores.append(pltpu.make_async_copy(p4.at[me], r4.at[me], lsem.at[1]))
    stores[-1].start()

    for k in FAR_FIRST:
        to = lax.rem(me + k, INNER)
        pick_pair(to)
        remote(p4.at[to], r4.at[me], 15, (region, to)).start()

    for halo in near + far:
        halo.wait_send()
    for t in range(2):
        wait_all(r1[t].at[pl.ds(0, 7), pl.ds(0, 12)], ssem.at[10 + t])
        wait_all(r2[t].at[pl.ds(0, INNER - 1), pl.ds(0, 6)], ssem.at[12 + t])
    wait_all(r3.at[pl.ds(0, 31), pl.ds(0, 5)], ssem.at[14])
    wait_all(p4.at[pl.ds(0, 31)], ssem.at[15])
    for store in stores:
        store.wait()
    keep.wait()
    wait_all(r4.at[pl.ds(0, 31)], rsem.at[15])


def place(stepped, means, fine, table, coarse_out, fine_out, h, m, f, keys, sem):
    me = lax.axis_index("inner")
    loads = [
        pltpu.make_async_copy(means, m.at[:, pl.ds(0, 10)], sem.at[0]),
        pltpu.make_async_copy(table, keys, sem.at[1]),
        pltpu.make_async_copy(stepped, h, sem.at[2]),
    ]
    move = pltpu.make_async_copy(fine, f, sem.at[3])
    for load in loads:
        load.start()
    move.start()
    for load in loads:
        load.wait()
    lane = iota((8, 128), 1)
    here = [lane // 16 == keys[2, 2 * me + s] for s in range(2)]
    rows_of = m.reshape(512, 128)
    stores = []
    for i in range(5):

        def body(a, carry):
            tiles = [rows_of[pl.ds(a * 128 + s * 5 + i, 8, stride=16)] for s in range(2)]
            for g in range(4):
                for odd in range(2):
                    at = pl.ds((a * 4 + g) * 16 + odd, 8, stride=2)
                    q = h[i, at]
                    for s in range(2):
                        q = jnp.where(here[s], take(tiles[s], lane % 16 + (g * 32 + odd * 16)), q)
                    h[i, at] = q
            return carry

        lax.fori_loop(0, 4, body, 0, unroll=4)
        stores.append(pltpu.make_async_copy(h.at[i], coarse_out.at[i], sem.at[4 + i]))
        stores[-1].start()
        if i == 0:
            move.wait()
            stores.append(pltpu.make_async_copy(f, fine_out, sem.at[3]))
            stores[-1].start()
    for store in stores:
        store.wait()


def per_device(coarse_state, fine_state, coarse_rate, fine_rate, parents, burn_steps):
    anywhere = pl.BlockSpec(memory_space=pl.ANY)
    stepped, fine_mid, means, table = pl.pallas_call(
        kernel,
        out_shape=(
            jax.ShapeDtypeStruct((5, 256, 128), F32),
            jax.ShapeDtypeStruct((5, 32, 1024), F32),
            jax.ShapeDtypeStruct((32, 10, 128), F32),
            jax.ShapeDtypeStruct((8, 128), jnp.int32),
        ),
        in_specs=[anywhere] * 6,
        out_specs=(anywhere,) * 4,
        scratch_shapes=[
            pltpu.VMEM((5, 288, 128), F32),
            pltpu.VMEM((5, 256, 128), F32),
            pltpu.VMEM((256, 128), F32),
            pltpu.VMEM((2, 2, 5, 16, 128), F32),
            pltpu.VMEM((2, 16, 128), F32),
            pltpu.VMEM((2, 2, 6, 16, 128), F32),
            pltpu.VMEM((2, 2, 6, 16, 128), F32),
            pltpu.VMEM((4, 8, 128), F32),
            pltpu.VMEM((4, 8, 128), F32),
            pltpu.VMEM((4, 4, 16, 128), F32),
            pltpu.VMEM((4, 256, 128), F32),
            pltpu.VMEM((8, 128), jnp.int32),
            pltpu.SMEM((8, 128), jnp.int32),
            pltpu.VMEM((2, 128, 128), F32),
            pltpu.VMEM((8, 16, 128), F32),
            pltpu.VMEM((8, 16, 128), F32),
            pltpu.VMEM((2, 32, 8, 128), F32),
            pltpu.VMEM((32, 8, 128), F32),
            pltpu.VMEM((32, 8, 128), F32),
            pltpu.VMEM((5, 34, 8, 128), F32),
            pltpu.VMEM((5, 34, 8, 128), F32),
            pltpu.VMEM((32, 8, 128), F32),
            pltpu.VMEM((32, 8, 128), F32),
            pltpu.VMEM((32, 8, 128), F32),
            pltpu.VMEM((64, 128), F32),
            pltpu.VMEM((4, 16, 128), F32),
            pltpu.VMEM((256, 128), F32),
            pltpu.VMEM((32, 8, 128), F32),
            pltpu.VMEM((32, 10, 128), F32),
            pltpu.VMEM((1, 32), jnp.int32),
            pltpu.SMEM((1,), jnp.int32),
            pltpu.SemaphoreType.DMA((20,)),
            pltpu.SemaphoreType.DMA((20,)),
            pltpu.SemaphoreType.DMA((20,)),
            pltpu.SemaphoreType.DMA,
            pltpu.SemaphoreType.REGULAR,
        ],
        compiler_params=pltpu.CompilerParams(
            collective_id=0, has_side_effects=True, vmem_limit_bytes=60 * 2**20
        ),
        name="reactive_step",
    )(
        coarse_state.reshape(5, 256, 128),
        fine_state.reshape(5, 32, 1024),
        coarse_rate.reshape(256, 128),
        fine_rate.reshape(32, 1024),
        parents,
        burn_steps,
    )
    coarse_new, fine_new = pl.pallas_call(
        place,
        out_shape=(
            jax.ShapeDtypeStruct((5, 256, 128), F32),
            jax.ShapeDtypeStruct((5, 32, 1024), F32),
        ),
        in_specs=[anywhere] * 4,
        out_specs=(anywhere,) * 2,
        scratch_shapes=[
            pltpu.VMEM((5, 256, 128), F32),
            pltpu.VMEM((32, 16, 128), F32),
            pltpu.VMEM((5, 32, 1024), F32),
            pltpu.SMEM((8, 128), jnp.int32),
            pltpu.SemaphoreType.DMA((9,)),
        ],
        compiler_params=pltpu.CompilerParams(vmem_limit_bytes=60 * 2**20),
        name="place",
    )(stepped, means, fine_mid, table)
    return coarse_new.reshape(5, 16, 16, 128), fine_new.reshape(1, 5, 32, 1024)


def solution(mesh):
    in_specs = (
        P(None, "region", "inner", None),
        P(("region", "inner"), None, None, None),
        P("region", "inner", None),
        P(("region", "inner"), None, None),
        P("region", None),
        P(("region", "inner")),
    )
    out_specs = (P(None, "region", "inner", None), P(("region", "inner"), None, None, None))
    return jax.shard_map(per_device, mesh=mesh, in_specs=in_specs, out_specs=out_specs, check_vma=False)
```

```python
import functools

import jax
import jax.numpy as jnp
from jax import lax
from jax.experimental import pallas as pl
from jax.experimental.pallas import tpu as pltpu
from jax.sharding import PartitionSpec as P

MESH = pl.DeviceIdType.MESH
F32 = jnp.float32
ADV = (0.5, -0.3, 0.2)
KEEP = 0.1
NB = 0.15
BURN_MAX = 8
REGIONS = 4
INNER = 32


def hops(offset):
    z, y = offset // 8, offset // 2 % 4
    return min(z, 4 - z) + min(y, 4 - y)


FAR_FIRST = sorted(range(1, INNER), key=hops, reverse=True)


def iota(shape, axis):
    return lax.broadcasted_iota(jnp.int32, shape, axis)


def lanes(q, shift):
    return pltpu.roll(q, shift % 128, 1)


def rows(q, shift):
    return pltpu.roll(q, shift % q.shape[0], 0)


def hydro(c, xm, xp, yd, yu, zd, zu):
    p, u, v, w, f = c
    sx, mx = xm[0] + xm[1], xp[0] - xp[1]
    sy, my = yd(p + v), yu(p - v)
    sz, mz = zd(p + w), zu(p - w)
    hp = (sx + mx) + (sy + my) + (sz + mz)
    hu = (sx - mx) + (yd(u) + yu(u)) + (zd(u) + zu(u))
    hv = (xm[2] + xp[2]) + (sy - my) + (zd(v) + zu(v))
    hw = (xm[3] + xp[3]) + (yd(w) + yu(w)) + (sz - mz)
    hf = (
        ((1 + ADV[0]) * xm[4] + (1 - ADV[0]) * xp[4])
        + ((1 + ADV[1]) * yd(f) + (1 - ADV[1]) * yu(f))
        + ((1 + ADV[2]) * zd(f) + (1 - ADV[2]) * zu(f))
    )
    return [KEEP * a + NB * b for a, b in zip(c, (hp, hu, hv, hw, hf))]


def take(q, index):
    return jnp.take_along_axis(q, index, axis=1, mode="promise_in_bounds")


def coarse_shifts(shape):
    row, lane = iota(shape, 0), iota(shape, 1)
    zd = lambda q: jnp.where(lane == 0, 0.0, lanes(q, 1))
    zu = lambda q: jnp.where(lane == 127, 0.0, lanes(q, -1))
    yd = lambda q: jnp.where(row == 0, 0.0, rows(q, 1))
    yu = lambda q: jnp.where(row == shape[0] - 1, 0.0, rows(q, -1))
    return yd, yu, zd, zu


def fine_shifts():
    sub, lane = iota((8, 128), 0), iota((8, 128), 1)
    z = lane % 32

    def yd(q):
        t = lanes(q, 32)
        t = jnp.where(lane < 32, rows(t, 1), t)
        return jnp.where((lane < 32) & (sub == 0), 0.0, t)

    def yu(q):
        t = lanes(q, -32)
        t = jnp.where(lane >= 96, rows(t, -1), t)
        return jnp.where((lane >= 96) & (sub == 7), 0.0, t)

    zd = lambda q: jnp.where(z == 0, 0.0, lanes(q, 1))
    zu = lambda q: jnp.where(z == 31, 0.0, lanes(q, -1))
    return yd, yu, zd, zu


def burn_once(p, f, rate):
    burned = f * pl.reciprocal(1.0 + 0.5 * rate * (1.0 + 0.5 * jnp.tanh(p)), approx=True)
    return p + 0.5 * (f - burned), burned


def face_values(p, n, t1, t2, f, axis, high):
    sign = -1.0 if high else 1.0
    return [NB * (p + sign * n), NB * t1, NB * t2, NB * (1 + sign * ADV[axis]) * f]


def ghost_step(near, far, own, dlo, dhi, rate, axis, high):
    n, r = (1, 2) if axis == 0 else (2, 1)
    row, lane = iota((16, 128), 0), iota((16, 128), 1)
    an, ar, az = ADV[axis], ADV[1 - axis], ADV[2]
    minus, plus = (own, far) if high else (far, own)
    p, w, f = near[0], near[3], near[4]

    def rd(q, d):
        return jnp.where(row == 0, d, rows(q, 1))

    def ru(q, d):
        return jnp.where(row == 15, d, rows(q, -1))

    zd = lambda q: jnp.where(lane == 0, 0.0, lanes(q, 1))
    zu = lambda q: jnp.where(lane == 127, 0.0, lanes(q, -1))
    sn, mn = minus[0] + minus[n], plus[0] - plus[n]
    sr, mr = rd(p + near[r], dlo[0] + dlo[r]), ru(p - near[r], dhi[0] - dhi[r])
    sz, mz = zd(p + w), zu(p - w)
    hp = (sn + mn) + (sr + mr) + (sz + mz)
    hn = (sn - mn) + (rd(near[n], dlo[n]) + ru(near[n], dhi[n])) + (zd(near[n]) + zu(near[n]))
    hr = (minus[r] + plus[r]) + (sr - mr) + (zd(near[r]) + zu(near[r]))
    hw = (minus[3] + plus[3]) + (rd(w, dlo[3]) + ru(w, dhi[3])) + (sz - mz)
    hf = (
        ((1 + an) * minus[4] + (1 - an) * plus[4])
        + ((1 + ar) * rd(f, dlo[4]) + (1 - ar) * ru(f, dhi[4]))
        + ((1 + az) * zd(f) + (1 - az) * zu(f))
    )
    pressure, normal, tangent, across, fuel = (
        KEEP * a + NB * b for a, b in zip((p, near[n], near[r], w, f), (hp, hn, hr, hw, hf))
    )
    pressure, fuel = burn_once(pressure, fuel, rate)
    return face_values(pressure, normal, tangent, across, fuel, axis, high)


def kernel(
    coarse, fine, crate, frate, parents, steps, h_out, fine_out, r4, table_out,
    c, h, cr, xh, xr, ys, yh, ds, dr, fv, zv, table, keys, p1, r1a, r1b, p2, r2a, r2b, f0, f1, fa, fb, fr, gt, ey,
    mb, r3, p4, pv, sv, ssem, rsem, lsem, tsem, ready,
):
    r1, r2 = (r1a, r1b), (r2a, r2b)
    region, me = lax.axis_index("region"), lax.axis_index("inner")
    up, down = lax.rem(region + 1, REGIONS), lax.rem(region + REGIONS - 1, REGIONS)
    right, left = lax.rem(me + 1, INNER), lax.rem(me + INNER - 1, INNER)
    plane, mine = (me // 8) * 8, lax.rem(me, 8)
    sub, lane = iota((8, 128), 0), iota((8, 128), 1)

    barrier = pltpu.get_barrier_semaphore()
    has_x = [region > 0, region < REGIONS - 1]
    has_y = [me > 0, me < INNER - 1]
    side_x, side_y = (down, up), (left, right)
    columns = [(region, lax.rem(me + 8 * k, INNER)) for k in (2, 1, 3)]
    greeted = [(True, other) for other in columns]
    for e in range(2):
        greeted.append((has_x[e], (side_x[e], me)))
        greeted.append((has_y[e] & (mine == 7 * e), (region, side_y[e])))
        for d in range(2):
            greeted.append((has_x[e] & has_y[d], (side_x[e], side_y[d])))
    for k in range(1, 8):
        greeted.append((True, (region, plane + lax.rem(mine + k, 8))))

    def hello(to):
        pl.semaphore_signal(barrier, inc=1, device_id=to, device_id_type=MESH)

    expected = 0
    for exists, to in greeted:
        if exists is True:
            hello(to)
            expected = expected + 1
        else:
            pl.when(exists)(functools.partial(hello, to))
            expected = expected + jnp.where(exists, 1, 0)
    loads = [
        pltpu.make_async_copy(coarse, c.at[:, pl.ds(16, 256)], lsem.at[0]),
        pltpu.make_async_copy(crate, cr, lsem.at[1]),
        pltpu.make_async_copy(parents, pv, lsem.at[18]),
        pltpu.make_async_copy(steps, sv, lsem.at[19]),
    ]
    for j in range(8):
        cut = pl.ds(j * 128, 128)
        loads.append(pltpu.make_async_copy(fine.at[:, :, cut], f0.at[:, pl.ds(1, 32), j], lsem.at[2 + j]))
        loads.append(pltpu.make_async_copy(frate.at[:, cut], fr.at[:, j], lsem.at[10 + j]))
    for load in loads:
        load.start()

    zero = jnp.zeros((8, 128), F32)
    for i in range(5):
        c[i, 0:16] = jnp.zeros((16, 128), F32)
        c[i, 272:288] = jnp.zeros((16, 128), F32)
        for a in (0, 33):
            f0[i, a] = zero
            f1[i, a] = zero
    loads[0].wait()
    loads[1].wait()
    for side, (near, far) in enumerate(((15, 14), (0, 1))):
        for half in range(2):
            dst = pl.ds(half * 8, 8)
            for i in range(5):
                ys[side, 0, i, dst] = c[i, pl.ds(16 + half * 128 + near, 8, stride=16)]
                ys[side, 1, i, dst] = c[i, pl.ds(16 + half * 128 + far, 8, stride=16)]
            ys[side, 1, 5, dst] = cr[pl.ds(half * 128 + near, 8, stride=16)]
    for n, at in enumerate((255, 240, 15, 0)):
        for i in range(5):
            ds[n, i : i + 1] = c[i, 16 + at : 17 + at]
        ds[n, 5:8] = jnp.zeros((3, 128), F32)

    for e in range(2):

        @pl.when(~has_x[e])
        def _():
            xh[e] = jnp.zeros(xh.shape[1:], F32)
            xr[e] = jnp.zeros(xr.shape[1:], F32)

        @pl.when(~has_y[e])
        def _():
            yh[e] = jnp.zeros(yh.shape[1:], F32)

        for d in range(2):

            @pl.when(~(has_x[e] & has_y[d]))
            def _():
                dr[2 * e + d] = jnp.zeros((8, 128), F32)

    pl.semaphore_wait(barrier, expected)

    def remote(src, dst, n, to):
        return pltpu.make_async_remote_copy(
            src_ref=src, dst_ref=dst, send_sem=ssem.at[n], recv_sem=rsem.at[n], device_id=to, device_id_type=MESH
        )

    near, far = [], []
    for e in range(2):
        o = 1 - e
        near.append((remote(c.at[:, pl.ds(16 + 240 * o, 16)], xh.at[e, 0], e, (side_x[o], me)), has_x[o], has_x[e]))
        near.append(
            (
                remote(ys.at[e, 0, pl.ds(0, 5)], yh.at[e, 0, pl.ds(0, 5)], 2 + e, (region, side_y[o])),
                has_y[o],
                has_y[e],
            )
        )
        far.append((remote(cr.at[pl.ds(240 * o, 16)], xr.at[e], 8 + e, (side_x[o], me)), has_x[o], has_x[e]))
        far.append(
            (remote(c.at[:, pl.ds(32 + 208 * o, 16)], xh.at[e, 1], 16 + e, (side_x[o], me)), has_x[o], has_x[e])
        )
        far.append((remote(ys.at[e, 1], yh.at[e, 1], 18 + e, (region, side_y[o])), has_y[o], has_y[e]))
    for n in range(4):
        e, d = n // 2, n % 2
        far.insert(
            n,
            (
                remote(ds.at[n], dr.at[n], 4 + n, (side_x[1 - e], side_y[1 - d])),
                has_x[1 - e] & has_y[1 - d],
                has_x[e] & has_y[d],
            ),
        )
    for halo, sends, _ in near + far:
        pl.when(sends)(halo.start)
    for other in columns:
        pl.semaphore_signal(ready, inc=1, device_id=other, device_id_type=MESH)

    loads[2].wait()
    block_row = jnp.broadcast_to(pv[...], (32, 32))
    ri, ci = iota((32, 32), 0), iota((32, 32), 1)
    block = jnp.sum(jnp.where(ri == ci, block_row, 0), axis=1, keepdims=True)
    owner = block >> 3
    slot = jnp.sum(
        jnp.where((jnp.broadcast_to(owner, (32, 32)) == (block_row >> 3)) & (ci < ri), 1, 0),
        axis=1,
        keepdims=True,
    )
    key = jnp.broadcast_to(owner * 2 + slot, (32, 128))
    ri, ci = iota((32, 128), 0), iota((32, 128), 1)
    layer = jnp.broadcast_to((block & 7) + 1, (32, 128))
    key_row = jnp.sum(jnp.where(ri == ci, key, 0), axis=0, keepdims=True)
    patch_row = jnp.sum(jnp.where(key == ci, ri, 0), axis=0, keepdims=True)
    layer_row = jnp.sum(jnp.where(key == ci, layer, 0), axis=0, keepdims=True) - 1
    table[...] = jnp.where(
        sub == 0,
        jnp.broadcast_to(key_row, (8, 128)),
        jnp.where(sub == 1, jnp.broadcast_to(patch_row, (8, 128)), jnp.broadcast_to(layer_row, (8, 128))),
    )
    keep = pltpu.make_async_copy(table, table_out, lsem.at[18])
    keep.start()
    look = pltpu.make_async_copy(table, keys, tsem)
    look.start()

    shifts = coarse_shifts((16, 128))

    def coarse_plane(x, carry):
        at = pl.multiple_of(x * 16, 16)
        cells = [c[i, pl.ds(at + 16, 16)] for i in range(5)]
        below = [c[i, pl.ds(at, 16)] for i in range(5)]
        above = [c[i, pl.ds(at + 32, 16)] for i in range(5)]
        for i, q in enumerate(hydro(cells, below, above, *shifts)):
            h[i, pl.ds(at, 16)] = q
        return carry

    lax.fori_loop(0, 16, coarse_plane, 0, unroll=4)

    look.wait()
    slots = [keys[2, 2 * me], keys[2, 2 * me + 1]]
    my_key = keys[0, me]

    side = lane % 2
    code = ((lane % 64) // 4) * 4 + (lane // 64) * 2 + (lane % 4) // 2
    picks = [lax.rem(jnp.where(side == 0, 16 * s + 127, 16 * s + 16) + 128, 128) for s in slots]
    cuts = [16 * jnp.maximum(s, 0) + lane % 16 for s in slots]
    inside = [
        jnp.where(((side == 0) & (s == 0)) | ((side == 1) & (s == 7)), 0.0, 1.0) for s in slots
    ]

    def z_values(src, base):
        low = iota((16, 128), 1) % 16 == 15

        def body(x, carry):
            at = pl.multiple_of(x * 16, 16)
            p, u, v, w, f = (src[i, pl.ds(at + base, 16)] for i in range(5))
            zv[0, pl.ds(at, 16)] = NB * (p + jnp.where(low, w, -w))
            zv[1, pl.ds(at, 16)] = NB * u
            zv[2, pl.ds(at, 16)] = NB * v
            zv[3, pl.ds(at, 16)] = f * jnp.where(low, NB * (1 + ADV[2]), NB * (1 - ADV[2]))
            return carry

        lax.fori_loop(0, 16, body, 0, unroll=4)

    def z_tiles():
        def body(x, tiles):
            tiles = list(tiles)
            for v in range(4):
                for odd in range(2):
                    q = zv[v, pl.ds(x * 16 + odd, 8, stride=2)]
                    here = code == x * 4 + (v % 2) * 2 + odd
                    for s in range(2):
                        tiles[s * 2 + v // 2] = jnp.where(here, take(q, picks[s]), tiles[s * 2 + v // 2])
            return tuple(tiles)

        tiles = lax.fori_loop(0, 16, body, (zero,) * 4, unroll=8)
        return [[tiles[s * 2 + w] * inside[s] for w in range(2)] for s in range(2)]

    def xy_tile(face, s):
        tile = zero
        for v in range(4):
            for odd in range(2):
                pos = v * 32 + odd * 16
                q = fv[face, v, pl.ds(odd, 8, stride=2)]
                tile = jnp.where(lane // 16 == pos // 16, take(q, cuts[s]), tile)
        return tile

    def put_tile(t, s, face, tile):
        p1[t, pl.ds(s * 6 + face, 8, stride=16)] = tile

    def get_tile(t, s, face):
        return p1[t, pl.ds(s * 6 + face, 8, stride=16)]

    z_values(c, 16)
    for s, pair in enumerate(z_tiles()):
        for w, tile in enumerate(pair):
            put_tile(0, s, 4 + w, tile)

    for halo, _, arrives in near:
        pl.when(arrives)(halo.wait_recv)
    mx = [jnp.where(exists, 1.0, 0.0) for exists in has_x]
    my = [jnp.where(exists, 1.0, 0.0) for exists in has_y]

    def near_x(e):
        return [xh[e, 0, i] for i in range(5)]

    def near_y(e):
        return [yh[e, 0, i] for i in range(5)]

    for e in range(2):
        p, u, v, w, f = near_x(e)
        for i, q in enumerate(face_values(p, u, v, w, f, 0, e == 1)):
            fv[e, i] = mx[e] * q
        p, u, v, w, f = near_y(e)
        for i, q in enumerate(face_values(p, v, u, w, f, 1, e == 1)):
            fv[2 + e, i] = my[e] * q
    for s in range(2):
        for face in range(4):
            put_tile(0, s, face, xy_tile(face, s))

    def send_pieces(t):
        r1[t][mine, 0:12] = p1[t, pl.ds(mine * 16, 12)]

        for k in (4, 3, 5, 2, 6, 1, 7):
            to = lax.rem(mine + k, 8)
            remote(
                p1.at[t, pl.ds(to * 16, 12)], r1[t].at[mine, pl.ds(0, 12)], 10 + t, (region, plane + to)
            ).start()

    send_pieces(0)

    def add_face(ref, cut, face, n, t1, high):
        e0, e1, e2, e3 = (fv[face, v, pl.ds(8 * cut[0], 8)] for v in range(4))
        at = cut[1]
        ref[0, at] = ref[0, at] + e0
        ref[n, at] = ref[n, at] - e0 if high else ref[n, at] + e0
        ref[t1, at] = ref[t1, at] + e1
        ref[3, at] = ref[3, at] + e2
        ref[4, at] = ref[4, at] + e3

    for half in range(2):
        add_face(h, (half, pl.ds(half * 8, 8)), 0, 1, 2, False)
        add_face(h, (half, pl.ds(240 + half * 8, 8)), 1, 1, 2, True)
        add_face(h, (half, pl.ds(half * 128, 8, stride=16)), 2, 2, 1, False)
        add_face(h, (half, pl.ds(half * 128 + 15, 8, stride=16)), 3, 2, 1, True)

    def coarse_burn(x, carry):
        at = pl.multiple_of(x * 64, 64)
        p, f = burn_once(h[0, pl.ds(at, 64)], h[4, pl.ds(at, 64)], cr[pl.ds(at, 64)])
        h[0, pl.ds(at, 64)] = p
        h[4, pl.ds(at, 64)] = f
        return carry

    lax.fori_loop(0, 4, coarse_burn, 0, unroll=4)

    z_values(h, 0)
    for s, pair in enumerate(z_tiles()):
        for w, tile in enumerate(pair):
            put_tile(1, s, 4 + w, 0.5 * (get_tile(0, s, 4 + w) + tile))
    for halo, _, arrives in far:
        pl.when(arrives)(halo.wait_recv)

    def own_rows(axis, e):
        if axis == 0:
            return [c[i, pl.ds(16 + 240 * e, 16)] for i in range(5)]
        return [
            jnp.concatenate([c[i, pl.ds(16 + 128 * b + 15 * e, 8, stride=16)] for b in range(2)], axis=0)
            for i in range(5)
        ]

    def corner(n, scale):
        return [dr[n, i : i + 1] * scale for i in range(5)]

    for e in range(2):
        values = ghost_step(
            near_x(e), [xh[e, 1, i] for i in range(5)], own_rows(0, e), corner(2 * e, my[0]), corner(2 * e + 1, my[1]), xr[e], 0, e == 1
        )
        for i, q in enumerate(values):
            fv[e, i] = mx[e] * q
        values = ghost_step(
            near_y(e), [yh[e, 1, i] for i in range(5)], own_rows(1, e),
            corner(e, mx[0]), corner(2 + e, mx[1]), yh[e, 1, 5], 1, e == 1,
        )
        for i, q in enumerate(values):
            fv[2 + e, i] = my[e] * q
    for s in range(2):
        for face in range(4):
            put_tile(1, s, face, 0.5 * (get_tile(0, s, face) + xy_tile(face, s)))
    send_pieces(1)
    stores = [pltpu.make_async_copy(h, h_out, lsem.at[0])]
    stores[0].start()

    for load in loads[3:]:
        load.wait()
    count = sv[0]
    counted = jnp.broadcast_to(count, (8, 128)).astype(F32)
    span = 0.25 / counted
    fine_shift = fine_shifts()

    def rates(x, carry):
        q = span * fr[x]
        fa[x] = 1.0 + q
        fb[x] = 0.5 * q
        return carry

    lax.fori_loop(0, 32, rates, 0, unroll=8)

    def fine_hydro(src, dst):
        def body(x, carry):
            cells = [src[i, x + 1] for i in range(5)]
            below = [src[i, x] for i in range(5)]
            above = [src[i, x + 2] for i in range(5)]
            for i, q in enumerate(hydro(cells, below, above, *fine_shift)):
                dst[i, x + 1] = q
            return carry

        lax.fori_loop(0, 32, body, 0, unroll=8)

    fine_hydro(f0, f1)

    def wait_all(ref, sem):
        pltpu.make_async_copy(ref, ref, sem).wait()

    def send_faces(t):
        wait_all(r1[t].at[pl.ds(0, 7), pl.ds(0, 12)], rsem.at[10 + t])

        def piece(key):
            pair = r1[t][(key & 15) >> 1]
            return jnp.where((key & 1) == 0, pair[0:6], pair[6:12])

        r2[t][me, 0:6] = piece(my_key)

        for k in FAR_FIRST:
            to = lax.rem(me + k, INNER)
            p2[t, to, 0:6] = piece(keys[0, to])
        for k in FAR_FIRST:
            to = lax.rem(me + k, INNER)
            remote(p2.at[t, to, pl.ds(0, 6)], r2[t].at[me, pl.ds(0, 6)], 12 + t, (region, to)).start()

    pl.semaphore_wait(ready, len(columns))
    send_faces(0)
    send_faces(1)

    q4, z = lane // 32, lane % 32
    edge_y = jnp.where((lane < 32) & (sub == 0) | (lane >= 96) & (sub == 7), 1.0, 0.0)
    sign_y = jnp.where(lane < 64, edge_y, -edge_y)
    edge_z = jnp.where((z == 0) | (z == 31), 1.0, 0.0)
    sign_z = jnp.where(z < 16, edge_z, -edge_z)
    pick_x = (q4 // 2) * 16 + z // 2
    pick_z = (q4 // 2) * 2 + z // 16

    def add_ghosts(t, dst):
        wait_all(r2[t].at[pl.ds(0, INNER - 1), pl.ds(0, 6)], rsem.at[12 + t])
        start = (my_key >> 4) * 8
        for k in range(8):
            gt[pl.ds(k * 8, 8)] = r2[t][start + k]
        tiles = [gt[pl.ds(face, 8, stride=8)] for face in range(6)]
        for face, x in ((0, 1), (1, 32)):
            e = [take(tiles[face], pick_x + 32 * v) for v in range(4)]
            dst[0, x] = dst[0, x] + e[0]
            dst[1, x] = dst[1, x] + e[0] if face == 0 else dst[1, x] - e[0]
            dst[2, x] = dst[2, x] + e[1]
            dst[3, x] = dst[3, x] + e[2]
            dst[4, x] = dst[4, x] + e[3]
        for v in range(4):
            for odd in range(2):
                pick = v * 32 + odd * 16 + z // 2
                ey[v, pl.ds(odd, 8, stride=2)] = jnp.where(lane < 64, take(tiles[2], pick), take(tiles[3], pick))

        def body(x, carry):
            y = [jnp.broadcast_to(ey[v, pl.ds(x, 1)], (8, 128)) for v in range(4)]
            zz = [take(tiles[4 + v // 2], pick_z + ((v % 2) * 64 + x * 4)) for v in range(4)]
            add = [
                edge_y * y[0] + edge_z * zz[0],
                edge_y * y[1] + edge_z * zz[1],
                sign_y * y[0] + edge_z * zz[2],
                edge_y * y[2] + sign_z * zz[0],
                edge_y * y[3] + edge_z * zz[3],
            ]
            for i in range(5):
                dst[i, 2 * x + 1] = dst[i, 2 * x + 1] + add[i]
                dst[i, 2 * x + 2] = dst[i, 2 * x + 2] + add[i]
            return carry

        lax.fori_loop(0, 16, body, 0, unroll=8)

    live = [jnp.where(turn < count, 1.0, 0.0) for turn in range(BURN_MAX)]
    group = 16

    def burn(dst, at):
        p = [dst[0, at + i + 1] for i in range(group)]
        f = [dst[4, at + i + 1] for i in range(group)]
        for turn in range(BURN_MAX):
            for i in range(group):
                r = pl.reciprocal(fa[at + i] + fb[at + i] * jnp.tanh(p[i]), approx=True)
                d = live[turn] * (f[i] - f[i] * r)
                f[i] = f[i] - d
                p[i] = p[i] + 0.5 * d
        for i in range(group):
            dst[0, at + i + 1] = p[i]
            dst[4, at + i + 1] = f[i]

    add_ghosts(0, f1)
    for at in range(0, 32, group):
        burn(f1, at)
    fine_hydro(f1, f0)
    add_ghosts(1, f0)
    pick_m = ((lane % 32) // 16) * 64 + 2 * (lane % 16)

    def means(a):
        for i in range(5):
            tile = zero
            for g in range(4):
                at = a * 8 + 2 * g
                q = f0[i, at + 1] + f0[i, at + 2]
                q = q + lanes(q, -1)
                q = q + lanes(q, -32)
                tile = jnp.where(q4 == g, take(q, pick_m), tile)
            mb[pl.ds(a * 64 + i, 8, stride=8)] = 0.125 * tile

    def send_mean(to):
        remote(mb.at[pl.ds(to * 8, 5)], r3.at[me, pl.ds(0, 5)], 14, (region, to)).start()

    for half in range(2):
        burn(f0, 16 * half)
        means(2 * half)
        means(2 * half + 1)
        for k in range(8, 24):
            to = 16 * half + lax.rem(me + k, 16)
            if k != 16:
                send_mean(to)
            else:
                pl.when(me != to)(functools.partial(send_mean, to))
    r3[me, 0:5] = mb[pl.ds(me * 8, 5)]
    for j in range(8):
        stores.append(
            pltpu.make_async_copy(
                f0.at[:, pl.ds(1, 32), j], fine_out.at[:, :, pl.ds(j * 128, 128)], lsem.at[2 + j]
            )
        )
        stores[-1].start()
    wait_all(r3.at[pl.ds(0, 31), pl.ds(0, 5)], rsem.at[14])

    def pick_pair(to):
        for s in range(2):
            p4[to, 5 * s : 5 * s + 5] = r3[keys[1, 2 * to + s], 0:5]

    pick_pair(me)
    stores.append(pltpu.make_async_copy(p4.at[me], r4.at[me], lsem.at[1]))
    stores[-1].start()

    for k in FAR_FIRST:
        to = lax.rem(me + k, INNER)
        pick_pair(to)
    for k in FAR_FIRST:
        to = lax.rem(me + k, INNER)
        remote(p4.at[to], r4.at[me], 15, (region, to)).start()

    for halo, sends, _ in near + far:
        pl.when(sends)(halo.wait_send)
    for t in range(2):
        wait_all(r1[t].at[pl.ds(0, 7), pl.ds(0, 12)], ssem.at[10 + t])
        wait_all(r2[t].at[pl.ds(0, INNER - 1), pl.ds(0, 6)], ssem.at[12 + t])
    wait_all(r3.at[pl.ds(0, 31), pl.ds(0, 5)], ssem.at[14])
    wait_all(p4.at[pl.ds(0, 31)], ssem.at[15])
    for store in stores:
        store.wait()
    keep.wait()
    wait_all(r4.at[pl.ds(0, 31)], rsem.at[15])


def place(stepped, means, fine, table, coarse_out, fine_out, h, m, f, keys, sem):
    me = lax.axis_index("inner")
    loads = [
        pltpu.make_async_copy(means, m.at[:, pl.ds(0, 10)], sem.at[0]),
        pltpu.make_async_copy(table, keys, sem.at[1]),
        pltpu.make_async_copy(stepped, h, sem.at[2]),
    ]
    move = pltpu.make_async_copy(fine, f, sem.at[3])
    for load in loads:
        load.start()
    move.start()
    for load in loads:
        load.wait()
    lane = iota((8, 128), 1)
    here = [lane // 16 == keys[2, 2 * me + s] for s in range(2)]
    rows_of = m.reshape(512, 128)
    stores = []
    for i in range(5):

        def body(a, carry):
            tiles = [rows_of[pl.ds(a * 128 + s * 5 + i, 8, stride=16)] for s in range(2)]
            for g in range(4):
                for odd in range(2):
                    at = pl.ds((a * 4 + g) * 16 + odd, 8, stride=2)
                    q = h[i, at]
                    for s in range(2):
                        q = jnp.where(here[s], take(tiles[s], lane % 16 + (g * 32 + odd * 16)), q)
                    h[i, at] = q
            return carry

        lax.fori_loop(0, 4, body, 0, unroll=4)
        stores.append(pltpu.make_async_copy(h.at[i], coarse_out.at[i], sem.at[4 + i]))
        stores[-1].start()
        if i == 0:
            move.wait()
            stores.append(pltpu.make_async_copy(f, fine_out, sem.at[3]))
            stores[-1].start()
    for store in stores:
        store.wait()


def per_device(coarse_state, fine_state, coarse_rate, fine_rate, parents, burn_steps):
    anywhere = pl.BlockSpec(memory_space=pl.ANY)
    stepped, fine_mid, means, table = pl.pallas_call(
        kernel,
        out_shape=(
            jax.ShapeDtypeStruct((5, 256, 128), F32),
            jax.ShapeDtypeStruct((5, 32, 1024), F32),
            jax.ShapeDtypeStruct((32, 10, 128), F32),
            jax.ShapeDtypeStruct((8, 128), jnp.int32),
        ),
        in_specs=[anywhere] * 6,
        out_specs=(anywhere,) * 4,
        scratch_shapes=[
            pltpu.VMEM((5, 288, 128), F32),
            pltpu.VMEM((5, 256, 128), F32),
            pltpu.VMEM((256, 128), F32),
            pltpu.VMEM((2, 2, 5, 16, 128), F32),
            pltpu.VMEM((2, 16, 128), F32),
            pltpu.VMEM((2, 2, 6, 16, 128), F32),
            pltpu.VMEM((2, 2, 6, 16, 128), F32),
            pltpu.VMEM((4, 8, 128), F32),
            pltpu.VMEM((4, 8, 128), F32),
            pltpu.VMEM((4, 4, 16, 128), F32),
            pltpu.VMEM((4, 256, 128), F32),
            pltpu.VMEM((8, 128), jnp.int32),
            pltpu.SMEM((8, 128), jnp.int32),
            pltpu.VMEM((2, 128, 128), F32),
            pltpu.VMEM((8, 16, 128), F32),
            pltpu.VMEM((8, 16, 128), F32),
            pltpu.VMEM((2, 32, 8, 128), F32),
            pltpu.VMEM((32, 8, 128), F32),
            pltpu.VMEM((32, 8, 128), F32),
            pltpu.VMEM((5, 34, 8, 128), F32),
            pltpu.VMEM((5, 34, 8, 128), F32),
            pltpu.VMEM((32, 8, 128), F32),
            pltpu.VMEM((32, 8, 128), F32),
            pltpu.VMEM((32, 8, 128), F32),
            pltpu.VMEM((64, 128), F32),
            pltpu.VMEM((4, 16, 128), F32),
            pltpu.VMEM((256, 128), F32),
            pltpu.VMEM((32, 8, 128), F32),
            pltpu.VMEM((32, 10, 128), F32),
            pltpu.VMEM((1, 32), jnp.int32),
            pltpu.SMEM((1,), jnp.int32),
            pltpu.SemaphoreType.DMA((20,)),
            pltpu.SemaphoreType.DMA((20,)),
            pltpu.SemaphoreType.DMA((20,)),
            pltpu.SemaphoreType.DMA,
            pltpu.SemaphoreType.REGULAR,
        ],
        compiler_params=pltpu.CompilerParams(
            collective_id=0, has_side_effects=True, vmem_limit_bytes=60 * 2**20
        ),
        name="reactive_step",
    )(
        coarse_state.reshape(5, 256, 128),
        fine_state.reshape(5, 32, 1024),
        coarse_rate.reshape(256, 128),
        fine_rate.reshape(32, 1024),
        parents,
        burn_steps,
    )
    coarse_new, fine_new = pl.pallas_call(
        place,
        out_shape=(
            jax.ShapeDtypeStruct((5, 256, 128), F32),
            jax.ShapeDtypeStruct((5, 32, 1024), F32),
        ),
        in_specs=[anywhere] * 4,
        out_specs=(anywhere,) * 2,
        scratch_shapes=[
            pltpu.VMEM((5, 256, 128), F32),
            pltpu.VMEM((32, 16, 128), F32),
            pltpu.VMEM((5, 32, 1024), F32),
            pltpu.SMEM((8, 128), jnp.int32),
            pltpu.SemaphoreType.DMA((9,)),
        ],
        compiler_params=pltpu.CompilerParams(vmem_limit_bytes=60 * 2**20),
        name="place",
    )(stepped, means, fine_mid, table)
    return coarse_new.reshape(5, 16, 16, 128), fine_new.reshape(1, 5, 32, 1024)


def solution(mesh):
    in_specs = (
        P(None, "region", "inner", None),
        P(("region", "inner"), None, None, None),
        P("region", "inner", None),
        P(("region", "inner"), None, None),
        P("region", None),
        P(("region", "inner")),
    )
    out_specs = (P(None, "region", "inner", None), P(("region", "inner"), None, None, None))
    return jax.shard_map(per_device, mesh=mesh, in_specs=in_specs, out_specs=out_specs, check_vma=False)
```

```python
import functools

import jax
import jax.numpy as jnp
from jax import lax
from jax.experimental import pallas as pl
from jax.experimental.pallas import tpu as pltpu
from jax.sharding import PartitionSpec as P

MESH = pl.DeviceIdType.MESH
F32 = jnp.float32
ADV = (0.5, -0.3, 0.2)
KEEP = 0.1
NB = 0.15
BURN_MAX = 8
REGIONS = 4
INNER = 32


def hops(offset):
    z, y = offset // 8, offset // 2 % 4
    return min(z, 4 - z) + min(y, 4 - y)


FAR_FIRST = sorted(range(1, INNER), key=hops, reverse=True)


def iota(shape, axis):
    return lax.broadcasted_iota(jnp.int32, shape, axis)


def lanes(q, shift):
    return pltpu.roll(q, shift % 128, 1)


def rows(q, shift):
    return pltpu.roll(q, shift % q.shape[0], 0)


def hydro(c, xm, xp, yd, yu, zd, zu):
    p, u, v, w, f = c
    sx, mx = xm[0] + xm[1], xp[0] - xp[1]
    sy, my = yd(p + v), yu(p - v)
    sz, mz = zd(p + w), zu(p - w)
    hp = (sx + mx) + (sy + my) + (sz + mz)
    hu = (sx - mx) + (yd(u) + yu(u)) + (zd(u) + zu(u))
    hv = (xm[2] + xp[2]) + (sy - my) + (zd(v) + zu(v))
    hw = (xm[3] + xp[3]) + (yd(w) + yu(w)) + (sz - mz)
    hf = (
        ((1 + ADV[0]) * xm[4] + (1 - ADV[0]) * xp[4])
        + ((1 + ADV[1]) * yd(f) + (1 - ADV[1]) * yu(f))
        + ((1 + ADV[2]) * zd(f) + (1 - ADV[2]) * zu(f))
    )
    return [KEEP * a + NB * b for a, b in zip(c, (hp, hu, hv, hw, hf))]


def take(q, index):
    return jnp.take_along_axis(q, index, axis=1, mode="promise_in_bounds")


def coarse_shifts(shape):
    row, lane = iota(shape, 0), iota(shape, 1)
    zd = lambda q: jnp.where(lane == 0, 0.0, lanes(q, 1))
    zu = lambda q: jnp.where(lane == 127, 0.0, lanes(q, -1))
    yd = lambda q: jnp.where(row == 0, 0.0, rows(q, 1))
    yu = lambda q: jnp.where(row == shape[0] - 1, 0.0, rows(q, -1))
    return yd, yu, zd, zu


def fine_shifts():
    sub, lane = iota((8, 128), 0), iota((8, 128), 1)
    z = lane % 32

    def yd(q):
        t = lanes(q, 32)
        t = jnp.where(lane < 32, rows(t, 1), t)
        return jnp.where((lane < 32) & (sub == 0), 0.0, t)

    def yu(q):
        t = lanes(q, -32)
        t = jnp.where(lane >= 96, rows(t, -1), t)
        return jnp.where((lane >= 96) & (sub == 7), 0.0, t)

    zd = lambda q: jnp.where(z == 0, 0.0, lanes(q, 1))
    zu = lambda q: jnp.where(z == 31, 0.0, lanes(q, -1))
    return yd, yu, zd, zu


def burn_once(p, f, rate):
    burned = f * pl.reciprocal(1.0 + 0.5 * rate * (1.0 + 0.5 * jnp.tanh(p)), approx=True)
    return p + 0.5 * (f - burned), burned


def face_values(p, n, t1, t2, f, axis, high):
    sign = -1.0 if high else 1.0
    return [NB * (p + sign * n), NB * t1, NB * t2, NB * (1 + sign * ADV[axis]) * f]


def ghost_step(near, far, own, dlo, dhi, rate, axis, high):
    n, r = (1, 2) if axis == 0 else (2, 1)
    row, lane = iota((16, 128), 0), iota((16, 128), 1)
    an, ar, az = ADV[axis], ADV[1 - axis], ADV[2]
    minus, plus = (own, far) if high else (far, own)
    p, w, f = near[0], near[3], near[4]

    def rd(q, d):
        return jnp.where(row == 0, d, rows(q, 1))

    def ru(q, d):
        return jnp.where(row == 15, d, rows(q, -1))

    zd = lambda q: jnp.where(lane == 0, 0.0, lanes(q, 1))
    zu = lambda q: jnp.where(lane == 127, 0.0, lanes(q, -1))
    sn, mn = minus[0] + minus[n], plus[0] - plus[n]
    sr, mr = rd(p + near[r], dlo[0] + dlo[r]), ru(p - near[r], dhi[0] - dhi[r])
    sz, mz = zd(p + w), zu(p - w)
    hp = (sn + mn) + (sr + mr) + (sz + mz)
    hn = (sn - mn) + (rd(near[n], dlo[n]) + ru(near[n], dhi[n])) + (zd(near[n]) + zu(near[n]))
    hr = (minus[r] + plus[r]) + (sr - mr) + (zd(near[r]) + zu(near[r]))
    hw = (minus[3] + plus[3]) + (rd(w, dlo[3]) + ru(w, dhi[3])) + (sz - mz)
    hf = (
        ((1 + an) * minus[4] + (1 - an) * plus[4])
        + ((1 + ar) * rd(f, dlo[4]) + (1 - ar) * ru(f, dhi[4]))
        + ((1 + az) * zd(f) + (1 - az) * zu(f))
    )
    pressure, normal, tangent, across, fuel = (
        KEEP * a + NB * b for a, b in zip((p, near[n], near[r], w, f), (hp, hn, hr, hw, hf))
    )
    pressure, fuel = burn_once(pressure, fuel, rate)
    return face_values(pressure, normal, tangent, across, fuel, axis, high)


def kernel(
    coarse, fine, crate, frate, parents, steps, h, fine_out, r4, covers,
    c, cr, xh, xr, ys, yh, ds, dr, fv, zv, table, keys, p1, r1a, r1b, p2, r2a, r2b, f0, f1, fa, fb, fr, gt, ey,
    mb, r3, p4, pv, sv, ssem, rsem, lsem, tsem, ready,
):
    r1, r2 = (r1a, r1b), (r2a, r2b)
    region, me = lax.axis_index("region"), lax.axis_index("inner")
    up, down = lax.rem(region + 1, REGIONS), lax.rem(region + REGIONS - 1, REGIONS)
    right, left = lax.rem(me + 1, INNER), lax.rem(me + INNER - 1, INNER)
    plane, mine = (me // 8) * 8, lax.rem(me, 8)
    sub, lane = iota((8, 128), 0), iota((8, 128), 1)

    barrier = pltpu.get_barrier_semaphore()
    has_x = [region > 0, region < REGIONS - 1]
    has_y = [me > 0, me < INNER - 1]
    side_x, side_y = (down, up), (left, right)
    columns = [(region, lax.rem(me + 8 * k, INNER)) for k in (2, 1, 3)]
    greeted = [(has_x[e] & has_y[d], (side_x[e], side_y[d])) for e in range(2) for d in range(2)]
    for e in range(2):
        greeted.append((has_x[e], (side_x[e], me)))
        greeted.append((has_y[e] & (mine == 7 * e), (region, side_y[e])))
    for k in (4, 3, 5, 2, 6, 1, 7):
        greeted.append((True, (region, plane + lax.rem(mine + k, 8))))
    greeted = greeted + [(True, other) for other in columns]

    def hello(to):
        pl.semaphore_signal(barrier, inc=1, device_id=to, device_id_type=MESH)

    expected = 0
    for exists, to in greeted:
        if exists is True:
            hello(to)
            expected = expected + 1
        else:
            pl.when(exists)(functools.partial(hello, to))
            expected = expected + jnp.where(exists, 1, 0)
    loads = [
        pltpu.make_async_copy(coarse, c.at[:, pl.ds(16, 256)], lsem.at[0]),
        pltpu.make_async_copy(crate, cr, lsem.at[1]),
        pltpu.make_async_copy(parents, pv, lsem.at[18]),
        pltpu.make_async_copy(steps, sv, lsem.at[19]),
    ]
    for j in range(8):
        cut = pl.ds(j * 128, 128)
        loads.append(pltpu.make_async_copy(fine.at[:, :, cut], f0.at[:, pl.ds(1, 32), j], lsem.at[2 + j]))
        loads.append(pltpu.make_async_copy(frate.at[:, cut], fr.at[:, j], lsem.at[10 + j]))
    for load in loads[:3]:
        load.start()

    zero = jnp.zeros((8, 128), F32)
    for i in range(5):
        c[i, 0:16] = jnp.zeros((16, 128), F32)
        c[i, 272:288] = jnp.zeros((16, 128), F32)
        for a in (0, 33):
            f0[i, a] = zero
            f1[i, a] = zero
    loads[0].wait()
    loads[1].wait()
    for side, (near, far) in enumerate(((15, 14), (0, 1))):
        for half in range(2):
            dst = pl.ds(half * 8, 8)
            for i in range(5):
                ys[side, 0, i, dst] = c[i, pl.ds(16 + half * 128 + near, 8, stride=16)]
                ys[side, 1, i, dst] = c[i, pl.ds(16 + half * 128 + far, 8, stride=16)]
            ys[side, 1, 5, dst] = cr[pl.ds(half * 128 + near, 8, stride=16)]
    for n, at in enumerate((255, 240, 15, 0)):
        for i in range(5):
            ds[n, i : i + 1] = c[i, 16 + at : 17 + at]
        ds[n, 5:8] = jnp.zeros((3, 128), F32)

    for e in range(2):

        @pl.when(~has_x[e])
        def _():
            xh[e] = jnp.zeros(xh.shape[1:], F32)
            xr[e] = jnp.zeros(xr.shape[1:], F32)

        @pl.when(~has_y[e])
        def _():
            yh[e] = jnp.zeros(yh.shape[1:], F32)

        for d in range(2):

            @pl.when(~(has_x[e] & has_y[d]))
            def _():
                dr[2 * e + d] = jnp.zeros((8, 128), F32)

    pl.semaphore_wait(barrier, expected)

    def remote(src, dst, n, to):
        return pltpu.make_async_remote_copy(
            src_ref=src, dst_ref=dst, send_sem=ssem.at[n], recv_sem=rsem.at[n], device_id=to, device_id_type=MESH
        )

    near, far = [], []
    for e in range(2):
        o = 1 - e
        near.append((remote(c.at[:, pl.ds(16 + 240 * o, 16)], xh.at[e, 0], e, (side_x[o], me)), has_x[o], has_x[e]))
        near.append(
            (
                remote(ys.at[e, 0, pl.ds(0, 5)], yh.at[e, 0, pl.ds(0, 5)], 2 + e, (region, side_y[o])),
                has_y[o],
                has_y[e],
            )
        )
        far.append((remote(cr.at[pl.ds(240 * o, 16)], xr.at[e], 8 + e, (side_x[o], me)), has_x[o], has_x[e]))
        far.append(
            (remote(c.at[:, pl.ds(32 + 208 * o, 16)], xh.at[e, 1], 16 + e, (side_x[o], me)), has_x[o], has_x[e])
        )
        far.append((remote(ys.at[e, 1], yh.at[e, 1], 18 + e, (region, side_y[o])), has_y[o], has_y[e]))
    for n in range(4):
        e, d = n // 2, n % 2
        far.insert(
            n,
            (
                remote(ds.at[n], dr.at[n], 4 + n, (side_x[1 - e], side_y[1 - d])),
                has_x[1 - e] & has_y[1 - d],
                has_x[e] & has_y[d],
            ),
        )
    for halo, sends, _ in near + far:
        pl.when(sends)(halo.start)
    for load in loads[3:]:
        load.start()
    for other in columns:
        pl.semaphore_signal(ready, inc=1, device_id=other, device_id_type=MESH)

    loads[2].wait()
    block_row = jnp.broadcast_to(pv[...], (32, 32))
    ri, ci = iota((32, 32), 0), iota((32, 32), 1)
    block = jnp.sum(jnp.where(ri == ci, block_row, 0), axis=1, keepdims=True)
    owner = block >> 3
    slot = jnp.sum(
        jnp.where((jnp.broadcast_to(owner, (32, 32)) == (block_row >> 3)) & (ci < ri), 1, 0),
        axis=1,
        keepdims=True,
    )
    key = jnp.broadcast_to(owner * 2 + slot, (32, 128))
    ri, ci = iota((32, 128), 0), iota((32, 128), 1)
    layer = jnp.broadcast_to((block & 7) + 1, (32, 128))
    key_row = jnp.sum(jnp.where(ri == ci, key, 0), axis=0, keepdims=True)
    patch_row = jnp.sum(jnp.where(key == ci, ri, 0), axis=0, keepdims=True)
    layer_row = jnp.sum(jnp.where(key == ci, layer, 0), axis=0, keepdims=True) - 1
    table[...] = jnp.where(
        sub == 0,
        jnp.broadcast_to(key_row, (8, 128)),
        jnp.where(sub == 1, jnp.broadcast_to(patch_row, (8, 128)), jnp.broadcast_to(layer_row, (8, 128))),
    )
    look = pltpu.make_async_copy(table, keys, tsem)
    look.start()

    shifts = coarse_shifts((16, 128))

    def coarse_plane(x, carry):
        at = pl.multiple_of(x * 16, 16)
        cells = [c[i, pl.ds(at + 16, 16)] for i in range(5)]
        below = [c[i, pl.ds(at, 16)] for i in range(5)]
        above = [c[i, pl.ds(at + 32, 16)] for i in range(5)]
        for i, q in enumerate(hydro(cells, below, above, *shifts)):
            h[i, pl.ds(at, 16)] = q
        return carry

    lax.fori_loop(0, 16, coarse_plane, 0, unroll=4)

    look.wait()
    slots = [keys[2, 2 * me], keys[2, 2 * me + 1]]
    for s in range(2):
        covers[8 * s : 8 * s + 8] = jnp.where(lane // 16 == slots[s], 1, 0)
    my_key = keys[0, me]

    side = lane % 2
    code = ((lane % 64) // 4) * 4 + (lane // 64) * 2 + (lane % 4) // 2
    picks = [lax.rem(jnp.where(side == 0, 16 * s + 127, 16 * s + 16) + 128, 128) for s in slots]
    cuts = [16 * jnp.maximum(s, 0) + lane % 16 for s in slots]
    inside = [
        jnp.where(((side == 0) & (s == 0)) | ((side == 1) & (s == 7)), 0.0, 1.0) for s in slots
    ]

    def z_values(src, base):
        low = iota((16, 128), 1) % 16 == 15

        def body(x, carry):
            at = pl.multiple_of(x * 16, 16)
            p, u, v, w, f = (src[i, pl.ds(at + base, 16)] for i in range(5))
            zv[0, pl.ds(at, 16)] = NB * (p + jnp.where(low, w, -w))
            zv[1, pl.ds(at, 16)] = NB * u
            zv[2, pl.ds(at, 16)] = NB * v
            zv[3, pl.ds(at, 16)] = f * jnp.where(low, NB * (1 + ADV[2]), NB * (1 - ADV[2]))
            return carry

        lax.fori_loop(0, 16, body, 0, unroll=8)

    def z_tiles():
        def body(x, tiles):
            tiles = list(tiles)
            for v in range(4):
                for odd in range(2):
                    q = zv[v, pl.ds(x * 16 + odd, 8, stride=2)]
                    here = code == x * 4 + (v % 2) * 2 + odd
                    for s in range(2):
                        tiles[s * 2 + v // 2] = jnp.where(here, take(q, picks[s]), tiles[s * 2 + v // 2])
            return tuple(tiles)

        tiles = lax.fori_loop(0, 16, body, (zero,) * 4, unroll=16)
        return [[tiles[s * 2 + w] * inside[s] for w in range(2)] for s in range(2)]

    def xy_tile(face, s):
        tile = zero
        for v in range(4):
            for odd in range(2):
                pos = v * 32 + odd * 16
                q = fv[face, v, pl.ds(odd, 8, stride=2)]
                tile = jnp.where(lane // 16 == pos // 16, take(q, cuts[s]), tile)
        return tile

    def put_tile(t, s, face, tile):
        p1[t, pl.ds(s * 6 + face, 8, stride=16)] = tile

    def get_tile(t, s, face):
        return p1[t, pl.ds(s * 6 + face, 8, stride=16)]

    z_values(c, 16)
    for s, pair in enumerate(z_tiles()):
        for w, tile in enumerate(pair):
            put_tile(0, s, 4 + w, tile)

    for halo, _, arrives in near:
        pl.when(arrives)(halo.wait_recv)
    mx = [jnp.where(exists, 1.0, 0.0) for exists in has_x]
    my = [jnp.where(exists, 1.0, 0.0) for exists in has_y]

    def near_x(e):
        return [xh[e, 0, i] for i in range(5)]

    def near_y(e):
        return [yh[e, 0, i] for i in range(5)]

    for e in range(2):
        p, u, v, w, f = near_x(e)
        for i, q in enumerate(face_values(p, u, v, w, f, 0, e == 1)):
            fv[e, i] = mx[e] * q
        p, u, v, w, f = near_y(e)
        for i, q in enumerate(face_values(p, v, u, w, f, 1, e == 1)):
            fv[2 + e, i] = my[e] * q
    for s in range(2):
        for face in range(4):
            put_tile(0, s, face, xy_tile(face, s))

    def send_pieces(t):
        r1[t][mine, 0:12] = p1[t, pl.ds(mine * 16, 12)]

        for k in (4, 3, 5, 2, 6, 1, 7):
            to = lax.rem(mine + k, 8)
            remote(
                p1.at[t, pl.ds(to * 16, 12)], r1[t].at[mine, pl.ds(0, 12)], 10 + t, (region, plane + to)
            ).start()

    send_pieces(0)

    def add_face(ref, cut, face, n, t1, high):
        e0, e1, e2, e3 = (fv[face, v, pl.ds(8 * cut[0], 8)] for v in range(4))
        at = cut[1]
        ref[0, at] = ref[0, at] + e0
        ref[n, at] = ref[n, at] - e0 if high else ref[n, at] + e0
        ref[t1, at] = ref[t1, at] + e1
        ref[3, at] = ref[3, at] + e2
        ref[4, at] = ref[4, at] + e3

    for half in range(2):
        add_face(h, (half, pl.ds(half * 8, 8)), 0, 1, 2, False)
        add_face(h, (half, pl.ds(240 + half * 8, 8)), 1, 1, 2, True)
        add_face(h, (half, pl.ds(half * 128, 8, stride=16)), 2, 2, 1, False)
        add_face(h, (half, pl.ds(half * 128 + 15, 8, stride=16)), 3, 2, 1, True)

    def coarse_burn(x, carry):
        at = pl.multiple_of(x * 64, 64)
        p, f = burn_once(h[0, pl.ds(at, 64)], h[4, pl.ds(at, 64)], cr[pl.ds(at, 64)])
        h[0, pl.ds(at, 64)] = p
        h[4, pl.ds(at, 64)] = f
        return carry

    lax.fori_loop(0, 4, coarse_burn, 0, unroll=4)

    z_values(h, 0)
    for s, pair in enumerate(z_tiles()):
        for w, tile in enumerate(pair):
            put_tile(1, s, 4 + w, 0.5 * (get_tile(0, s, 4 + w) + tile))
    for halo, _, arrives in far:
        pl.when(arrives)(halo.wait_recv)

    def own_rows(axis, e):
        if axis == 0:
            return [c[i, pl.ds(16 + 240 * e, 16)] for i in range(5)]
        return [
            jnp.concatenate([c[i, pl.ds(16 + 128 * b + 15 * e, 8, stride=16)] for b in range(2)], axis=0)
            for i in range(5)
        ]

    def corner(n, scale):
        return [dr[n, i : i + 1] * scale for i in range(5)]

    for e in range(2):
        values = ghost_step(
            near_x(e), [xh[e, 1, i] for i in range(5)], own_rows(0, e), corner(2 * e, my[0]), corner(2 * e + 1, my[1]), xr[e], 0, e == 1
        )
        for i, q in enumerate(values):
            fv[e, i] = mx[e] * q
        values = ghost_step(
            near_y(e), [yh[e, 1, i] for i in range(5)], own_rows(1, e),
            corner(e, mx[0]), corner(2 + e, mx[1]), yh[e, 1, 5], 1, e == 1,
        )
        for i, q in enumerate(values):
            fv[2 + e, i] = my[e] * q
    for s in range(2):
        for face in range(4):
            put_tile(1, s, face, 0.5 * (get_tile(0, s, face) + xy_tile(face, s)))
    send_pieces(1)

    for load in loads[3:]:
        load.wait()
    count = sv[0]
    counted = jnp.broadcast_to(count, (8, 128)).astype(F32)
    span = 0.25 / counted
    fine_shift = fine_shifts()

    def rates(x, carry):
        q = span * fr[x]
        fa[x] = 1.0 + q
        fb[x] = 0.5 * q
        return carry

    lax.fori_loop(0, 32, rates, 0, unroll=8)

    def fine_hydro(src, dst):
        def body(x, carry):
            cells = [src[i, x + 1] for i in range(5)]
            below = [src[i, x] for i in range(5)]
            above = [src[i, x + 2] for i in range(5)]
            for i, q in enumerate(hydro(cells, below, above, *fine_shift)):
                dst[i, x + 1] = q
            return carry

        lax.fori_loop(0, 32, body, 0, unroll=16)

    fine_hydro(f0, f1)

    def wait_all(ref, sem):
        pltpu.make_async_copy(ref, ref, sem).wait()

    def send_faces(t):
        wait_all(r1[t].at[pl.ds(0, 7), pl.ds(0, 12)], rsem.at[10 + t])

        def piece(key):
            pair = r1[t][(key & 15) >> 1]
            return jnp.where((key & 1) == 0, pair[0:6], pair[6:12])

        r2[t][me, 0:6] = piece(my_key)

        for k in FAR_FIRST:
            to = lax.rem(me + k, INNER)
            p2[t, to, 0:6] = piece(keys[0, to])
        for k in FAR_FIRST:
            to = lax.rem(me + k, INNER)
            remote(p2.at[t, to, pl.ds(0, 6)], r2[t].at[me, pl.ds(0, 6)], 12 + t, (region, to)).start()

    pl.semaphore_wait(ready, len(columns))
    send_faces(0)
    send_faces(1)
    stores = []

    q4, z = lane // 32, lane % 32
    edge_y = jnp.where((lane < 32) & (sub == 0) | (lane >= 96) & (sub == 7), 1.0, 0.0)
    sign_y = jnp.where(lane < 64, edge_y, -edge_y)
    edge_z = jnp.where((z == 0) | (z == 31), 1.0, 0.0)
    sign_z = jnp.where(z < 16, edge_z, -edge_z)
    pick_x = (q4 // 2) * 16 + z // 2
    pick_z = (q4 // 2) * 2 + z // 16

    def add_ghosts(t, dst):
        wait_all(r2[t].at[pl.ds(0, INNER - 1), pl.ds(0, 6)], rsem.at[12 + t])
        start = (my_key >> 4) * 8
        for k in range(8):
            gt[pl.ds(k * 8, 8)] = r2[t][start + k]
        tiles = [gt[pl.ds(face, 8, stride=8)] for face in range(6)]
        for face, x in ((0, 1), (1, 32)):
            e = [take(tiles[face], pick_x + 32 * v) for v in range(4)]
            dst[0, x] = dst[0, x] + e[0]
            dst[1, x] = dst[1, x] + e[0] if face == 0 else dst[1, x] - e[0]
            dst[2, x] = dst[2, x] + e[1]
            dst[3, x] = dst[3, x] + e[2]
            dst[4, x] = dst[4, x] + e[3]
        for v in range(4):
            for odd in range(2):
                pick = v * 32 + odd * 16 + z // 2
                ey[v, pl.ds(odd, 8, stride=2)] = jnp.where(lane < 64, take(tiles[2], pick), take(tiles[3], pick))

        def body(x, carry):
            y = [jnp.broadcast_to(ey[v, pl.ds(x, 1)], (8, 128)) for v in range(4)]
            zz = [take(tiles[4 + v // 2], pick_z + ((v % 2) * 64 + x * 4)) for v in range(4)]
            add = [
                edge_y * y[0] + edge_z * zz[0],
                edge_y * y[1] + edge_z * zz[1],
                sign_y * y[0] + edge_z * zz[2],
                edge_y * y[2] + sign_z * zz[0],
                edge_y * y[3] + edge_z * zz[3],
            ]
            for i in range(5):
                dst[i, 2 * x + 1] = dst[i, 2 * x + 1] + add[i]
                dst[i, 2 * x + 2] = dst[i, 2 * x + 2] + add[i]
            return carry

        lax.fori_loop(0, 16, body, 0, unroll=16)

    live = [jnp.where(turn < count, 1.0, 0.0) for turn in range(BURN_MAX)]
    group = 16

    def burn(dst, at):
        p = [dst[0, at + i + 1] for i in range(group)]
        f = [dst[4, at + i + 1] for i in range(group)]
        for turn in range(BURN_MAX):
            for i in range(group):
                r = pl.reciprocal(fa[at + i] + fb[at + i] * jnp.tanh(p[i]), approx=True)
                d = live[turn] * (f[i] - f[i] * r)
                f[i] = f[i] - d
                p[i] = p[i] + 0.5 * d
        for i in range(group):
            dst[0, at + i + 1] = p[i]
            dst[4, at + i + 1] = f[i]

    add_ghosts(0, f1)
    for at in range(0, 32, group):
        burn(f1, at)
    fine_hydro(f1, f0)
    add_ghosts(1, f0)
    pick_m = ((lane % 32) // 16) * 64 + 2 * (lane % 16)

    def means(a):
        for i in range(5):
            tile = zero
            for g in range(4):
                at = a * 8 + 2 * g
                q = f0[i, at + 1] + f0[i, at + 2]
                q = q + lanes(q, -1)
                q = q + lanes(q, -32)
                tile = jnp.where(q4 == g, take(q, pick_m), tile)
            mb[pl.ds(a * 64 + i, 8, stride=8)] = 0.125 * tile

    def send_mean(to):
        remote(mb.at[pl.ds(to * 8, 5)], r3.at[me, pl.ds(0, 5)], 14, (region, to)).start()

    for half in range(2):
        burn(f0, 16 * half)
        means(2 * half)
        means(2 * half + 1)
        for k in range(8, 24):
            to = 16 * half + lax.rem(me + k, 16)
            if k != 16:
                send_mean(to)
            else:
                pl.when(me != to)(functools.partial(send_mean, to))
    r3[me, 0:5] = mb[pl.ds(me * 8, 5)]

    wait_all(r3.at[pl.ds(0, 31), pl.ds(0, 5)], rsem.at[14])

    def pick_pair(to):
        for s in range(2):
            p4[to, 5 * s : 5 * s + 5] = r3[keys[1, 2 * to + s], 0:5]

    pick_pair(me)
    r4[me, 0:10] = p4[me]

    for k in FAR_FIRST:
        to = lax.rem(me + k, INNER)
        pick_pair(to)
    for k in FAR_FIRST:
        to = lax.rem(me + k, INNER)
        remote(p4.at[to], r4.at[me, pl.ds(0, 10)], 15, (region, to)).start()

    for j in range(8):
        stores.append(
            pltpu.make_async_copy(
                f0.at[:, pl.ds(1, 32), j], fine_out.at[:, :, pl.ds(j * 128, 128)], lsem.at[2 + j]
            )
        )
        stores[-1].start()

    for halo, sends, _ in near + far:
        pl.when(sends)(halo.wait_send)
    for t in range(2):
        wait_all(r1[t].at[pl.ds(0, 7), pl.ds(0, 12)], ssem.at[10 + t])
        wait_all(r2[t].at[pl.ds(0, INNER - 1), pl.ds(0, 6)], ssem.at[12 + t])
    wait_all(r3.at[pl.ds(0, 31), pl.ds(0, 5)], ssem.at[14])
    wait_all(p4.at[pl.ds(0, 31)], ssem.at[15])
    for store in stores:
        store.wait()
    wait_all(r4.at[pl.ds(0, 31), pl.ds(0, 10)], rsem.at[15])


def place(stepped, means, fine, covers, coarse_out, fine_out, h, sem):
    stores = [pltpu.make_async_copy(fine, fine_out, sem.at[5])]
    stores[0].start()
    lane = iota((8, 128), 1)
    here = [covers[8 * s : 8 * s + 8] > 0 for s in range(2)]
    rows_of = means.reshape(512, 128)
    for i in range(5):

        def body(a, carry):
            tiles = [rows_of[pl.ds(a * 128 + s * 5 + i, 8, stride=16)] for s in range(2)]
            for g in range(4):
                for odd in range(2):
                    at = pl.ds((a * 4 + g) * 16 + odd, 8, stride=2)
                    q = stepped[i, at]
                    for s in range(2):
                        q = jnp.where(here[s], take(tiles[s], lane % 16 + (g * 32 + odd * 16)), q)
                    h[i, at] = q
            return carry

        lax.fori_loop(0, 4, body, 0, unroll=4)
        stores.append(pltpu.make_async_copy(h.at[i], coarse_out.at[i], sem.at[i]))
        stores[-1].start()
    for store in stores:
        store.wait()


def per_device(coarse_state, fine_state, coarse_rate, fine_rate, parents, burn_steps):
    vmem, hbm = pl.BlockSpec(memory_space=pltpu.VMEM), pl.BlockSpec(memory_space=pltpu.HBM)
    stepped, fine_mid, means, covers = pl.pallas_call(
        kernel,
        out_shape=(
            jax.ShapeDtypeStruct((5, 256, 128), F32),
            jax.ShapeDtypeStruct((5, 32, 1024), F32),
            jax.ShapeDtypeStruct((32, 16, 128), F32),
            jax.ShapeDtypeStruct((16, 128), jnp.int32),
        ),
        in_specs=[hbm] * 6,
        out_specs=(vmem,) * 4,
        scratch_shapes=[
            pltpu.VMEM((5, 288, 128), F32),
            pltpu.VMEM((256, 128), F32),
            pltpu.VMEM((2, 2, 5, 16, 128), F32),
            pltpu.VMEM((2, 16, 128), F32),
            pltpu.VMEM((2, 2, 6, 16, 128), F32),
            pltpu.VMEM((2, 2, 6, 16, 128), F32),
            pltpu.VMEM((4, 8, 128), F32),
            pltpu.VMEM((4, 8, 128), F32),
            pltpu.VMEM((4, 4, 16, 128), F32),
            pltpu.VMEM((4, 256, 128), F32),
            pltpu.VMEM((8, 128), jnp.int32),
            pltpu.SMEM((8, 128), jnp.int32),
            pltpu.VMEM((2, 128, 128), F32),
            pltpu.VMEM((8, 16, 128), F32),
            pltpu.VMEM((8, 16, 128), F32),
            pltpu.VMEM((2, 32, 8, 128), F32),
            pltpu.VMEM((32, 8, 128), F32),
            pltpu.VMEM((32, 8, 128), F32),
            pltpu.VMEM((5, 34, 8, 128), F32),
            pltpu.VMEM((5, 34, 8, 128), F32),
            pltpu.VMEM((32, 8, 128), F32),
            pltpu.VMEM((32, 8, 128), F32),
            pltpu.VMEM((32, 8, 128), F32),
            pltpu.VMEM((64, 128), F32),
            pltpu.VMEM((4, 16, 128), F32),
            pltpu.VMEM((256, 128), F32),
            pltpu.VMEM((32, 8, 128), F32),
            pltpu.VMEM((32, 10, 128), F32),
            pltpu.VMEM((1, 32), jnp.int32),
            pltpu.SMEM((1,), jnp.int32),
            pltpu.SemaphoreType.DMA((20,)),
            pltpu.SemaphoreType.DMA((20,)),
            pltpu.SemaphoreType.DMA((20,)),
            pltpu.SemaphoreType.DMA,
            pltpu.SemaphoreType.REGULAR,
        ],
        compiler_params=pltpu.CompilerParams(
            collective_id=0, has_side_effects=True, vmem_limit_bytes=24 * 2**20
        ),
        name="reactive_step",
    )(
        *(
            pltpu.with_memory_space_constraint(x, pltpu.HBM)
            for x in (
                coarse_state.reshape(5, 256, 128),
                fine_state.reshape(5, 32, 1024),
                coarse_rate.reshape(256, 128),
                fine_rate.reshape(32, 1024),
                parents,
            )
        ),
        burn_steps,
    )
    coarse_new, fine_new = pl.pallas_call(
        place,
        out_shape=(
            jax.ShapeDtypeStruct((5, 256, 128), F32),
            jax.ShapeDtypeStruct((5, 32, 1024), F32),
        ),
        in_specs=[vmem] * 4,
        out_specs=(hbm,) * 2,
        scratch_shapes=[
            pltpu.VMEM((5, 256, 128), F32),
            pltpu.SemaphoreType.DMA((6,)),
        ],
        compiler_params=pltpu.CompilerParams(vmem_limit_bytes=24 * 2**20),
        name="place",
    )(stepped, means, fine_mid, covers)
    return coarse_new.reshape(5, 16, 16, 128), fine_new.reshape(1, 5, 32, 1024)


def solution(mesh):
    in_specs = (
        P(None, "region", "inner", None),
        P(("region", "inner"), None, None, None),
        P("region", "inner", None),
        P(("region", "inner"), None, None),
        P("region", None),
        P(("region", "inner")),
    )
    out_specs = (P(None, "region", "inner", None), P(("region", "inner"), None, None, None))
    return jax.shard_map(per_device, mesh=mesh, in_specs=in_specs, out_specs=out_specs, check_vma=False)
```

```python
import functools

import jax
import jax.numpy as jnp
from jax import lax
from jax.experimental import pallas as pl
from jax.experimental.pallas import tpu as pltpu
from jax.sharding import PartitionSpec as P

MESH = pl.DeviceIdType.MESH
F32 = jnp.float32
ADV = (0.5, -0.3, 0.2)
KEEP = 0.1
NB = 0.15
BURN_MAX = 8
REGIONS = 4
INNER = 32


def hops(offset):
    z, y = offset // 8, offset // 2 % 4
    return min(z, 4 - z) + min(y, 4 - y)


FAR_FIRST = sorted(range(1, INNER), key=hops, reverse=True)


def iota(shape, axis):
    return lax.broadcasted_iota(jnp.int32, shape, axis)


def lanes(q, shift):
    return pltpu.roll(q, shift % 128, 1)


def rows(q, shift):
    return pltpu.roll(q, shift % q.shape[0], 0)


def hydro(c, xm, xp, yd, yu, zd, zu):
    p, u, v, w, f = c
    sx, mx = xm[0] + xm[1], xp[0] - xp[1]
    sy, my = yd(p + v), yu(p - v)
    sz, mz = zd(p + w), zu(p - w)
    hp = (sx + mx) + (sy + my) + (sz + mz)
    hu = (sx - mx) + (yd(u) + yu(u)) + (zd(u) + zu(u))
    hv = (xm[2] + xp[2]) + (sy - my) + (zd(v) + zu(v))
    hw = (xm[3] + xp[3]) + (yd(w) + yu(w)) + (sz - mz)
    hf = (
        ((1 + ADV[0]) * xm[4] + (1 - ADV[0]) * xp[4])
        + ((1 + ADV[1]) * yd(f) + (1 - ADV[1]) * yu(f))
        + ((1 + ADV[2]) * zd(f) + (1 - ADV[2]) * zu(f))
    )
    return [KEEP * a + NB * b for a, b in zip(c, (hp, hu, hv, hw, hf))]


def take(q, index):
    return jnp.take_along_axis(q, index, axis=1, mode="promise_in_bounds")


def coarse_shifts(shape):
    row, lane = iota(shape, 0), iota(shape, 1)
    zd = lambda q: jnp.where(lane == 0, 0.0, lanes(q, 1))
    zu = lambda q: jnp.where(lane == 127, 0.0, lanes(q, -1))
    yd = lambda q: jnp.where(row == 0, 0.0, rows(q, 1))
    yu = lambda q: jnp.where(row == shape[0] - 1, 0.0, rows(q, -1))
    return yd, yu, zd, zu


def fine_shifts():
    sub, lane = iota((8, 128), 0), iota((8, 128), 1)
    z = lane % 32

    def yd(q):
        t = lanes(q, 32)
        t = jnp.where(lane < 32, rows(t, 1), t)
        return jnp.where((lane < 32) & (sub == 0), 0.0, t)

    def yu(q):
        t = lanes(q, -32)
        t = jnp.where(lane >= 96, rows(t, -1), t)
        return jnp.where((lane >= 96) & (sub == 7), 0.0, t)

    zd = lambda q: jnp.where(z == 0, 0.0, lanes(q, 1))
    zu = lambda q: jnp.where(z == 31, 0.0, lanes(q, -1))
    return yd, yu, zd, zu


def burn_once(p, f, rate):
    burned = f * pl.reciprocal(1.0 + 0.5 * rate * (1.0 + 0.5 * jnp.tanh(p)), approx=True)
    return p + 0.5 * (f - burned), burned


def face_values(p, n, t1, t2, f, axis, high):
    sign = -1.0 if high else 1.0
    return [NB * (p + sign * n), NB * t1, NB * t2, NB * (1 + sign * ADV[axis]) * f]


def ghost_step(near, far, own, dlo, dhi, rate, axis, high):
    n, r = (1, 2) if axis == 0 else (2, 1)
    row, lane = iota((16, 128), 0), iota((16, 128), 1)
    an, ar, az = ADV[axis], ADV[1 - axis], ADV[2]
    minus, plus = (own, far) if high else (far, own)
    p, w, f = near[0], near[3], near[4]

    def rd(q, d):
        return jnp.where(row == 0, d, rows(q, 1))

    def ru(q, d):
        return jnp.where(row == 15, d, rows(q, -1))

    zd = lambda q: jnp.where(lane == 0, 0.0, lanes(q, 1))
    zu = lambda q: jnp.where(lane == 127, 0.0, lanes(q, -1))
    sn, mn = minus[0] + minus[n], plus[0] - plus[n]
    sr, mr = rd(p + near[r], dlo[0] + dlo[r]), ru(p - near[r], dhi[0] - dhi[r])
    sz, mz = zd(p + w), zu(p - w)
    hp = (sn + mn) + (sr + mr) + (sz + mz)
    hn = (sn - mn) + (rd(near[n], dlo[n]) + ru(near[n], dhi[n])) + (zd(near[n]) + zu(near[n]))
    hr = (minus[r] + plus[r]) + (sr - mr) + (zd(near[r]) + zu(near[r]))
    hw = (minus[3] + plus[3]) + (rd(w, dlo[3]) + ru(w, dhi[3])) + (sz - mz)
    hf = (
        ((1 + an) * minus[4] + (1 - an) * plus[4])
        + ((1 + ar) * rd(f, dlo[4]) + (1 - ar) * ru(f, dhi[4]))
        + ((1 + az) * zd(f) + (1 - az) * zu(f))
    )
    pressure, normal, tangent, across, fuel = (
        KEEP * a + NB * b for a, b in zip((p, near[n], near[r], w, f), (hp, hn, hr, hw, hf))
    )
    pressure, fuel = burn_once(pressure, fuel, rate)
    return face_values(pressure, normal, tangent, across, fuel, axis, high)


def kernel(
    coarse, fine, crate, frate, parents, steps, h, fine_out, r4, covers,
    c, cr, xh, xr, ys, yh, ds, dr, fv, zv, table, keys, p1, r1a, r1b, p2, r2a, r2b, f0, f1, fa, fb, fr, gt, ey,
    mb, r3, p4, pv, sv, ssem, rsem, lsem, tsem, ready,
):
    r1, r2 = (r1a, r1b), (r2a, r2b)
    region, me = lax.axis_index("region"), lax.axis_index("inner")
    up, down = lax.rem(region + 1, REGIONS), lax.rem(region + REGIONS - 1, REGIONS)
    right, left = lax.rem(me + 1, INNER), lax.rem(me + INNER - 1, INNER)
    plane, mine = (me // 8) * 8, lax.rem(me, 8)
    sub, lane = iota((8, 128), 0), iota((8, 128), 1)

    barrier = pltpu.get_barrier_semaphore()
    has_x = [region > 0, region < REGIONS - 1]
    has_y = [me > 0, me < INNER - 1]
    side_x, side_y = (down, up), (left, right)
    columns = [(region, lax.rem(me + 8 * k, INNER)) for k in (2, 1, 3)]
    greeted = [(has_x[e] & has_y[d], (side_x[e], side_y[d])) for e in range(2) for d in range(2)]
    for e in range(2):
        greeted.append((has_x[e], (side_x[e], me)))
        greeted.append((has_y[e] & (mine == 7 * e), (region, side_y[e])))
    for k in (4, 3, 5, 2, 6, 1, 7):
        greeted.append((True, (region, plane + lax.rem(mine + k, 8))))
    greeted = greeted + [(True, other) for other in columns]

    def hello(to):
        pl.semaphore_signal(barrier, inc=1, device_id=to, device_id_type=MESH)

    expected = 0
    for exists, to in greeted:
        if exists is True:
            hello(to)
            expected = expected + 1
        else:
            pl.when(exists)(functools.partial(hello, to))
            expected = expected + jnp.where(exists, 1, 0)
    loads = [
        pltpu.make_async_copy(coarse, c.at[:, pl.ds(16, 256)], lsem.at[0]),
        pltpu.make_async_copy(crate, cr, lsem.at[1]),
        pltpu.make_async_copy(parents, pv, lsem.at[18]),
        pltpu.make_async_copy(steps, sv, lsem.at[19]),
    ]
    for j in range(8):
        cut = pl.ds(j * 128, 128)
        loads.append(pltpu.make_async_copy(fine.at[:, :, cut], f0.at[:, pl.ds(1, 32), j], lsem.at[2 + j]))
        loads.append(pltpu.make_async_copy(frate.at[:, cut], fr.at[:, j], lsem.at[10 + j]))
    for load in loads[:3]:
        load.start()

    zero = jnp.zeros((8, 128), F32)
    for i in range(5):
        c[i, 0:16] = jnp.zeros((16, 128), F32)
        c[i, 272:288] = jnp.zeros((16, 128), F32)
        for a in (0, 33):
            f0[i, a] = zero
            f1[i, a] = zero
    loads[0].wait()
    loads[1].wait()
    for side, (near, far) in enumerate(((15, 14), (0, 1))):
        for half in range(2):
            dst = pl.ds(half * 8, 8)
            for i in range(5):
                ys[side, 0, i, dst] = c[i, pl.ds(16 + half * 128 + near, 8, stride=16)]
                ys[side, 1, i, dst] = c[i, pl.ds(16 + half * 128 + far, 8, stride=16)]
            ys[side, 1, 5, dst] = cr[pl.ds(half * 128 + near, 8, stride=16)]
    for n, at in enumerate((255, 240, 15, 0)):
        for i in range(5):
            ds[n, i : i + 1] = c[i, 16 + at : 17 + at]
        ds[n, 5:8] = jnp.zeros((3, 128), F32)

    for e in range(2):

        @pl.when(~has_x[e])
        def _():
            xh[e] = jnp.zeros(xh.shape[1:], F32)
            xr[e] = jnp.zeros(xr.shape[1:], F32)

        @pl.when(~has_y[e])
        def _():
            yh[e] = jnp.zeros(yh.shape[1:], F32)

        for d in range(2):

            @pl.when(~(has_x[e] & has_y[d]))
            def _():
                dr[2 * e + d] = jnp.zeros((8, 128), F32)

    pl.semaphore_wait(barrier, expected)

    def remote(src, dst, n, to):
        return pltpu.make_async_remote_copy(
            src_ref=src, dst_ref=dst, send_sem=ssem.at[n], recv_sem=rsem.at[n], device_id=to, device_id_type=MESH
        )

    near, far = [], []
    for e in range(2):
        o = 1 - e
        near.append((remote(c.at[:, pl.ds(16 + 240 * o, 16)], xh.at[e, 0], e, (side_x[o], me)), has_x[o], has_x[e]))
        near.append(
            (
                remote(ys.at[e, 0, pl.ds(0, 5)], yh.at[e, 0, pl.ds(0, 5)], 2 + e, (region, side_y[o])),
                has_y[o],
                has_y[e],
            )
        )
        far.append((remote(cr.at[pl.ds(240 * o, 16)], xr.at[e], 8 + e, (side_x[o], me)), has_x[o], has_x[e]))
        far.append(
            (remote(c.at[:, pl.ds(32 + 208 * o, 16)], xh.at[e, 1], 16 + e, (side_x[o], me)), has_x[o], has_x[e])
        )
        far.append((remote(ys.at[e, 1], yh.at[e, 1], 18 + e, (region, side_y[o])), has_y[o], has_y[e]))
    for n in range(4):
        e, d = n // 2, n % 2
        far.insert(
            n,
            (
                remote(ds.at[n], dr.at[n], 4 + n, (side_x[1 - e], side_y[1 - d])),
                has_x[1 - e] & has_y[1 - d],
                has_x[e] & has_y[d],
            ),
        )
    for halo, sends, _ in near + far:
        pl.when(sends)(halo.start)
    for load in loads[3:]:
        load.start()
    for other in columns:
        pl.semaphore_signal(ready, inc=1, device_id=other, device_id_type=MESH)

    loads[2].wait()
    block_row = jnp.broadcast_to(pv[...], (32, 32))
    ri, ci = iota((32, 32), 0), iota((32, 32), 1)
    block = jnp.sum(jnp.where(ri == ci, block_row, 0), axis=1, keepdims=True)
    owner = block >> 3
    slot = jnp.sum(
        jnp.where((jnp.broadcast_to(owner, (32, 32)) == (block_row >> 3)) & (ci < ri), 1, 0),
        axis=1,
        keepdims=True,
    )
    key = jnp.broadcast_to(owner * 2 + slot, (32, 128))
    ri, ci = iota((32, 128), 0), iota((32, 128), 1)
    layer = jnp.broadcast_to((block & 7) + 1, (32, 128))
    key_row = jnp.sum(jnp.where(ri == ci, key, 0), axis=0, keepdims=True)
    patch_row = jnp.sum(jnp.where(key == ci, ri, 0), axis=0, keepdims=True)
    layer_row = jnp.sum(jnp.where(key == ci, layer, 0), axis=0, keepdims=True) - 1
    table[...] = jnp.where(
        sub == 0,
        jnp.broadcast_to(key_row, (8, 128)),
        jnp.where(sub == 1, jnp.broadcast_to(patch_row, (8, 128)), jnp.broadcast_to(layer_row, (8, 128))),
    )
    look = pltpu.make_async_copy(table, keys, tsem)
    look.start()

    shifts = coarse_shifts((16, 128))

    def coarse_plane(x, carry):
        at = pl.multiple_of(x * 16, 16)
        cells = [c[i, pl.ds(at + 16, 16)] for i in range(5)]
        below = [c[i, pl.ds(at, 16)] for i in range(5)]
        above = [c[i, pl.ds(at + 32, 16)] for i in range(5)]
        for i, q in enumerate(hydro(cells, below, above, *shifts)):
            h[i, pl.ds(at, 16)] = q
        return carry

    lax.fori_loop(0, 16, coarse_plane, 0, unroll=4)

    look.wait()
    slots = [keys[2, 2 * me], keys[2, 2 * me + 1]]
    for s in range(2):
        covers[8 * s : 8 * s + 8] = jnp.where(lane // 16 == slots[s], 1, 0)
    my_key = keys[0, me]

    side = lane % 2
    first = (lane % 4) // 2 == 0
    own_slot = jnp.where(first, slots[0], slots[1])
    pick = lax.rem(jnp.where(side == 0, 16 * own_slot + 127, 16 * own_slot + 16) + 128, 128)
    spread = ((lane % 64) // 4) * 8 + ((lane % 4) // 2) * 4 + side
    cuts = [16 * jnp.maximum(s, 0) + lane % 16 for s in slots]
    inside = [
        jnp.where(((side == 0) & (s == 0)) | ((side == 1) & (s == 7)), 0.0, 1.0) for s in slots
    ]

    def z_values(src, base):
        low = iota((16, 128), 1) % 16 == 15

        def body(x, carry):
            at = pl.multiple_of(x * 16, 16)
            p, u, v, w, f = (src[i, pl.ds(at + base, 16)] for i in range(5))
            zv[0, pl.ds(at, 16)] = NB * (p + jnp.where(low, w, -w))
            zv[1, pl.ds(at, 16)] = NB * u
            zv[2, pl.ds(at, 16)] = NB * v
            zv[3, pl.ds(at, 16)] = f * jnp.where(low, NB * (1 + ADV[2]), NB * (1 - ADV[2]))
            return carry

        lax.fori_loop(0, 16, body, 0, unroll=8)

    def z_tiles():
        def body(x, tiles):
            tiles = list(tiles)
            for v in range(4):
                for odd in range(2):
                    q = zv[v, pl.ds(x * 16 + odd, 8, stride=2)]
                    tiles[v] = jnp.where(lane // 4 == x * 2 + odd, take(q, pick), tiles[v])
            return tuple(tiles)

        tiles = lax.fori_loop(0, 16, body, (zero,) * 4, unroll=16)
        return [
            [
                inside[s] * jnp.where(lane < 64, take(tiles[2 * w], spread + 2 * s), take(tiles[2 * w + 1], spread + 2 * s))
                for w in range(2)
            ]
            for s in range(2)
        ]

    def xy_tile(face, s):
        tile = zero
        for v in range(4):
            for odd in range(2):
                pos = v * 32 + odd * 16
                q = fv[face, v, pl.ds(odd, 8, stride=2)]
                tile = jnp.where(lane // 16 == pos // 16, take(q, cuts[s]), tile)
        return tile

    def put_tile(t, s, face, tile):
        p1[t, pl.ds(s * 6 + face, 8, stride=16)] = tile

    def get_tile(t, s, face):
        return p1[t, pl.ds(s * 6 + face, 8, stride=16)]

    z_values(c, 16)
    for s, pair in enumerate(z_tiles()):
        for w, tile in enumerate(pair):
            put_tile(0, s, 4 + w, tile)

    for halo, _, arrives in near:
        pl.when(arrives)(halo.wait_recv)
    mx = [jnp.where(exists, 1.0, 0.0) for exists in has_x]
    my = [jnp.where(exists, 1.0, 0.0) for exists in has_y]

    def near_x(e):
        return [xh[e, 0, i] for i in range(5)]

    def near_y(e):
        return [yh[e, 0, i] for i in range(5)]

    for e in range(2):
        p, u, v, w, f = near_x(e)
        for i, q in enumerate(face_values(p, u, v, w, f, 0, e == 1)):
            fv[e, i] = mx[e] * q
        p, u, v, w, f = near_y(e)
        for i, q in enumerate(face_values(p, v, u, w, f, 1, e == 1)):
            fv[2 + e, i] = my[e] * q
    for s in range(2):
        for face in range(4):
            put_tile(0, s, face, xy_tile(face, s))

    def send_pieces(t):
        r1[t][mine, 0:12] = p1[t, pl.ds(mine * 16, 12)]

        for k in (4, 3, 5, 2, 6, 1, 7):
            to = lax.rem(mine + k, 8)
            remote(
                p1.at[t, pl.ds(to * 16, 12)], r1[t].at[mine, pl.ds(0, 12)], 10 + t, (region, plane + to)
            ).start()

    send_pieces(0)

    def add_face(ref, cut, face, n, t1, high):
        e0, e1, e2, e3 = (fv[face, v, pl.ds(8 * cut[0], 8)] for v in range(4))
        at = cut[1]
        ref[0, at] = ref[0, at] + e0
        ref[n, at] = ref[n, at] - e0 if high else ref[n, at] + e0
        ref[t1, at] = ref[t1, at] + e1
        ref[3, at] = ref[3, at] + e2
        ref[4, at] = ref[4, at] + e3

    for half in range(2):
        add_face(h, (half, pl.ds(half * 8, 8)), 0, 1, 2, False)
        add_face(h, (half, pl.ds(240 + half * 8, 8)), 1, 1, 2, True)
        add_face(h, (half, pl.ds(half * 128, 8, stride=16)), 2, 2, 1, False)
        add_face(h, (half, pl.ds(half * 128 + 15, 8, stride=16)), 3, 2, 1, True)

    def coarse_burn(x, carry):
        at = pl.multiple_of(x * 64, 64)
        p, f = burn_once(h[0, pl.ds(at, 64)], h[4, pl.ds(at, 64)], cr[pl.ds(at, 64)])
        h[0, pl.ds(at, 64)] = p
        h[4, pl.ds(at, 64)] = f
        return carry

    lax.fori_loop(0, 4, coarse_burn, 0, unroll=4)

    z_values(h, 0)
    for s, pair in enumerate(z_tiles()):
        for w, tile in enumerate(pair):
            put_tile(1, s, 4 + w, 0.5 * (get_tile(0, s, 4 + w) + tile))
    for halo, _, arrives in far:
        pl.when(arrives)(halo.wait_recv)

    def own_rows(axis, e):
        if axis == 0:
            return [c[i, pl.ds(16 + 240 * e, 16)] for i in range(5)]
        return [
            jnp.concatenate([c[i, pl.ds(16 + 128 * b + 15 * e, 8, stride=16)] for b in range(2)], axis=0)
            for i in range(5)
        ]

    def corner(n, scale):
        return [dr[n, i : i + 1] * scale for i in range(5)]

    for e in range(2):
        values = ghost_step(
            near_x(e), [xh[e, 1, i] for i in range(5)], own_rows(0, e), corner(2 * e, my[0]), corner(2 * e + 1, my[1]), xr[e], 0, e == 1
        )
        for i, q in enumerate(values):
            fv[e, i] = mx[e] * q
        values = ghost_step(
            near_y(e), [yh[e, 1, i] for i in range(5)], own_rows(1, e),
            corner(e, mx[0]), corner(2 + e, mx[1]), yh[e, 1, 5], 1, e == 1,
        )
        for i, q in enumerate(values):
            fv[2 + e, i] = my[e] * q
    for s in range(2):
        for face in range(4):
            put_tile(1, s, face, 0.5 * (get_tile(0, s, face) + xy_tile(face, s)))
    send_pieces(1)

    for load in loads[3:]:
        load.wait()
    count = sv[0]
    counted = jnp.broadcast_to(count, (8, 128)).astype(F32)
    span = 0.25 / counted
    fine_shift = fine_shifts()

    def rates(x, carry):
        q = span * fr[x]
        fa[x] = 1.0 + q
        fb[x] = 0.5 * q
        return carry

    lax.fori_loop(0, 32, rates, 0, unroll=8)

    def fine_hydro(src, dst):
        def body(x, carry):
            cells = [src[i, x + 1] for i in range(5)]
            below = [src[i, x] for i in range(5)]
            above = [src[i, x + 2] for i in range(5)]
            for i, q in enumerate(hydro(cells, below, above, *fine_shift)):
                dst[i, x + 1] = q
            return carry

        lax.fori_loop(0, 32, body, 0, unroll=16)

    fine_hydro(f0, f1)

    def wait_all(ref, sem):
        pltpu.make_async_copy(ref, ref, sem).wait()

    def send_faces(t):
        wait_all(r1[t].at[pl.ds(0, 7), pl.ds(0, 12)], rsem.at[10 + t])

        def piece(key):
            pair = r1[t][(key & 15) >> 1]
            return jnp.where((key & 1) == 0, pair[0:6], pair[6:12])

        for k in FAR_FIRST:
            to = lax.rem(me + k, INNER)
            p2[t, to, 0:6] = piece(keys[0, to])
            remote(p2.at[t, to, pl.ds(0, 6)], r2[t].at[me, pl.ds(0, 6)], 12 + t, (region, to)).start()
        r2[t][me, 0:6] = piece(my_key)

    pl.semaphore_wait(ready, len(columns))
    send_faces(0)
    send_faces(1)
    stores = []

    q4, z = lane // 32, lane % 32
    edge_y = jnp.where((lane < 32) & (sub == 0) | (lane >= 96) & (sub == 7), 1.0, 0.0)
    sign_y = jnp.where(lane < 64, edge_y, -edge_y)
    edge_z = jnp.where((z == 0) | (z == 31), 1.0, 0.0)
    sign_z = jnp.where(z < 16, edge_z, -edge_z)
    pick_x = (q4 // 2) * 16 + z // 2
    pick_z = (q4 // 2) * 2 + z // 16

    def add_ghosts(t, dst):
        wait_all(r2[t].at[pl.ds(0, INNER - 1), pl.ds(0, 6)], rsem.at[12 + t])
        start = (my_key >> 4) * 8
        for k in range(8):
            gt[pl.ds(k * 8, 8)] = r2[t][start + k]
        tiles = [gt[pl.ds(face, 8, stride=8)] for face in range(6)]
        for face, x in ((0, 1), (1, 32)):
            e = [take(tiles[face], pick_x + 32 * v) for v in range(4)]
            dst[0, x] = dst[0, x] + e[0]
            dst[1, x] = dst[1, x] + e[0] if face == 0 else dst[1, x] - e[0]
            dst[2, x] = dst[2, x] + e[1]
            dst[3, x] = dst[3, x] + e[2]
            dst[4, x] = dst[4, x] + e[3]
        for v in range(4):
            for odd in range(2):
                pick = v * 32 + odd * 16 + z // 2
                ey[v, pl.ds(odd, 8, stride=2)] = jnp.where(lane < 64, take(tiles[2], pick), take(tiles[3], pick))

        def body(x, carry):
            y = [jnp.broadcast_to(ey[v, pl.ds(x, 1)], (8, 128)) for v in range(4)]
            zz = [take(tiles[4 + v // 2], pick_z + ((v % 2) * 64 + x * 4)) for v in range(4)]
            add = [
                edge_y * y[0] + edge_z * zz[0],
                edge_y * y[1] + edge_z * zz[1],
                sign_y * y[0] + edge_z * zz[2],
                edge_y * y[2] + sign_z * zz[0],
                edge_y * y[3] + edge_z * zz[3],
            ]
            for i in range(5):
                dst[i, 2 * x + 1] = dst[i, 2 * x + 1] + add[i]
                dst[i, 2 * x + 2] = dst[i, 2 * x + 2] + add[i]
            return carry

        lax.fori_loop(0, 16, body, 0, unroll=16)

    live = [jnp.where(turn < count, 1.0, 0.0) for turn in range(BURN_MAX)]
    group = 16

    def burn(dst, at):
        p = [dst[0, at + i + 1] for i in range(group)]
        f = [dst[4, at + i + 1] for i in range(group)]
        for turn in range(BURN_MAX):
            for i in range(group):
                r = pl.reciprocal(fa[at + i] + fb[at + i] * jnp.tanh(p[i]), approx=True)
                d = live[turn] * (f[i] - f[i] * r)
                f[i] = f[i] - d
                p[i] = p[i] + 0.5 * d
        for i in range(group):
            dst[0, at + i + 1] = p[i]
            dst[4, at + i + 1] = f[i]

    add_ghosts(0, f1)
    for at in range(0, 32, group):
        burn(f1, at)
    fine_hydro(f1, f0)
    add_ghosts(1, f0)
    pick_m = ((lane % 32) // 16) * 64 + 2 * (lane % 16)

    def means(a):
        for i in range(5):
            tile = zero
            for g in range(4):
                at = a * 8 + 2 * g
                q = f0[i, at + 1] + f0[i, at + 2]
                q = q + lanes(q, -1)
                q = q + lanes(q, -32)
                tile = jnp.where(q4 == g, take(q, pick_m), tile)
            mb[pl.ds(a * 64 + i, 8, stride=8)] = 0.125 * tile

    def send_mean(to):
        remote(mb.at[pl.ds(to * 8, 5)], r3.at[me, pl.ds(0, 5)], 14, (region, to)).start()

    for half in range(2):
        burn(f0, 16 * half)
        means(2 * half)
        means(2 * half + 1)
        for k in range(8, 24):
            to = 16 * half + lax.rem(me + k, 16)
            if k != 16:
                send_mean(to)
            else:
                pl.when(me != to)(functools.partial(send_mean, to))
    r3[me, 0:5] = mb[pl.ds(me * 8, 5)]

    wait_all(r3.at[pl.ds(0, 31), pl.ds(0, 5)], rsem.at[14])

    def pick_pair(to):
        for s in range(2):
            p4[to, 5 * s : 5 * s + 5] = r3[keys[1, 2 * to + s], 0:5]

    for k in FAR_FIRST:
        to = lax.rem(me + k, INNER)
        pick_pair(to)
        remote(p4.at[to], r4.at[me, pl.ds(0, 10)], 15, (region, to)).start()

    pick_pair(me)
    r4[me, 0:10] = p4[me]
    for j in range(8):
        stores.append(
            pltpu.make_async_copy(
                f0.at[:, pl.ds(1, 32), j], fine_out.at[:, :, pl.ds(j * 128, 128)], lsem.at[2 + j]
            )
        )
        stores[-1].start()

    for halo, sends, _ in near + far:
        pl.when(sends)(halo.wait_send)
    for t in range(2):
        wait_all(r1[t].at[pl.ds(0, 7), pl.ds(0, 12)], ssem.at[10 + t])
        wait_all(r2[t].at[pl.ds(0, INNER - 1), pl.ds(0, 6)], ssem.at[12 + t])
    wait_all(r3.at[pl.ds(0, 31), pl.ds(0, 5)], ssem.at[14])
    wait_all(p4.at[pl.ds(0, 31)], ssem.at[15])
    for store in stores:
        store.wait()
    wait_all(r4.at[pl.ds(0, 31), pl.ds(0, 10)], rsem.at[15])


def place(stepped, means, fine, covers, coarse_out, fine_out, h, sem):
    stores = [pltpu.make_async_copy(fine, fine_out, sem.at[5])]
    stores[0].start()
    lane = iota((8, 128), 1)
    here = [covers[8 * s : 8 * s + 8] > 0 for s in range(2)]
    rows_of = means.reshape(512, 128)
    for i in range(5):

        def body(a, carry):
            tiles = [rows_of[pl.ds(a * 128 + s * 5 + i, 8, stride=16)] for s in range(2)]
            for g in range(4):
                for odd in range(2):
                    at = pl.ds((a * 4 + g) * 16 + odd, 8, stride=2)
                    q = stepped[i, at]
                    for s in range(2):
                        q = jnp.where(here[s], take(tiles[s], lane % 16 + (g * 32 + odd * 16)), q)
                    h[i, at] = q
            return carry

        lax.fori_loop(0, 4, body, 0, unroll=4)
        stores.append(pltpu.make_async_copy(h.at[i], coarse_out.at[i], sem.at[i]))
        stores[-1].start()
    for store in stores:
        store.wait()


def per_device(coarse_state, fine_state, coarse_rate, fine_rate, parents, burn_steps):
    vmem, hbm = pl.BlockSpec(memory_space=pltpu.VMEM), pl.BlockSpec(memory_space=pltpu.HBM)
    stepped, fine_mid, means, covers = pl.pallas_call(
        kernel,
        out_shape=(
            jax.ShapeDtypeStruct((5, 256, 128), F32),
            jax.ShapeDtypeStruct((5, 32, 1024), F32),
            jax.ShapeDtypeStruct((32, 16, 128), F32),
            jax.ShapeDtypeStruct((16, 128), jnp.int32),
        ),
        in_specs=[hbm] * 6,
        out_specs=(vmem,) * 4,
        scratch_shapes=[
            pltpu.VMEM((5, 288, 128), F32),
            pltpu.VMEM((256, 128), F32),
            pltpu.VMEM((2, 2, 5, 16, 128), F32),
            pltpu.VMEM((2, 16, 128), F32),
            pltpu.VMEM((2, 2, 6, 16, 128), F32),
            pltpu.VMEM((2, 2, 6, 16, 128), F32),
            pltpu.VMEM((4, 8, 128), F32),
            pltpu.VMEM((4, 8, 128), F32),
            pltpu.VMEM((4, 4, 16, 128), F32),
            pltpu.VMEM((4, 256, 128), F32),
            pltpu.VMEM((8, 128), jnp.int32),
            pltpu.SMEM((8, 128), jnp.int32),
            pltpu.VMEM((2, 128, 128), F32),
            pltpu.VMEM((8, 16, 128), F32),
            pltpu.VMEM((8, 16, 128), F32),
            pltpu.VMEM((2, 32, 8, 128), F32),
            pltpu.VMEM((32, 8, 128), F32),
            pltpu.VMEM((32, 8, 128), F32),
            pltpu.VMEM((5, 34, 8, 128), F32),
            pltpu.VMEM((5, 34, 8, 128), F32),
            pltpu.VMEM((32, 8, 128), F32),
            pltpu.VMEM((32, 8, 128), F32),
            pltpu.VMEM((32, 8, 128), F32),
            pltpu.VMEM((64, 128), F32),
            pltpu.VMEM((4, 16, 128), F32),
            pltpu.VMEM((256, 128), F32),
            pltpu.VMEM((32, 8, 128), F32),
            pltpu.VMEM((32, 10, 128), F32),
            pltpu.VMEM((1, 32), jnp.int32),
            pltpu.SMEM((1,), jnp.int32),
            pltpu.SemaphoreType.DMA((20,)),
            pltpu.SemaphoreType.DMA((20,)),
            pltpu.SemaphoreType.DMA((20,)),
            pltpu.SemaphoreType.DMA,
            pltpu.SemaphoreType.REGULAR,
        ],
        compiler_params=pltpu.CompilerParams(
            collective_id=0, has_side_effects=True, vmem_limit_bytes=24 * 2**20
        ),
        name="reactive_step",
    )(
        *(
            pltpu.with_memory_space_constraint(x, pltpu.HBM)
            for x in (
                coarse_state.reshape(5, 256, 128),
                fine_state.reshape(5, 32, 1024),
                coarse_rate.reshape(256, 128),
                fine_rate.reshape(32, 1024),
                parents,
            )
        ),
        burn_steps,
    )
    coarse_new, fine_new = pl.pallas_call(
        place,
        out_shape=(
            jax.ShapeDtypeStruct((5, 256, 128), F32),
            jax.ShapeDtypeStruct((5, 32, 1024), F32),
        ),
        in_specs=[vmem] * 4,
        out_specs=(hbm,) * 2,
        scratch_shapes=[
            pltpu.VMEM((5, 256, 128), F32),
            pltpu.SemaphoreType.DMA((6,)),
        ],
        compiler_params=pltpu.CompilerParams(vmem_limit_bytes=24 * 2**20),
        name="place",
    )(stepped, means, fine_mid, covers)
    return coarse_new.reshape(5, 16, 16, 128), fine_new.reshape(1, 5, 32, 1024)


def solution(mesh):
    in_specs = (
        P(None, "region", "inner", None),
        P(("region", "inner"), None, None, None),
        P("region", "inner", None),
        P(("region", "inner"), None, None),
        P("region", None),
        P(("region", "inner")),
    )
    out_specs = (P(None, "region", "inner", None), P(("region", "inner"), None, None, None))
    return jax.shard_map(per_device, mesh=mesh, in_specs=in_specs, out_specs=out_specs, check_vma=False)
```

```python
import functools

import jax
import jax.numpy as jnp
from jax import lax
from jax.experimental import pallas as pl
from jax.experimental.pallas import tpu as pltpu
from jax.sharding import PartitionSpec as P

MESH = pl.DeviceIdType.MESH
F32 = jnp.float32
ADV = (0.5, -0.3, 0.2)
KEEP = 0.1
NB = 0.15
BURN_MAX = 8
REGIONS = 4
INNER = 32


def hops(offset):
    z, y = offset // 8, offset // 2 % 4
    return min(z, 4 - z) + min(y, 4 - y)


FAR_FIRST = sorted(range(1, INNER), key=hops, reverse=True)


def iota(shape, axis):
    return lax.broadcasted_iota(jnp.int32, shape, axis)


def lanes(q, shift):
    return pltpu.roll(q, shift % 128, 1)


def rows(q, shift):
    return pltpu.roll(q, shift % q.shape[0], 0)


def hydro(c, xm, xp, yd, yu, zd, zu):
    p, u, v, w, f = c
    sx, mx = xm[0] + xm[1], xp[0] - xp[1]
    sy, my = yd(p + v), yu(p - v)
    sz, mz = zd(p + w), zu(p - w)
    hp = (sx + mx) + (sy + my) + (sz + mz)
    hu = (sx - mx) + (yd(u) + yu(u)) + (zd(u) + zu(u))
    hv = (xm[2] + xp[2]) + (sy - my) + (zd(v) + zu(v))
    hw = (xm[3] + xp[3]) + (yd(w) + yu(w)) + (sz - mz)
    hf = (
        ((1 + ADV[0]) * xm[4] + (1 - ADV[0]) * xp[4])
        + ((1 + ADV[1]) * yd(f) + (1 - ADV[1]) * yu(f))
        + ((1 + ADV[2]) * zd(f) + (1 - ADV[2]) * zu(f))
    )
    return [KEEP * a + NB * b for a, b in zip(c, (hp, hu, hv, hw, hf))]


def take(q, index):
    return jnp.take_along_axis(q, index, axis=1, mode="promise_in_bounds")


def coarse_shifts(shape):
    row, lane = iota(shape, 0), iota(shape, 1)
    zd = lambda q: jnp.where(lane == 0, 0.0, lanes(q, 1))
    zu = lambda q: jnp.where(lane == 127, 0.0, lanes(q, -1))
    yd = lambda q: jnp.where(row == 0, 0.0, rows(q, 1))
    yu = lambda q: jnp.where(row == shape[0] - 1, 0.0, rows(q, -1))
    return yd, yu, zd, zu


def fine_shifts():
    sub, lane = iota((8, 128), 0), iota((8, 128), 1)
    z = lane % 32

    def yd(q):
        t = lanes(q, 32)
        t = jnp.where(lane < 32, rows(t, 1), t)
        return jnp.where((lane < 32) & (sub == 0), 0.0, t)

    def yu(q):
        t = lanes(q, -32)
        t = jnp.where(lane >= 96, rows(t, -1), t)
        return jnp.where((lane >= 96) & (sub == 7), 0.0, t)

    zd = lambda q: jnp.where(z == 0, 0.0, lanes(q, 1))
    zu = lambda q: jnp.where(z == 31, 0.0, lanes(q, -1))
    return yd, yu, zd, zu


def burn_once(p, f, rate):
    burned = f * pl.reciprocal(1.0 + 0.5 * rate * (1.0 + 0.5 * jnp.tanh(p)), approx=True)
    return p + 0.5 * (f - burned), burned


def face_values(p, n, t1, t2, f, axis, high):
    sign = -1.0 if high else 1.0
    return [NB * (p + sign * n), NB * t1, NB * t2, NB * (1 + sign * ADV[axis]) * f]


def ghost_step(near, far, own, dlo, dhi, rate, axis, high):
    n, r = (1, 2) if axis == 0 else (2, 1)
    row, lane = iota((16, 128), 0), iota((16, 128), 1)
    an, ar, az = ADV[axis], ADV[1 - axis], ADV[2]
    beyond, tr, tw, tf = far
    sn = own[0] + own[n] if high else beyond
    mn = beyond if high else own[0] - own[n]
    minus_f, plus_f = (own[4], tf) if high else (tf, own[4])
    p, w, f = near[0], near[3], near[4]

    def rd(q, d):
        return jnp.where(row == 0, d, rows(q, 1))

    def ru(q, d):
        return jnp.where(row == 15, d, rows(q, -1))

    zd = lambda q: jnp.where(lane == 0, 0.0, lanes(q, 1))
    zu = lambda q: jnp.where(lane == 127, 0.0, lanes(q, -1))
    sr, mr = rd(p + near[r], dlo[0] + dlo[r]), ru(p - near[r], dhi[0] - dhi[r])
    sz, mz = zd(p + w), zu(p - w)
    hp = (sn + mn) + (sr + mr) + (sz + mz)
    hn = (sn - mn) + (rd(near[n], dlo[n]) + ru(near[n], dhi[n])) + (zd(near[n]) + zu(near[n]))
    hr = (own[r] + tr) + (sr - mr) + (zd(near[r]) + zu(near[r]))
    hw = (own[3] + tw) + (rd(w, dlo[3]) + ru(w, dhi[3])) + (sz - mz)
    hf = (
        ((1 + an) * minus_f + (1 - an) * plus_f)
        + ((1 + ar) * rd(f, dlo[4]) + (1 - ar) * ru(f, dhi[4]))
        + ((1 + az) * zd(f) + (1 - az) * zu(f))
    )
    pressure, normal, tangent, across, fuel = (
        KEEP * a + NB * b for a, b in zip((p, near[n], near[r], w, f), (hp, hn, hr, hw, hf))
    )
    pressure, fuel = burn_once(pressure, fuel, rate)
    return face_values(pressure, normal, tangent, across, fuel, axis, high)


def kernel(
    coarse, fine, crate, frate, parents, steps, h, fine_out, r4, covers,
    c, cr, xs, xh, xr, ys, yh, ds, dr, fv, zv, table, keys, p1, r1a, r1b, p2, r2a, r2b, f0, f1, fa, fb, fr, gt, ey,
    mb, r3, p4, pv, sv, ssem, rsem, lsem, tsem, ready,
):
    r1, r2 = (r1a, r1b), (r2a, r2b)
    region, me = lax.axis_index("region"), lax.axis_index("inner")
    up, down = lax.rem(region + 1, REGIONS), lax.rem(region + REGIONS - 1, REGIONS)
    right, left = lax.rem(me + 1, INNER), lax.rem(me + INNER - 1, INNER)
    plane, mine = (me // 8) * 8, lax.rem(me, 8)
    sub, lane = iota((8, 128), 0), iota((8, 128), 1)

    barrier = pltpu.get_barrier_semaphore()
    has_x = [region > 0, region < REGIONS - 1]
    has_y = [me > 0, me < INNER - 1]
    side_x, side_y = (down, up), (left, right)
    columns = [(region, lax.rem(me + 8 * k, INNER)) for k in (2, 1, 3)]
    greeted = [(has_x[e] & has_y[d], (side_x[e], side_y[d])) for e in range(2) for d in range(2)]
    for e in range(2):
        greeted.append((has_x[e], (side_x[e], me)))
        greeted.append((has_y[e] & (mine == 7 * e), (region, side_y[e])))
    for k in (4, 3, 5, 2, 6, 1, 7):
        greeted.append((True, (region, plane + lax.rem(mine + k, 8))))
    greeted = greeted + [(True, other) for other in columns]

    def hello(to):
        pl.semaphore_signal(barrier, inc=1, device_id=to, device_id_type=MESH)

    expected = 0
    for exists, to in greeted:
        if exists is True:
            hello(to)
            expected = expected + 1
        else:
            pl.when(exists)(functools.partial(hello, to))
            expected = expected + jnp.where(exists, 1, 0)
    loads = [
        pltpu.make_async_copy(coarse, c.at[:, pl.ds(16, 256)], lsem.at[0]),
        pltpu.make_async_copy(crate, cr, lsem.at[1]),
        pltpu.make_async_copy(parents, pv, lsem.at[18]),
        pltpu.make_async_copy(steps, sv, lsem.at[19]),
    ]
    for j in range(8):
        cut = pl.ds(j * 128, 128)
        loads.append(pltpu.make_async_copy(fine.at[:, :, cut], f0.at[:, pl.ds(1, 32), j], lsem.at[2 + j]))
        loads.append(pltpu.make_async_copy(frate.at[:, cut], fr.at[:, j], lsem.at[10 + j]))
    for load in loads[:3]:
        load.start()

    zero = jnp.zeros((8, 128), F32)
    for i in range(5):
        c[i, 0:16] = jnp.zeros((16, 128), F32)
        c[i, 272:288] = jnp.zeros((16, 128), F32)
        for a in (0, 33):
            f0[i, a] = zero
            f1[i, a] = zero
    loads[0].wait()
    loads[1].wait()
    for side, (near, far) in enumerate(((15, 14), (0, 1))):
        for half in range(2):
            dst = pl.ds(half * 8, 8)
            for i in range(5):
                ys[side, 0, i, dst] = c[i, pl.ds(16 + half * 128 + near, 8, stride=16)]
            p, u, v, w, f = (c[i, pl.ds(16 + half * 128 + far, 8, stride=16)] for i in range(5))
            for i, q in enumerate((p - v if side else p + v, u, w, f)):
                ys[side, 1, i, dst] = q
            p, u, v, w, f = (c[i, pl.ds(16 + far * 16 + half * 8, 8)] for i in range(5))
            for i, q in enumerate((p - u if side else p + u, v, w, f)):
                xs[side, i, dst] = q
            ys[side, 1, 4, dst] = cr[pl.ds(half * 128 + near, 8, stride=16)]
    for n, at in enumerate((255, 240, 15, 0)):
        for i in range(5):
            ds[n, i : i + 1] = c[i, 16 + at : 17 + at]
        ds[n, 5:8] = jnp.zeros((3, 128), F32)

    for e in range(2):

        @pl.when(~has_x[e])
        def _():
            xh[e] = jnp.zeros(xh.shape[1:], F32)
            xr[e] = jnp.zeros(xr.shape[1:], F32)

        @pl.when(~has_y[e])
        def _():
            yh[e] = jnp.zeros(yh.shape[1:], F32)

        for d in range(2):

            @pl.when(~(has_x[e] & has_y[d]))
            def _():
                dr[2 * e + d] = jnp.zeros((8, 128), F32)

    pl.semaphore_wait(barrier, expected)

    def remote(src, dst, n, to):
        return pltpu.make_async_remote_copy(
            src_ref=src, dst_ref=dst, send_sem=ssem.at[n], recv_sem=rsem.at[n], device_id=to, device_id_type=MESH
        )

    near, far = [], []
    for e in range(2):
        o = 1 - e
        near.append((remote(c.at[:, pl.ds(16 + 240 * o, 16)], xh.at[e, 0], e, (side_x[o], me)), has_x[o], has_x[e]))
        near.append(
            (
                remote(ys.at[e, 0, pl.ds(0, 5)], yh.at[e, 0, pl.ds(0, 5)], 2 + e, (region, side_y[o])),
                has_y[o],
                has_y[e],
            )
        )
        far.append((remote(cr.at[pl.ds(240 * o, 16)], xr.at[e], 8 + e, (side_x[o], me)), has_x[o], has_x[e]))
        far.append(
            (remote(xs.at[e], xh.at[e, 1, pl.ds(0, 4)], 16 + e, (side_x[o], me)), has_x[o], has_x[e])
        )
        far.append((remote(ys.at[e, 1, pl.ds(0, 5)], yh.at[e, 1, pl.ds(0, 5)], 18 + e, (region, side_y[o])), has_y[o], has_y[e]))
    for n in range(4):
        e, d = n // 2, n % 2
        far.insert(
            n,
            (
                remote(ds.at[n], dr.at[n], 4 + n, (side_x[1 - e], side_y[1 - d])),
                has_x[1 - e] & has_y[1 - d],
                has_x[e] & has_y[d],
            ),
        )
    for halo, sends, _ in near + far:
        pl.when(sends)(halo.start)
    for load in loads[3:]:
        load.start()
    for other in columns:
        pl.semaphore_signal(ready, inc=1, device_id=other, device_id_type=MESH)

    loads[2].wait()
    block_row = jnp.broadcast_to(pv[...], (32, 32))
    ri, ci = iota((32, 32), 0), iota((32, 32), 1)
    block = jnp.sum(jnp.where(ri == ci, block_row, 0), axis=1, keepdims=True)
    owner = block >> 3
    slot = jnp.sum(
        jnp.where((jnp.broadcast_to(owner, (32, 32)) == (block_row >> 3)) & (ci < ri), 1, 0),
        axis=1,
        keepdims=True,
    )
    key = jnp.broadcast_to(owner * 2 + slot, (32, 128))
    ri, ci = iota((32, 128), 0), iota((32, 128), 1)
    layer = jnp.broadcast_to((block & 7) + 1, (32, 128))
    key_row = jnp.sum(jnp.where(ri == ci, key, 0), axis=0, keepdims=True)
    patch_row = jnp.sum(jnp.where(key == ci, ri, 0), axis=0, keepdims=True)
    layer_row = jnp.sum(jnp.where(key == ci, layer, 0), axis=0, keepdims=True) - 1
    table[...] = jnp.where(
        sub == 0,
        jnp.broadcast_to(key_row, (8, 128)),
        jnp.where(sub == 1, jnp.broadcast_to(patch_row, (8, 128)), jnp.broadcast_to(layer_row, (8, 128))),
    )
    look = pltpu.make_async_copy(table, keys, tsem)
    look.start()

    shifts = coarse_shifts((16, 128))

    def coarse_plane(x, carry):
        at = pl.multiple_of(x * 16, 16)
        cells = [c[i, pl.ds(at + 16, 16)] for i in range(5)]
        below = [c[i, pl.ds(at, 16)] for i in range(5)]
        above = [c[i, pl.ds(at + 32, 16)] for i in range(5)]
        for i, q in enumerate(hydro(cells, below, above, *shifts)):
            h[i, pl.ds(at, 16)] = q
        return carry

    lax.fori_loop(0, 16, coarse_plane, 0, unroll=4)

    look.wait()
    slots = [keys[2, 2 * me], keys[2, 2 * me + 1]]
    for s in range(2):
        covers[8 * s : 8 * s + 8] = jnp.where(lane // 16 == slots[s], 1, 0)
    my_key = keys[0, me]

    side = lane % 2
    first = (lane % 4) // 2 == 0
    own_slot = jnp.where(first, slots[0], slots[1])
    pick = lax.rem(jnp.where(side == 0, 16 * own_slot + 127, 16 * own_slot + 16) + 128, 128)
    spread = ((lane % 64) // 4) * 8 + ((lane % 4) // 2) * 4 + side
    cuts = [16 * jnp.maximum(s, 0) + lane % 16 for s in slots]
    inside = [
        jnp.where(((side == 0) & (s == 0)) | ((side == 1) & (s == 7)), 0.0, 1.0) for s in slots
    ]

    def z_values(src, base):
        low = iota((16, 128), 1) % 16 == 15

        def body(x, carry):
            at = pl.multiple_of(x * 16, 16)
            p, u, v, w, f = (src[i, pl.ds(at + base, 16)] for i in range(5))
            zv[0, pl.ds(at, 16)] = NB * (p + jnp.where(low, w, -w))
            zv[1, pl.ds(at, 16)] = NB * u
            zv[2, pl.ds(at, 16)] = NB * v
            zv[3, pl.ds(at, 16)] = f * jnp.where(low, NB * (1 + ADV[2]), NB * (1 - ADV[2]))
            return carry

        lax.fori_loop(0, 16, body, 0, unroll=8)

    def z_tiles():
        def body(x, tiles):
            tiles = list(tiles)
            for v in range(4):
                for odd in range(2):
                    q = zv[v, pl.ds(x * 16 + odd, 8, stride=2)]
                    tiles[v] = jnp.where(lane // 4 == x * 2 + odd, take(q, pick), tiles[v])
            return tuple(tiles)

        tiles = lax.fori_loop(0, 16, body, (zero,) * 4, unroll=16)
        return [
            [
                inside[s] * jnp.where(lane < 64, take(tiles[2 * w], spread + 2 * s), take(tiles[2 * w + 1], spread + 2 * s))
                for w in range(2)
            ]
            for s in range(2)
        ]

    def xy_tile(face, s):
        tile = zero
        for v in range(4):
            for odd in range(2):
                pos = v * 32 + odd * 16
                q = fv[face, v, pl.ds(odd, 8, stride=2)]
                tile = jnp.where(lane // 16 == pos // 16, take(q, cuts[s]), tile)
        return tile

    def put_tile(t, s, face, tile):
        p1[t, pl.ds(s * 6 + face, 8, stride=16)] = tile

    def get_tile(t, s, face):
        return p1[t, pl.ds(s * 6 + face, 8, stride=16)]

    z_values(c, 16)
    for s, pair in enumerate(z_tiles()):
        for w, tile in enumerate(pair):
            put_tile(0, s, 4 + w, tile)

    for halo, _, arrives in near:
        pl.when(arrives)(halo.wait_recv)
    mx = [jnp.where(exists, 1.0, 0.0) for exists in has_x]
    my = [jnp.where(exists, 1.0, 0.0) for exists in has_y]

    def near_x(e):
        return [xh[e, 0, i] for i in range(5)]

    def near_y(e):
        return [yh[e, 0, i] for i in range(5)]

    for e in range(2):
        p, u, v, w, f = near_x(e)
        for i, q in enumerate(face_values(p, u, v, w, f, 0, e == 1)):
            fv[e, i] = mx[e] * q
        p, u, v, w, f = near_y(e)
        for i, q in enumerate(face_values(p, v, u, w, f, 1, e == 1)):
            fv[2 + e, i] = my[e] * q
    for s in range(2):
        for face in range(4):
            put_tile(0, s, face, xy_tile(face, s))

    def send_pieces(t):
        r1[t][mine, 0:12] = p1[t, pl.ds(mine * 16, 12)]

        for k in (4, 3, 5, 2, 6, 1, 7):
            to = lax.rem(mine + k, 8)
            remote(
                p1.at[t, pl.ds(to * 16, 12)], r1[t].at[mine, pl.ds(0, 12)], 10 + t, (region, plane + to)
            ).start()

    send_pieces(0)

    def add_face(ref, cut, face, n, t1, high):
        e0, e1, e2, e3 = (fv[face, v, pl.ds(8 * cut[0], 8)] for v in range(4))
        at = cut[1]
        ref[0, at] = ref[0, at] + e0
        ref[n, at] = ref[n, at] - e0 if high else ref[n, at] + e0
        ref[t1, at] = ref[t1, at] + e1
        ref[3, at] = ref[3, at] + e2
        ref[4, at] = ref[4, at] + e3

    for half in range(2):
        add_face(h, (half, pl.ds(half * 8, 8)), 0, 1, 2, False)
        add_face(h, (half, pl.ds(240 + half * 8, 8)), 1, 1, 2, True)
        add_face(h, (half, pl.ds(half * 128, 8, stride=16)), 2, 2, 1, False)
        add_face(h, (half, pl.ds(half * 128 + 15, 8, stride=16)), 3, 2, 1, True)

    def coarse_burn(x, carry):
        at = pl.multiple_of(x * 64, 64)
        p, f = burn_once(h[0, pl.ds(at, 64)], h[4, pl.ds(at, 64)], cr[pl.ds(at, 64)])
        h[0, pl.ds(at, 64)] = p
        h[4, pl.ds(at, 64)] = f
        return carry

    lax.fori_loop(0, 4, coarse_burn, 0, unroll=4)

    z_values(h, 0)
    for s, pair in enumerate(z_tiles()):
        for w, tile in enumerate(pair):
            put_tile(1, s, 4 + w, 0.5 * (get_tile(0, s, 4 + w) + tile))
    for halo, _, arrives in far:
        pl.when(arrives)(halo.wait_recv)

    def own_rows(axis, e):
        if axis == 0:
            return [c[i, pl.ds(16 + 240 * e, 16)] for i in range(5)]
        return [
            jnp.concatenate([c[i, pl.ds(16 + 128 * b + 15 * e, 8, stride=16)] for b in range(2)], axis=0)
            for i in range(5)
        ]

    def corner(n, scale):
        return [dr[n, i : i + 1] * scale for i in range(5)]

    for e in range(2):
        values = ghost_step(
            near_x(e), [xh[e, 1, i] for i in range(4)], own_rows(0, e), corner(2 * e, my[0]), corner(2 * e + 1, my[1]), xr[e], 0, e == 1
        )
        for i, q in enumerate(values):
            fv[e, i] = mx[e] * q
        values = ghost_step(
            near_y(e), [yh[e, 1, i] for i in range(4)], own_rows(1, e),
            corner(e, mx[0]), corner(2 + e, mx[1]), yh[e, 1, 4], 1, e == 1,
        )
        for i, q in enumerate(values):
            fv[2 + e, i] = my[e] * q
    for s in range(2):
        for face in range(4):
            put_tile(1, s, face, 0.5 * (get_tile(0, s, face) + xy_tile(face, s)))
    send_pieces(1)

    for load in loads[3:]:
        load.wait()
    count = sv[0]
    counted = jnp.broadcast_to(count, (8, 128)).astype(F32)
    span = 0.25 / counted
    fine_shift = fine_shifts()

    def rates(x, carry):
        q = span * fr[x]
        fa[x] = 1.0 + q
        fb[x] = 0.5 * q
        return carry

    lax.fori_loop(0, 32, rates, 0, unroll=8)

    def fine_hydro(src, dst):
        def body(x, carry):
            cells = [src[i, x + 1] for i in range(5)]
            below = [src[i, x] for i in range(5)]
            above = [src[i, x + 2] for i in range(5)]
            for i, q in enumerate(hydro(cells, below, above, *fine_shift)):
                dst[i, x + 1] = q
            return carry

        lax.fori_loop(0, 32, body, 0, unroll=16)

    fine_hydro(f0, f1)

    def wait_all(ref, sem):
        pltpu.make_async_copy(ref, ref, sem).wait()

    def send_faces(t):
        wait_all(r1[t].at[pl.ds(0, 7), pl.ds(0, 12)], rsem.at[10 + t])

        def piece(key):
            pair = r1[t][(key & 15) >> 1]
            return jnp.where((key & 1) == 0, pair[0:6], pair[6:12])

        for k in FAR_FIRST:
            to = lax.rem(me + k, INNER)
            p2[t, to, 0:6] = piece(keys[0, to])
            remote(p2.at[t, to, pl.ds(0, 6)], r2[t].at[me, pl.ds(0, 6)], 12 + t, (region, to)).start()
        r2[t][me, 0:6] = piece(my_key)

    pl.semaphore_wait(ready, len(columns))
    send_faces(0)
    send_faces(1)
    stores = []

    q4, z = lane // 32, lane % 32
    edge_y = jnp.where((lane < 32) & (sub == 0) | (lane >= 96) & (sub == 7), 1.0, 0.0)
    sign_y = jnp.where(lane < 64, edge_y, -edge_y)
    edge_z = jnp.where((z == 0) | (z == 31), 1.0, 0.0)
    sign_z = jnp.where(z < 16, edge_z, -edge_z)
    pick_x = (q4 // 2) * 16 + z // 2
    pick_z = (q4 // 2) * 2 + z // 16

    def add_ghosts(t, dst):
        wait_all(r2[t].at[pl.ds(0, INNER - 1), pl.ds(0, 6)], rsem.at[12 + t])
        start = (my_key >> 4) * 8
        for k in range(8):
            gt[pl.ds(k * 8, 8)] = r2[t][start + k]
        tiles = [gt[pl.ds(face, 8, stride=8)] for face in range(6)]
        for face, x in ((0, 1), (1, 32)):
            e = [take(tiles[face], pick_x + 32 * v) for v in range(4)]
            dst[0, x] = dst[0, x] + e[0]
            dst[1, x] = dst[1, x] + e[0] if face == 0 else dst[1, x] - e[0]
            dst[2, x] = dst[2, x] + e[1]
            dst[3, x] = dst[3, x] + e[2]
            dst[4, x] = dst[4, x] + e[3]
        for v in range(4):
            for odd in range(2):
                pick = v * 32 + odd * 16 + z // 2
                ey[v, pl.ds(odd, 8, stride=2)] = jnp.where(lane < 64, take(tiles[2], pick), take(tiles[3], pick))

        def body(x, carry):
            y = [jnp.broadcast_to(ey[v, pl.ds(x, 1)], (8, 128)) for v in range(4)]
            zz = [take(tiles[4 + v // 2], pick_z + ((v % 2) * 64 + x * 4)) for v in range(4)]
            add = [
                edge_y * y[0] + edge_z * zz[0],
                edge_y * y[1] + edge_z * zz[1],
                sign_y * y[0] + edge_z * zz[2],
                edge_y * y[2] + sign_z * zz[0],
                edge_y * y[3] + edge_z * zz[3],
            ]
            for i in range(5):
                dst[i, 2 * x + 1] = dst[i, 2 * x + 1] + add[i]
                dst[i, 2 * x + 2] = dst[i, 2 * x + 2] + add[i]
            return carry

        lax.fori_loop(0, 16, body, 0, unroll=16)

    live = [jnp.where(turn < count, 1.0, 0.0) for turn in range(BURN_MAX)]
    group = 16

    def burn(dst, at):
        p = [dst[0, at + i + 1] for i in range(group)]
        f = [dst[4, at + i + 1] for i in range(group)]
        for turn in range(BURN_MAX):
            for i in range(group):
                r = pl.reciprocal(fa[at + i] + fb[at + i] * jnp.tanh(p[i]), approx=True)
                d = live[turn] * (f[i] - f[i] * r)
                f[i] = f[i] - d
                p[i] = p[i] + 0.5 * d
        for i in range(group):
            dst[0, at + i + 1] = p[i]
            dst[4, at + i + 1] = f[i]

    add_ghosts(0, f1)
    for at in range(0, 32, group):
        burn(f1, at)
    fine_hydro(f1, f0)
    add_ghosts(1, f0)
    pick_m = ((lane % 32) // 16) * 64 + 2 * (lane % 16)

    def means(a):
        for i in range(5):
            tile = zero
            for g in range(4):
                at = a * 8 + 2 * g
                q = f0[i, at + 1] + f0[i, at + 2]
                q = q + lanes(q, -1)
                q = q + lanes(q, -32)
                tile = jnp.where(q4 == g, take(q, pick_m), tile)
            mb[pl.ds(a * 64 + i, 8, stride=8)] = 0.125 * tile

    def send_mean(to):
        remote(mb.at[pl.ds(to * 8, 5)], r3.at[me, pl.ds(0, 5)], 14, (region, to)).start()

    for half in range(2):
        burn(f0, 16 * half)
        means(2 * half)
        means(2 * half + 1)
        for k in range(8, 24):
            to = 16 * half + lax.rem(me + k, 16)
            if k != 16:
                send_mean(to)
            else:
                pl.when(me != to)(functools.partial(send_mean, to))
    r3[me, 0:5] = mb[pl.ds(me * 8, 5)]

    wait_all(r3.at[pl.ds(0, 31), pl.ds(0, 5)], rsem.at[14])

    def pick_pair(to):
        for s in range(2):
            p4[to, 5 * s : 5 * s + 5] = r3[keys[1, 2 * to + s], 0:5]

    for k in FAR_FIRST:
        to = lax.rem(me + k, INNER)
        pick_pair(to)
        remote(p4.at[to], r4.at[me, pl.ds(0, 10)], 15, (region, to)).start()

    pick_pair(me)
    r4[me, 0:10] = p4[me]
    for j in range(8):
        stores.append(
            pltpu.make_async_copy(
                f0.at[:, pl.ds(1, 32), j], fine_out.at[:, :, pl.ds(j * 128, 128)], lsem.at[2 + j]
            )
        )
        stores[-1].start()

    for halo, sends, _ in near + far:
        pl.when(sends)(halo.wait_send)
    for t in range(2):
        wait_all(r1[t].at[pl.ds(0, 7), pl.ds(0, 12)], ssem.at[10 + t])
        wait_all(r2[t].at[pl.ds(0, INNER - 1), pl.ds(0, 6)], ssem.at[12 + t])
    wait_all(r3.at[pl.ds(0, 31), pl.ds(0, 5)], ssem.at[14])
    wait_all(p4.at[pl.ds(0, 31)], ssem.at[15])
    for store in stores:
        store.wait()
    wait_all(r4.at[pl.ds(0, 31), pl.ds(0, 10)], rsem.at[15])


def place(stepped, means, fine, covers, coarse_out, fine_out, h, sem):
    stores = [pltpu.make_async_copy(fine, fine_out, sem.at[5])]
    stores[0].start()
    lane = iota((8, 128), 1)
    here = [covers[8 * s : 8 * s + 8] > 0 for s in range(2)]
    rows_of = means.reshape(512, 128)
    for i in range(5):

        def body(a, carry):
            tiles = [rows_of[pl.ds(a * 128 + s * 5 + i, 8, stride=16)] for s in range(2)]
            for g in range(4):
                for odd in range(2):
                    at = pl.ds((a * 4 + g) * 16 + odd, 8, stride=2)
                    q = stepped[i, at]
                    for s in range(2):
                        q = jnp.where(here[s], take(tiles[s], lane % 16 + (g * 32 + odd * 16)), q)
                    h[i, at] = q
            return carry

        lax.fori_loop(0, 4, body, 0, unroll=4)
        stores.append(pltpu.make_async_copy(h.at[i], coarse_out.at[i], sem.at[i]))
        stores[-1].start()
    for store in stores:
        store.wait()


def per_device(coarse_state, fine_state, coarse_rate, fine_rate, parents, burn_steps):
    vmem, hbm = pl.BlockSpec(memory_space=pltpu.VMEM), pl.BlockSpec(memory_space=pltpu.HBM)
    stepped, fine_mid, means, covers = pl.pallas_call(
        kernel,
        out_shape=(
            jax.ShapeDtypeStruct((5, 256, 128), F32),
            jax.ShapeDtypeStruct((5, 32, 1024), F32),
            jax.ShapeDtypeStruct((32, 16, 128), F32),
            jax.ShapeDtypeStruct((16, 128), jnp.int32),
        ),
        in_specs=[hbm] * 6,
        out_specs=(vmem,) * 4,
        scratch_shapes=[
            pltpu.VMEM((5, 288, 128), F32),
            pltpu.VMEM((256, 128), F32),
            pltpu.VMEM((2, 4, 16, 128), F32),
            pltpu.VMEM((2, 2, 5, 16, 128), F32),
            pltpu.VMEM((2, 16, 128), F32),
            pltpu.VMEM((2, 2, 6, 16, 128), F32),
            pltpu.VMEM((2, 2, 6, 16, 128), F32),
            pltpu.VMEM((4, 8, 128), F32),
            pltpu.VMEM((4, 8, 128), F32),
            pltpu.VMEM((4, 4, 16, 128), F32),
            pltpu.VMEM((4, 256, 128), F32),
            pltpu.VMEM((8, 128), jnp.int32),
            pltpu.SMEM((8, 128), jnp.int32),
            pltpu.VMEM((2, 128, 128), F32),
            pltpu.VMEM((8, 16, 128), F32),
            pltpu.VMEM((8, 16, 128), F32),
            pltpu.VMEM((2, 32, 8, 128), F32),
            pltpu.VMEM((32, 8, 128), F32),
            pltpu.VMEM((32, 8, 128), F32),
            pltpu.VMEM((5, 34, 8, 128), F32),
            pltpu.VMEM((5, 34, 8, 128), F32),
            pltpu.VMEM((32, 8, 128), F32),
            pltpu.VMEM((32, 8, 128), F32),
            pltpu.VMEM((32, 8, 128), F32),
            pltpu.VMEM((64, 128), F32),
            pltpu.VMEM((4, 16, 128), F32),
            pltpu.VMEM((256, 128), F32),
            pltpu.VMEM((32, 8, 128), F32),
            pltpu.VMEM((32, 10, 128), F32),
            pltpu.VMEM((1, 32), jnp.int32),
            pltpu.SMEM((1,), jnp.int32),
            pltpu.SemaphoreType.DMA((20,)),
            pltpu.SemaphoreType.DMA((20,)),
            pltpu.SemaphoreType.DMA((20,)),
            pltpu.SemaphoreType.DMA,
            pltpu.SemaphoreType.REGULAR,
        ],
        compiler_params=pltpu.CompilerParams(
            collective_id=0, has_side_effects=True, vmem_limit_bytes=24 * 2**20
        ),
        name="reactive_step",
    )(
        *(
            pltpu.with_memory_space_constraint(x, pltpu.HBM)
            for x in (
                coarse_state.reshape(5, 256, 128),
                fine_state.reshape(5, 32, 1024),
                coarse_rate.reshape(256, 128),
                fine_rate.reshape(32, 1024),
                parents,
            )
        ),
        burn_steps,
    )
    coarse_new, fine_new = pl.pallas_call(
        place,
        out_shape=(
            jax.ShapeDtypeStruct((5, 256, 128), F32),
            jax.ShapeDtypeStruct((5, 32, 1024), F32),
        ),
        in_specs=[vmem] * 4,
        out_specs=(hbm,) * 2,
        scratch_shapes=[
            pltpu.VMEM((5, 256, 128), F32),
            pltpu.SemaphoreType.DMA((6,)),
        ],
        compiler_params=pltpu.CompilerParams(vmem_limit_bytes=24 * 2**20),
        name="place",
    )(stepped, means, fine_mid, covers)
    return coarse_new.reshape(5, 16, 16, 128), fine_new.reshape(1, 5, 32, 1024)


def solution(mesh):
    in_specs = (
        P(None, "region", "inner", None),
        P(("region", "inner"), None, None, None),
        P("region", "inner", None),
        P(("region", "inner"), None, None),
        P("region", None),
        P(("region", "inner")),
    )
    out_specs = (P(None, "region", "inner", None), P(("region", "inner"), None, None, None))
    return jax.shard_map(per_device, mesh=mesh, in_specs=in_specs, out_specs=out_specs, check_vma=False)
```
